128 devices in a mesh: dp: 8 (over x, y_lo), tp: 16 (over z, y_hi, core).
Axes of the slice: x: 4, y: 4 (y_hi: 2, y_lo: 2; y = y_hi * 2 + y_lo), z: 4, core: 2. Of those that a mesh axis runs over, the one named last changes fastest.
Arguments:
- queries: bfloat16 [1024, 128, 576], P(('dp', 'tp')), may hold values from -48 to 48
- kv_cache: bfloat16 [1024, 1024, 576], P(('dp', 'tp')), may hold values from -6 to 6
- lengths: int32 [8, 16, 8], P(None, 'tp'), may hold values from 1 to 1024
- dest_group: int32 [8, 16], P(None, 'tp'), may hold values from 0 to 7, as said below
- moved_slot: int32 [8, 16], P(None, 'tp'), may hold values from 0 to 7
- residual_in: bfloat16 [1024, 7168], P('dp', 'tp'), may hold values from -31 to 31
- norm_gain: bfloat16 [7168], P('tp'), may hold values from 0.099609375 to 1.8984375
- up_value: bfloat16 [128, 512, 128], P('dp'), may hold values from -0.75 to 0.75
- out_proj: bfloat16 [16384, 7168], P('dp', 'tp'), may hold values from -0.046875 to 0.046875
- gate_proj: bfloat16 [7168, 18432], P('tp', 'dp'), may hold values from -0.0625 to 0.0625
- up_proj: bfloat16 [7168, 18432], P('tp', 'dp'), may hold values from -0.0625 to 0.0625
- down_proj: bfloat16 [18432, 7168], P('dp', 'tp'), may hold values from -0.046875 to 0.046875
Outputs:
- attended: bfloat16 [1024, 7168], P('dp', 'tp')
- layer_out: bfloat16 [1024, 7168], P('dp', 'tp')
The draws below stay inside these ranges and needn't reach their ends.
Inputs may be any that keep to these rules, and one draw needn't show every extreme that they name: dest_group[g, t] = g XOR m_t, where the mask m_t lies in 1 to 7 and is the same for every g of column t; so dest_group[dest_group[g, t], t] = g.
All inputs are finite; a program needn't handle non-finite values.
Results may differ from the reference program's by a relative error of at most 0.022.
Values may be sent and summed in bfloat16 or wider, within the bound.
A program may use at most 128 MiB of HBM per device.

```python
import jax
import jax.numpy as jnp
from jax import lax

D = 7168
H = 128
KV = 512
ROPE = 64
V_DIM = 128
FF = 18432
R_DEV = 8
LCAP = 1024
REQ = 1024
N_DP = 8
N_TP = 16


def draw_plan(key):
    base = jax.random.fold_in(key, 7)
    mask_key, side_key, slot_key, long_key, short_key = jax.random.split(base, 5)
    column_mask = jax.random.randint(mask_key, (N_TP,), 1, N_DP, dtype=jnp.int32)
    side_bit = jax.random.randint(side_key, (N_TP,), 0, 2, dtype=jnp.int32)
    top_bit = jnp.zeros((N_TP,), jnp.int32)
    for level in range(1, N_DP.bit_length()):
        top_bit = jnp.where(jnp.right_shift(column_mask, level) > 0, level, top_bit)
    groups = jnp.arange(N_DP, dtype=jnp.int32)[:, None]
    heavy = jnp.right_shift(groups, top_bit[None, :]) & 1 == side_bit[None, :]
    partners = jnp.bitwise_xor(groups, column_mask[None, :])
    slots = jax.random.randint(slot_key, (N_DP, N_TP), 0, R_DEV, dtype=jnp.int32)
    long_len = jax.random.randint(long_key, (N_DP, N_TP, R_DEV), LCAP // 2, LCAP + 1, dtype=jnp.int32)
    short_len = jax.random.randint(short_key, (N_DP, N_TP, R_DEV), 1, LCAP // 4 + 1, dtype=jnp.int32)
    slot_ids = jnp.arange(R_DEV, dtype=jnp.int32)[None, None, :]
    context = jnp.where(heavy[:, :, None], long_len, short_len)
    context = jnp.where(heavy[:, :, None] & (slot_ids == slots[:, :, None]), LCAP, context)
    return (context.astype(jnp.int32), partners.astype(jnp.int32), slots)


def shared_keys(key):
    base = jax.random.normal(jax.random.fold_in(key, 50), (REQ, 2, KV + ROPE), jnp.float32)
    base = jnp.clip(base, -6.0, 6.0)
    leading = base[:, 0]
    second = jnp.clip(leading + 0.15 * base[:, 1], -6.0, 6.0)
    return (leading, second)


def draw_lengths(key, part):
    return draw_plan(key)[0]


def draw_dest_group(key, part):
    return draw_plan(key)[1]


def draw_moved_slot(key, part):
    return draw_plan(key)[2]


def draw_kv_cache(key, part):
    leading, second = shared_keys(key)
    key = jax.random.fold_in(key, 1)
    entries = jnp.clip(jax.random.normal(key, (REQ, LCAP, KV + ROPE), jnp.float32), -6.0, 6.0)
    entries = entries.at[:, 0].set(leading).at[:, 1].set(second)
    return entries.astype(jnp.bfloat16)


def draw_queries(key, part):
    key = jax.random.fold_in(key, 2)
    base_key = jax.random.fold_in(key, 0)
    values = jnp.clip(jax.random.normal(base_key, (REQ, H, KV + ROPE), jnp.float32), -6.0, 6.0)
    return values.astype(jnp.bfloat16)


def draw_residual_in(key, part):
    key = jax.random.fold_in(key, 3)
    base_key = jax.random.fold_in(key, 0)
    ramp = jnp.arange(D, dtype=jnp.float32)[None, :] / (D - 1)
    values = jnp.clip(jax.random.normal(base_key, (REQ, D), jnp.float32), -6.0, 6.0) * (0.75 + 0.55 * ramp)
    return values.astype(jnp.bfloat16)


def levels(stream_key, dims, cuts, least, top_value):
    def one(dim, parts):
        steps = jax.random.uniform(jax.random.fold_in(jax.random.fold_in(stream_key, 6), dim), (parts,), jnp.float32, least / len(cuts), top_value / len(cuts))
        return jnp.repeat(jnp.exp(steps), dims[dim] // parts).reshape((-1,) + (1,) * (len(dims) - dim - 1))

    level = one(*cuts[0])
    for cut in cuts[1:]:
        level = level * one(*cut)
    return level


def bell_draw(own_key, shape, deviation, bound, cuts=(), kind=jnp.bfloat16):
    drawn = jax.random.normal(own_key, shape, jnp.float32) * deviation
    if len(cuts) > 0:
        drawn = levels(own_key, shape, cuts, -0.22, 0.18) * drawn
    return jnp.clip(drawn, min=-bound, max=bound).astype(kind)


def setup_inputs(seed: int = 0) -> dict:
    streams_of = jax.random.split(jax.random.key(seed), 13)
    return {
        "queries": draw_queries(jax.random.fold_in(streams_of[12], 71), 0),
        "kv_cache": draw_kv_cache(jax.random.fold_in(streams_of[12], 71), 0),
        "lengths": draw_lengths(jax.random.fold_in(streams_of[12], 71), 0),
        "dest_group": draw_dest_group(jax.random.fold_in(streams_of[12], 71), 0),
        "moved_slot": draw_moved_slot(jax.random.fold_in(streams_of[12], 71), 0),
        "residual_in": draw_residual_in(jax.random.fold_in(streams_of[12], 71), 0),
        "norm_gain": jnp.clip(1.0 + 0.18 * jax.random.normal(streams_of[6], (D,), jnp.float32), 0.099609375, 1.8984375).astype(jnp.bfloat16),
        "up_value": bell_draw(streams_of[7], (H, KV, V_DIM), 64 ** -0.5, 0.75, ((0, 8),)),
        "out_proj": bell_draw(streams_of[8], (H * V_DIM, D), (H * V_DIM) ** -0.5, 0.046875, ((0, 8), (1, 16))),
        "gate_proj": bell_draw(streams_of[9], (D, FF), D ** -0.5, 0.0625, ((0, 16), (1, 8))),
        "up_proj": bell_draw(streams_of[10], (D, FF), D ** -0.5, 0.0625, ((0, 16), (1, 8))),
        "down_proj": bell_draw(streams_of[11], (FF, D), FF ** -0.5, 0.046875, ((0, 8), (1, 16))),
    }


score_scale = 192.0 ** (-0.5)
norm_eps = 1e-06

def attend_one(query_row, cache_rows, length_one):
    scores = jnp.einsum('hc,kc->hk', query_row.astype(jnp.float32), cache_rows.astype(jnp.float32)) * score_scale
    position = jnp.arange(cache_rows.shape[0], dtype=jnp.int32)
    allowed = (position < length_one)[None, :]
    masked = jnp.where(allowed, scores, -jnp.inf)
    largest = lax.optimization_barrier(jnp.max(masked, axis=1, keepdims=True))
    expterm = jnp.where(allowed, jnp.exp(masked - largest), 0.0)
    weights = (expterm / lax.optimization_barrier(jnp.sum(expterm, axis=1, keepdims=True))).astype(jnp.bfloat16)
    latent = jnp.einsum('hk,kc->hc', weights.astype(jnp.float32), cache_rows[:, :KV].astype(jnp.float32))
    return latent.astype(jnp.bfloat16)

def source_rows(dest_group, moved_slot):
    groups = jnp.arange(N_DP, dtype=jnp.int32)[:, None, None]
    columns = jnp.arange(N_TP, dtype=jnp.int32)[None, :, None]
    slot_ids = jnp.arange(R_DEV, dtype=jnp.int32)[None, None, :]
    partner = dest_group[:, :, None]
    own_slot = moved_slot[:, :, None]
    column_ids = jnp.broadcast_to(jnp.arange(N_TP, dtype=jnp.int32)[None, :], dest_group.shape)
    partner_slot = moved_slot[dest_group, column_ids][:, :, None]
    incoming = (partner * N_TP + columns) * R_DEV + partner_slot
    staying = (groups * N_TP + columns) * R_DEV + slot_ids
    anchor = jnp.where(slot_ids == own_slot, incoming, staying)
    return jnp.transpose(anchor, (1, 0, 2)).reshape(-1).astype(jnp.int32)

def reference(queries, kv_cache, lengths, dest_group, moved_slot, residual_in, norm_gain, up_value, out_proj, gate_proj, up_proj, down_proj):
    anchor = source_rows(dest_group, moved_slot)
    flat_lengths = lengths.reshape(-1)

    def attend_row(index):
        return attend_one(queries[index], kv_cache[index], flat_lengths[index])
    latent = lax.map(attend_row, anchor)
    values = jnp.einsum('nhc,hcd->nhd', latent.astype(jnp.float32), up_value.astype(jnp.float32))
    values = values.astype(jnp.bfloat16).reshape(latent.shape[0], H * V_DIM)
    attn = jnp.dot(values, out_proj, preferred_element_type=jnp.float32)
    attended = attn.astype(jnp.bfloat16)
    resid = residual_in.astype(jnp.float32) + attn
    row_scale = lax.rsqrt(lax.optimization_barrier(jnp.mean(resid * resid, axis=1, keepdims=True)) + norm_eps)
    normed = (resid * row_scale * norm_gain.astype(jnp.float32)).astype(jnp.bfloat16)
    gate = jnp.dot(normed, gate_proj, preferred_element_type=jnp.float32)
    upward = jnp.dot(normed, up_proj, preferred_element_type=jnp.float32)
    hidden = (jax.nn.silu(gate) * upward).astype(jnp.bfloat16)
    layer_out = (resid + jnp.dot(hidden, down_proj, preferred_element_type=jnp.float32)).astype(jnp.bfloat16)
    return (attended, layer_out)
```

```python
import jax
import jax.numpy as jnp
from jax import lax
from jax.sharding import PartitionSpec as P

D = 7168
KV = 512


score_scale = 192.0 ** (-0.5)
norm_eps = 1e-06


def attend_block(query_rows, cache_rows, length_rows):
    scores = (
        jnp.einsum("rhc,rkc->rhk", query_rows, cache_rows, preferred_element_type=jnp.float32)
        * score_scale
    )
    position = lax.broadcasted_iota(jnp.int32, scores.shape, 2)
    allowed = position < length_rows[:, None, None]
    masked = jnp.where(allowed, scores, -jnp.inf)
    largest = jnp.max(masked, axis=2, keepdims=True)
    expterm = jnp.where(allowed, jnp.exp(masked - largest), 0.0)
    weights = (expterm / jnp.sum(expterm, axis=2, keepdims=True)).astype(jnp.bfloat16)
    latent = jnp.einsum(
        "rhk,rkc->rhc", weights, cache_rows[:, :, :KV], preferred_element_type=jnp.float32
    )
    return latent.astype(jnp.bfloat16)


def placed_sources(partners, slots, slot_count):
    groups = jnp.arange(partners.shape[0], dtype=jnp.int32)[:, None]
    slot_ids = jnp.arange(slot_count, dtype=jnp.int32)[None, :]
    incoming = partners[:, None] * slot_count + slots[partners][:, None]
    staying = groups * slot_count + slot_ids
    return jnp.where(slot_ids == slots[:, None], incoming, staying).reshape(-1)


def shards(
    queries,
    kv_cache,
    lengths,
    dest_group,
    moved_slot,
    residual_in,
    norm_gain,
    up_value,
    out_proj,
    gate_proj,
    up_proj,
    down_proj,
):
    group = lax.axis_index("dp")
    own_lengths = lax.dynamic_index_in_dim(lengths[:, 0, :], group, 0, keepdims=False)
    latent = attend_block(queries, kv_cache, own_lengths)
    head_rows = lax.all_to_all(latent, "dp", split_axis=1, concat_axis=0, tiled=True)
    values = jnp.einsum(
        "rhc,hcd->rhd", head_rows, up_value, preferred_element_type=jnp.float32
    ).astype(jnp.bfloat16)
    values = values.reshape(values.shape[0], values.shape[1] * values.shape[2])
    values = values[placed_sources(dest_group[:, 0], moved_slot[:, 0], own_lengths.shape[0])]
    head_terms = jnp.dot(
        lax.all_gather(values, "tp", axis=0, tiled=True),
        out_proj,
        preferred_element_type=jnp.float32,
    )
    attn = lax.psum_scatter(
        head_terms.astype(jnp.bfloat16), "dp", scatter_dimension=0, tiled=True
    ).astype(jnp.float32)
    resid = residual_in.astype(jnp.float32) + attn
    square_sum = jnp.sum(resid * resid, axis=1)
    scaled = (resid * norm_gain.astype(jnp.float32)).astype(jnp.bfloat16)
    block_rows = lax.all_gather(scaled, "dp", axis=0, tiled=True)
    block_sums = lax.all_gather(square_sum, "dp", axis=0, tiled=True)
    gate_part = jnp.dot(block_rows, gate_proj, preferred_element_type=jnp.float32)
    upward_part = jnp.dot(block_rows, up_proj, preferred_element_type=jnp.float32)
    partial_gate = jnp.concatenate((gate_part, upward_part), axis=1)
    ff_local = gate_proj.shape[1]
    summed = lax.psum_scatter(
        partial_gate.astype(jnp.bfloat16), "tp", scatter_dimension=0, tiled=True
    ).astype(jnp.float32)
    row_sums = lax.psum_scatter(block_sums, "tp", scatter_dimension=0, tiled=True)
    row_scale = lax.rsqrt(row_sums / D + norm_eps)[:, None]
    summed = summed * row_scale
    hidden = (jax.nn.silu(summed[:, :ff_local]) * summed[:, ff_local:]).astype(jnp.bfloat16)
    hidden = lax.all_gather(hidden, "tp", axis=0, tiled=True)
    block_rows = hidden
    down = lax.psum_scatter(
        jnp.dot(block_rows, down_proj, preferred_element_type=jnp.float32).astype(jnp.bfloat16),
        "dp",
        scatter_dimension=0,
        tiled=True,
    ).astype(jnp.float32)
    return (attn.astype(jnp.bfloat16), (resid + down).astype(jnp.bfloat16))


def solution(mesh):
    return jax.shard_map(
        shards,
        mesh=mesh,
        in_specs=(
            P(("dp", "tp"), None, None),
            P(("dp", "tp"), None, None),
            P(None, "tp", None),
            P(None, "tp"),
            P(None, "tp"),
            P("dp", "tp"),
            P("tp"),
            P("dp", None, None),
            P("dp", "tp"),
            P("tp", "dp"),
            P("tp", "dp"),
            P("dp", "tp"),
        ),
        out_specs=(P("dp", "tp"), P("dp", "tp")),
        check_vma=False,
    )
```

```python
import functools

import jax
import jax.numpy as jnp
from jax import lax
from jax.experimental import pallas as pl
from jax.experimental.pallas import tpu as pltpu
from jax.sharding import PartitionSpec as P

MESH = pl.DeviceIdType.MESH
KV = 512
GROUPS = 8
score_scale = 192.0 ** (-0.5)


def attend_kernel(
    length_ref, partner_ref, slot_ref, query_ref, cache_ref, up_ref, out_ref,
    query_buf, cache_buf, up_buf, lat_out, lat_in, wide, vals,
    load_sem, up_sem, own_sem, send_sem, recv_sem,
):
    g = lax.axis_index("dp")
    t = lax.axis_index("tp")
    slots = query_ref.shape[0]
    heads = up_ref.shape[0]

    def loads(r):
        return (
            pltpu.make_async_copy(query_ref.at[r], query_buf.at[r], load_sem.at[0, r]),
            pltpu.make_async_copy(cache_ref.at[r], cache_buf.at[r], load_sem.at[1, r]),
        )

    for r in range(slots):
        for copy in loads(r):
            copy.start()
    up_copy = pltpu.make_async_copy(up_ref, up_buf, up_sem)
    up_copy.start()
    barrier = pltpu.get_barrier_semaphore()
    for k in range(1, GROUPS):
        pl.semaphore_signal(
            barrier, inc=1, device_id=(lax.rem(g + k, GROUPS), t), device_id_type=MESH
        )
    pl.semaphore_wait(barrier, GROUPS - 1)

    def send(k, r):
        p = lax.rem(g + k, GROUPS)
        return pltpu.make_async_remote_copy(
            src_ref=lat_out.at[pl.ds(r, 2), pl.ds(pl.multiple_of(p * heads, heads), heads)],
            dst_ref=lat_in.at[g, pl.ds(r, 2)],
            send_sem=send_sem.at[k],
            recv_sem=recv_sem.at[g],
            device_id=(p, t),
            device_id_type=MESH,
        )

    def attend(r):
        for copy in loads(r):
            copy.wait()
        length = length_ref[g, r]
        cache = cache_buf[r]
        scores = lax.dot_general(
            query_buf[r], cache, (((0,), (0,)), ((), ())), preferred_element_type=jnp.float32
        )
        position = lax.broadcasted_iota(jnp.int32, scores.shape, 1)
        masked = jnp.where(position < length, scores * score_scale, -jnp.inf)
        largest = jnp.max(masked, axis=1, keepdims=True)
        expterm = jnp.exp(masked - largest)
        total = jnp.sum(expterm, axis=1, keepdims=True)
        weights = (expterm / total).astype(jnp.bfloat16)
        latent = lax.dot_general(
            weights, cache[:KV], (((1,), (1,)), ((), ())), preferred_element_type=jnp.float32
        )
        lat_out[r] = latent.astype(jnp.bfloat16)

    def pair(i, carry):
        attend(2 * i)
        attend(2 * i + 1)
        for k in (4, 3, 5, 2, 6, 1, 7):
            send(k, 2 * i).start()
        return carry

    lax.fori_loop(0, slots // 2, pair, 0)
    own = pltpu.make_async_copy(
        lat_out.at[:, pl.ds(pl.multiple_of(g * heads, heads), heads)], lat_in.at[g], own_sem
    )
    own.start()
    own.wait()
    up_copy.wait()

    def widen(k, carry):
        s = lax.rem(g + k, GROUPS)

        @pl.when(k > 0)
        def _():
            pltpu.make_async_remote_copy(
                src_ref=lat_in.at[s], dst_ref=lat_in.at[s], send_sem=send_sem.at[0],
                recv_sem=recv_sem.at[s], device_id=(s, t), device_id_type=MESH,
            ).wait_recv()

        rows = slots * heads
        block = lat_in[s].astype(jnp.float32).reshape(rows, KV)
        for lane in range(KV // 128):
            wide[lane, pl.ds(pl.multiple_of(s * rows, rows), rows)] = block[
                :, lane * 128 : (lane + 1) * 128
            ]
        return carry

    lax.fori_loop(0, GROUPS, widen, 0)
    count = GROUPS * slots
    for h in range(heads):
        head_rows = jnp.concatenate(
            [wide[lane, pl.ds(h, count, stride=heads), :] for lane in range(KV // 128)], axis=1
        )
        vals[:, h * 128 : (h + 1) * 128] = jnp.dot(
            head_rows.astype(jnp.bfloat16),
            up_buf[h],
            preferred_element_type=jnp.float32,
        ).astype(jnp.bfloat16)
    row = lax.broadcasted_iota(jnp.int32, (count, count), 0)
    column = lax.broadcasted_iota(jnp.int32, (count, count), 1)
    source = row
    for group in range(GROUPS):
        partner = partner_ref[group]
        own_row = group * slots + slot_ref[group]
        source = jnp.where(row == own_row, partner * slots + slot_ref[partner], source)
    place = jnp.where(column == source, 1.0, 0.0).astype(jnp.bfloat16)
    out_ref[...] = jnp.dot(place, vals[...], preferred_element_type=jnp.float32).astype(
        jnp.bfloat16
    )
    for k in range(1, GROUPS):
        pltpu.make_async_remote_copy(
            src_ref=lat_in.at[0], dst_ref=lat_in.at[0], send_sem=send_sem.at[k],
            recv_sem=recv_sem.at[0], device_id=(lax.rem(g + k, GROUPS), t), device_id_type=MESH,
        ).wait_send()


def attend_values(lengths, dest_group, moved_slot, queries, kv_cache, up_value):
    slots, all_heads, _ = queries.shape
    queries = jnp.swapaxes(queries, 1, 2)
    kv_cache = jnp.swapaxes(kv_cache, 1, 2)
    heads = up_value.shape[0]
    rows = GROUPS * slots
    smem = pl.BlockSpec(memory_space=pltpu.SMEM)
    hbm = pl.BlockSpec(memory_space=pl.ANY)
    bf16 = jnp.bfloat16
    return pl.pallas_call(
        attend_kernel,
        name="attend",
        out_shape=jax.ShapeDtypeStruct((rows, heads * 128), bf16),
        in_specs=[smem, smem, smem, hbm, hbm, hbm],
        out_specs=pl.BlockSpec(memory_space=pltpu.VMEM),
        scratch_shapes=[
            pltpu.VMEM(queries.shape, bf16),
            pltpu.VMEM(kv_cache.shape, bf16),
            pltpu.VMEM(up_value.shape, bf16),
            pltpu.VMEM((slots, all_heads, KV), bf16),
            pltpu.VMEM((GROUPS, slots, heads, KV), bf16),
            pltpu.VMEM((KV // 128, GROUPS * slots * heads, 128), jnp.float32),
            pltpu.VMEM((rows, heads * 128), bf16),
            pltpu.SemaphoreType.DMA((2, slots)),
            pltpu.SemaphoreType.DMA,
            pltpu.SemaphoreType.DMA,
            pltpu.SemaphoreType.DMA((GROUPS,)),
            pltpu.SemaphoreType.DMA((GROUPS,)),
        ],
        compiler_params=pltpu.CompilerParams(
            collective_id=0, has_side_effects=True, vmem_limit_bytes=56 << 20
        ),
        cost_estimate=pl.CostEstimate(
            flops=2 * slots * all_heads * 1024 * 1088, bytes_accessed=13 << 20, transcendentals=1 << 20
        ),
    )(lengths[:, 0, :], dest_group[:, 0], moved_slot[:, 0], queries, kv_cache, up_value)


D = 7168
norm_eps = 1e-06


def shards(
    queries,
    kv_cache,
    lengths,
    dest_group,
    moved_slot,
    residual_in,
    norm_gain,
    up_value,
    out_proj,
    gate_proj,
    up_proj,
    down_proj,
):
    values = attend_values(lengths, dest_group, moved_slot, queries, kv_cache, up_value)
    head_terms = jnp.dot(
        lax.all_gather(values, "tp", axis=0, tiled=True),
        out_proj,
        preferred_element_type=jnp.float32,
    )
    attn = lax.psum_scatter(
        head_terms.astype(jnp.bfloat16), "dp", scatter_dimension=0, tiled=True
    ).astype(jnp.float32)
    resid = residual_in.astype(jnp.float32) + attn
    square_sum = jnp.sum(resid * resid, axis=1)
    scaled = (resid * norm_gain.astype(jnp.float32)).astype(jnp.bfloat16)
    block_rows = lax.all_gather(scaled, "dp", axis=0, tiled=True)
    block_sums = lax.all_gather(square_sum, "dp", axis=0, tiled=True)
    gate_part = jnp.dot(block_rows, gate_proj, preferred_element_type=jnp.float32)
    upward_part = jnp.dot(block_rows, up_proj, preferred_element_type=jnp.float32)
    partial_gate = jnp.concatenate((gate_part, upward_part), axis=1)
    ff_local = gate_proj.shape[1]
    summed = lax.psum_scatter(
        partial_gate.astype(jnp.bfloat16), "tp", scatter_dimension=0, tiled=True
    ).astype(jnp.float32)
    row_sums = lax.psum_scatter(block_sums, "tp", scatter_dimension=0, tiled=True)
    row_scale = lax.rsqrt(row_sums / D + norm_eps)[:, None]
    summed = summed * row_scale
    hidden = (jax.nn.silu(summed[:, :ff_local]) * summed[:, ff_local:]).astype(jnp.bfloat16)
    hidden = lax.all_gather(hidden, "tp", axis=0, tiled=True)
    block_rows = hidden
    down = lax.psum_scatter(
        jnp.dot(block_rows, down_proj, preferred_element_type=jnp.float32).astype(jnp.bfloat16),
        "dp",
        scatter_dimension=0,
        tiled=True,
    ).astype(jnp.float32)
    return (attn.astype(jnp.bfloat16), (resid + down).astype(jnp.bfloat16))


def solution(mesh):
    return jax.shard_map(
        shards,
        mesh=mesh,
        in_specs=(
            P(("dp", "tp"), None, None),
            P(("dp", "tp"), None, None),
            P(None, "tp", None),
            P(None, "tp"),
            P(None, "tp"),
            P("dp", "tp"),
            P("tp"),
            P("dp", None, None),
            P("dp", "tp"),
            P("tp", "dp"),
            P("tp", "dp"),
            P("dp", "tp"),
        ),
        out_specs=(P("dp", "tp"), P("dp", "tp")),
        check_vma=False,
    )
```

```python
import jax
import jax.numpy as jnp
from jax import lax
from jax.experimental import pallas as pl
from jax.experimental.pallas import tpu as pltpu
from jax.sharding import PartitionSpec as P

MESH = pl.DeviceIdType.MESH
KV = 512
GROUPS = 8
score_scale = 192.0 ** (-0.5)


def attend_kernel(
    length_ref, partner_ref, slot_ref, query_ref, cache_ref, up_ref, out_ref,
    query_buf, cache_buf, up_buf, lat_out, lat_in, wide, vals,
    load_sem, up_sem, own_sem, send_sem, recv_sem,
):
    g = lax.axis_index("dp")
    t = lax.axis_index("tp")
    slots = query_ref.shape[0]
    heads = up_ref.shape[0]

    def loads(r):
        return (
            pltpu.make_async_copy(query_ref.at[r], query_buf.at[r], load_sem.at[0, r]),
            pltpu.make_async_copy(cache_ref.at[r], cache_buf.at[r], load_sem.at[1, r]),
        )

    for r in range(slots):
        for copy in loads(r):
            copy.start()
    up_copy = pltpu.make_async_copy(up_ref, up_buf, up_sem)
    up_copy.start()
    barrier = pltpu.get_barrier_semaphore()
    for k in range(1, GROUPS):
        pl.semaphore_signal(
            barrier, inc=1, device_id=(lax.rem(g + k, GROUPS), t), device_id_type=MESH
        )
    pl.semaphore_wait(barrier, GROUPS - 1)

    def send(k, r):
        p = lax.rem(g + k, GROUPS)
        return pltpu.make_async_remote_copy(
            src_ref=lat_out.at[pl.ds(r, 2), pl.ds(pl.multiple_of(p * heads, heads), heads)],
            dst_ref=lat_in.at[g, pl.ds(r, 2)],
            send_sem=send_sem.at[k],
            recv_sem=recv_sem.at[g],
            device_id=(p, t),
            device_id_type=MESH,
        )

    def attend(r):
        for copy in loads(r):
            copy.wait()
        length = length_ref[g, r]
        cache = cache_buf[r]
        scores = lax.dot_general(
            query_buf[r], cache, (((0,), (0,)), ((), ())), preferred_element_type=jnp.float32
        )
        position = lax.broadcasted_iota(jnp.int32, scores.shape, 1)
        masked = jnp.where(position < length, scores * score_scale, -jnp.inf)
        largest = jnp.max(masked, axis=1, keepdims=True)
        expterm = jnp.exp(masked - largest)
        total = jnp.sum(expterm, axis=1, keepdims=True)
        weights = (expterm / total).astype(jnp.bfloat16)
        latent = lax.dot_general(
            weights, cache[:KV], (((1,), (1,)), ((), ())), preferred_element_type=jnp.float32
        )
        lat_out[r] = latent.astype(jnp.bfloat16)

    def pair(i, carry):
        attend(2 * i)
        attend(2 * i + 1)
        for k in (4, 3, 5, 2, 6, 1, 7):
            send(k, 2 * i).start()
        return carry

    lax.fori_loop(0, slots // 2, pair, 0)
    own = pltpu.make_async_copy(
        lat_out.at[:, pl.ds(pl.multiple_of(g * heads, heads), heads)], lat_in.at[g], own_sem
    )
    own.start()
    own.wait()
    up_copy.wait()

    def widen(k, carry):
        s = lax.rem(g + k, GROUPS)

        @pl.when(k > 0)
        def _():
            pltpu.make_async_remote_copy(
                src_ref=lat_in.at[s], dst_ref=lat_in.at[s], send_sem=send_sem.at[0],
                recv_sem=recv_sem.at[s], device_id=(s, t), device_id_type=MESH,
            ).wait_recv()

        rows = slots * heads
        block = lat_in[s].astype(jnp.float32).reshape(rows, KV)
        for lane in range(KV // 128):
            wide[lane, pl.ds(pl.multiple_of(s * rows, rows), rows)] = block[
                :, lane * 128 : (lane + 1) * 128
            ]
        return carry

    lax.fori_loop(0, GROUPS, widen, 0)
    count = GROUPS * slots
    for h in range(heads):
        head_rows = jnp.concatenate(
            [wide[lane, pl.ds(h, count, stride=heads), :] for lane in range(KV // 128)], axis=1
        )
        vals[:, h * 128 : (h + 1) * 128] = jnp.dot(
            head_rows.astype(jnp.bfloat16),
            up_buf[h],
            preferred_element_type=jnp.float32,
        ).astype(jnp.bfloat16)
    row = lax.broadcasted_iota(jnp.int32, (count, count), 0)
    column = lax.broadcasted_iota(jnp.int32, (count, count), 1)
    source = row
    for group in range(GROUPS):
        partner = partner_ref[group]
        own_row = group * slots + slot_ref[group]
        source = jnp.where(row == own_row, partner * slots + slot_ref[partner], source)
    place = jnp.where(column == source, 1.0, 0.0).astype(jnp.bfloat16)
    out_ref[...] = jnp.dot(place, vals[...], preferred_element_type=jnp.float32).astype(
        jnp.bfloat16
    )
    for k in range(1, GROUPS):
        pltpu.make_async_remote_copy(
            src_ref=lat_in.at[0], dst_ref=lat_in.at[0], send_sem=send_sem.at[k],
            recv_sem=recv_sem.at[0], device_id=(lax.rem(g + k, GROUPS), t), device_id_type=MESH,
        ).wait_send()


def attend_values(lengths, dest_group, moved_slot, queries, kv_cache, up_value):
    slots, all_heads, _ = queries.shape
    queries = jnp.swapaxes(queries, 1, 2)
    kv_cache = jnp.swapaxes(kv_cache, 1, 2)
    heads = up_value.shape[0]
    rows = GROUPS * slots
    smem = pl.BlockSpec(memory_space=pltpu.SMEM)
    hbm = pl.BlockSpec(memory_space=pl.ANY)
    bf16 = jnp.bfloat16
    return pl.pallas_call(
        attend_kernel,
        name="attend",
        out_shape=jax.ShapeDtypeStruct((rows, heads * 128), bf16),
        in_specs=[smem, smem, smem, hbm, hbm, hbm],
        out_specs=pl.BlockSpec(memory_space=pltpu.VMEM),
        scratch_shapes=[
            pltpu.VMEM(queries.shape, bf16),
            pltpu.VMEM(kv_cache.shape, bf16),
            pltpu.VMEM(up_value.shape, bf16),
            pltpu.VMEM((slots, all_heads, KV), bf16),
            pltpu.VMEM((GROUPS, slots, heads, KV), bf16),
            pltpu.VMEM((KV // 128, GROUPS * slots * heads, 128), jnp.float32),
            pltpu.VMEM((rows, heads * 128), bf16),
            pltpu.SemaphoreType.DMA((2, slots)),
            pltpu.SemaphoreType.DMA,
            pltpu.SemaphoreType.DMA,
            pltpu.SemaphoreType.DMA((GROUPS,)),
            pltpu.SemaphoreType.DMA((GROUPS,)),
        ],
        compiler_params=pltpu.CompilerParams(
            collective_id=0, has_side_effects=True, vmem_limit_bytes=56 << 20
        ),
        cost_estimate=pl.CostEstimate(
            flops=2 * slots * all_heads * 1024 * 1088, bytes_accessed=13 << 20, transcendentals=1 << 20
        ),
    )(lengths[:, 0, :], dest_group[:, 0], moved_slot[:, 0], queries, kv_cache, up_value)


D = 7168
norm_eps = 1e-06
A_EXTRA = 512


def layer_kernel(
    vals_ref, resid_ref, gain_ref, wo_ref, wg_ref, wu_ref, wd_ref, attended_ref, out_ref,
    wo, wg, wu, wd, resid_both, gain_own, gain_both,
    vb, c_out, c_in, xb, part_a, part_b, a1_in, a2_out, a2_in, b1_in, b2_out, b2_in, b_keep,
    hb, g_out, g_in, resid_rows, att_x, lay_x, turned,
    w_l, w_s, w_r, v_s, v_r, c_s, c_r, x_s, x_r, a1_s, a1_r, a2_s, a2_r, b1_s, b1_r, b2_s, b2_r,
    h_s, h_r, g_s, g_r, o_s, o_r,
):
    g = lax.axis_index("dp")
    t = lax.axis_index("tp")
    c = lax.rem(t, 2)
    q = t // 2
    z = q // 2
    yh = lax.rem(q, 2)
    x = g // 2
    rows = vals_ref.shape[0]
    feats = wo_ref.shape[0]
    ff = wg_ref.shape[1]
    both = 2 * feats
    a_cols = ff + A_EXTRA
    b_cols = ff - A_EXTRA
    half = rows // 2
    f32 = jnp.float32
    bf16 = jnp.bfloat16

    def other_group(k):
        return (lax.rem(g + k, GROUPS), t)

    def other_z(k):
        return (g, lax.rem(z + k, 4) * 4 + yh * 2 + c)

    def chip(zp):
        return (g, zp * 4 + yh * 2 + c)

    y_peer = (g, z * 4 + (1 - yh) * 2 + c)
    sibling = (g, q * 2 + 1 - c)

    def remote(src, dst, send_sem, recv_sem, device):
        return pltpu.make_async_remote_copy(
            src_ref=src, dst_ref=dst, send_sem=send_sem, recv_sem=recv_sem,
            device_id=device, device_id_type=MESH,
        )

    def arrived(ref, sem):
        remote(ref, ref, sem, sem, sibling).wait_recv()

    def left(ref, sem):
        remote(ref, ref, sem, sem, sibling).wait_send()

    def order(i):
        return i + (i // 2) * (5 - 2 * i)

    barrier = pltpu.get_barrier_semaphore()
    greeted = [other_group(k) for k in range(1, GROUPS)]
    greeted += [other_z(k) for k in (1, 2, 3)] + [y_peer, sibling]
    for device in greeted:
        pl.semaphore_signal(barrier, inc=1, device_id=device, device_id_type=MESH)

    own_rows = pl.ds(pl.multiple_of(c * feats, feats), feats)
    gain_own[...] = jnp.transpose(
        jnp.broadcast_to(gain_ref[...].astype(f32), (128, feats)), (1, 0)
    ).astype(bf16)
    weights = (
        (wo_ref, wo), (resid_ref, resid_both), (gain_own, gain_both),
        (wg_ref, wg), (wu_ref, wu), (wd_ref, wd),
    )
    for i, (src, dst) in enumerate(weights):
        pltpu.make_async_copy(src, dst.at[own_rows], w_l.at[i]).start()
    vb[q] = vals_ref[...]
    pl.semaphore_wait(barrier, len(greeted))

    upper = pl.ds(0, half)
    lower = pl.ds(half, half)

    def gather_start(buf, s, r):
        own_a = buf.at[q, upper]
        own_b = buf.at[q, lower]
        remote(own_a, own_a, s.at[0], r.at[0], y_peer).start()
        for k in (2, 1, 3):
            remote(own_b, own_b, s.at[k], r.at[k], other_z(k)).start()
        remote(own_b, own_b, s.at[10], r.at[10], y_peer).start()
        for k in (2, 1, 3):
            remote(own_a, own_a, s.at[3 + k], r.at[3 + k], other_z(k)).start()

    def forward_y(buf, s, r):
        block = buf.at[z * 2 + 1 - yh, upper]
        arrived(block, r.at[0])
        for k in (2, 1, 3):
            remote(block, block, s.at[6 + k], r.at[6 + k], other_z(k)).start()

    def forward_z(buf, s, r, k):
        block = buf.at[lax.rem(z + 4 - k, 4) * 2 + yh, lower]
        arrived(block, r.at[k])
        remote(block, block, s.at[10 + k], r.at[10 + k], y_peer).start()

    def project(buf, w, s, r, out, landed, out_s, out_r):
        forward_y(buf, s, r)
        forward_z(buf, s, r, 1)
        forward_z(buf, s, r, 3)

        def step(i, carry):
            k = order(i)
            zp = lax.rem(z + 4 - k, 4)
            arrived(buf.at[0, lower], r.at[10 + k])

            @pl.when(k > 0)
            def _():
                arrived(buf.at[0, upper], r.at[3 + k])
                arrived(buf.at[0, upper], r.at[6 + k])

            left_rows = buf[pl.ds(2 * zp, 2)].reshape(2 * rows, buf.shape[2])
            product = lax.dot_general(
                left_rows, w[...], (((1,), (1,)), ((), ())), preferred_element_type=f32
            )
            out[pl.ds(2 * zp, 2)] = product.astype(bf16).reshape(2, rows, both)
            for j in range(2):
                d = 2 * zp + j

                @pl.when(d != g)
                def _():
                    remote(out.at[d], landed.at[g], out_s.at[d], out_r.at[g], (d, t)).start()

            @pl.when(i == 0)
            def _():
                forward_z(buf, s, r, 2)

            return carry

        lax.fori_loop(0, 4, step, 0)

    def gathered_sum(out, landed, out_r):
        total = out[g].astype(f32)
        for k in range(1, GROUPS):
            d = lax.rem(g + k, GROUPS)
            arrived(landed.at[d], out_r.at[d])
            total += landed[d].astype(f32)
        return total

    def finish_gather(buf, s):
        for i in range(14):
            left(buf.at[0, upper], s.at[i])

    def finish_sends(out, out_s):
        for k in range(1, GROUPS):
            left(out.at[0], out_s.at[lax.rem(g + k, GROUPS)])

    def with_sum(square_sum):
        high = square_sum.astype(bf16).astype(f32)
        lane = lax.broadcasted_iota(jnp.int32, (square_sum.shape[0], 128), 1)
        return jnp.where(
            lane == 0, high, jnp.where(lane == 1, square_sum - high, 0.0)
        ).astype(bf16)

    def placed(exchange, target):
        stacked = exchange[...].reshape(2 * rows, both).astype(f32)
        turned[...] = jnp.transpose(stacked, (1, 0))
        target[...] = turned[own_rows].astype(bf16)

    gather_start(vb, v_s, v_r)
    for i, (src, dst) in enumerate(weights):
        remote(src, dst.at[own_rows], w_s.at[i], w_r.at[i], sibling).start()

    def weight_ready(i):
        src, dst = weights[i]
        pltpu.make_async_copy(src, dst.at[own_rows], w_l.at[i]).wait()
        arrived(dst.at[own_rows], w_r.at[i])

    for i in range(3):
        weight_ready(i)
    mine = pl.ds(pl.multiple_of(c * rows, rows), rows)
    turned[...] = resid_both[...].astype(f32)
    resid_rows[...] = jnp.transpose(turned[...], (1, 0))
    project(vb, wo, v_s, v_r, c_out, c_in, c_s, c_r)
    attn = gathered_sum(c_out, c_in, c_r)
    att_x[c] = attn.astype(bf16)
    remote(att_x.at[c], att_x.at[c], o_s.at[0], o_r.at[0], sibling).start()
    resid = resid_rows[mine] + attn
    resid_rows[mine] = resid
    gain = jnp.transpose(gain_both[...].astype(f32), (1, 0))[:1]
    xb[g, :, :both] = (resid * gain).astype(bf16)
    xb[g, :, both:] = with_sum(jnp.sum(resid * resid, axis=1, keepdims=True))
    for k in (4, 3, 5, 2, 6, 1, 7):
        remote(xb.at[g], xb.at[g], x_s.at[k], x_r.at[g], other_group(k)).start()
    arrived(att_x.at[1 - c], o_r.at[0])
    placed(att_x, attended_ref)
    for i in range(3, 6):
        weight_ready(i)

    def first_products(i, carry):
        xp = lax.rem(x + 4 - order(i), 4)
        for j in range(2):
            d = 2 * xp + j

            @pl.when(d != g)
            def _():
                arrived(xb.at[d], x_r.at[d])

        block = xb[pl.ds(2 * xp, 2)].reshape(2 * rows, both + 128)
        pair = pl.ds(2 * xp, 2)
        lhs = block[:, :both]

        def product(w, start, width):
            return jnp.dot(
                lhs, w[:, start : start + width], preferred_element_type=f32
            ).astype(bf16).reshape(2, rows, width)

        for n in range(0, ff, 768):
            part_a[pair, :, n : n + 768] = product(wg, n, 768)
        part_a[pair, :, ff:] = product(wu, 0, A_EXTRA)
        remote(
            part_a.at[2 * xp + 1 - yh], a1_in.at[xp], a1_s.at[xp], a1_r.at[xp], y_peer
        ).start()
        for n in range(0, b_cols, 896):
            part_b[pair, :, n : n + 896] = product(wu, A_EXTRA + n, 896)
        part_b[pair, :, b_cols:] = block[:, both:].reshape(2, rows, 128)

        @pl.when(xp != z)
        def _():
            remote(part_b.at[pair], b1_in.at[z], b1_s.at[xp], b1_r.at[z], chip(xp)).start()

        return carry

    lax.fori_loop(0, 4, first_products, 0)

    def second_a(i, carry):
        xp = lax.rem(x + 4 - order(i), 4)
        arrived(a1_in.at[xp], a1_r.at[xp])
        a2_out[xp] = (
            part_a[2 * xp + yh].astype(f32) + a1_in[xp].astype(f32)
        ).astype(bf16)

        @pl.when(xp != z)
        def _():
            remote(a2_out.at[xp], a2_in.at[z], a2_s.at[xp], a2_r.at[z], chip(xp)).start()

        return carry

    lax.fori_loop(0, 3, second_a, 0)
    for k in (1, 3, 2):
        s = lax.rem(z + k, 4)
        arrived(b1_in.at[s], b1_r.at[s])

    def sum_b(j):
        total = part_b[2 * z + j].astype(f32)
        for k in (1, 2, 3):
            total += b1_in[lax.rem(z + k, 4), j].astype(f32)
        return total

    def total_squares(block):
        return block[:, b_cols : b_cols + 1] + block[:, b_cols + 1 : b_cols + 2]

    away = sum_b(1 - yh)
    b2_out[:, :b_cols] = away[:, :b_cols].astype(bf16)
    b2_out[:, b_cols:] = with_sum(total_squares(away))
    remote(b2_out, b2_in, b2_s.at[0], b2_r.at[0], y_peer).start()
    b_keep[...] = sum_b(yh)
    lax.fori_loop(3, 4, second_a, 0)
    arrived(b2_in, b2_r.at[0])
    for k in (1, 3, 2):
        s = lax.rem(z + k, 4)
        arrived(a2_in.at[s], a2_r.at[s])

    def sum_a(start, width):
        cols = slice(start, start + width)
        total = a2_out[z, :, cols].astype(f32)
        for k in (1, 2, 3):
            total += a2_in[lax.rem(z + k, 4), :, cols].astype(f32)
        return total

    def sum_b2(start, width):
        cols = slice(start, start + width)
        return b_keep[:, cols] + b2_in[:, cols].astype(f32)

    square_sum = total_squares(jnp.concatenate(
        [jnp.zeros((rows, b_cols), f32), sum_b2(b_cols, 128)], axis=1
    ))
    scale = lax.rsqrt(square_sum / D + norm_eps)

    def write_hidden(start, width, upward):
        gate = sum_a(start, width) * scale
        hb[q, :, start : start + width] = (
            gate / (1.0 + jnp.exp(-gate)) * (upward * scale)
        ).astype(bf16)

    write_hidden(0, A_EXTRA, sum_a(ff, A_EXTRA))
    for n in range(0, b_cols, 896):
        write_hidden(A_EXTRA + n, 896, sum_b2(n, 896))
    gather_start(hb, h_s, h_r)
    project(hb, wd, h_s, h_r, g_out, g_in, g_s, g_r)
    down = gathered_sum(g_out, g_in, g_r)
    lay_x[c] = (resid_rows[mine] + down).astype(bf16)
    remote(lay_x.at[c], lay_x.at[c], o_s.at[1], o_r.at[1], sibling).start()
    arrived(lay_x.at[1 - c], o_r.at[1])
    placed(lay_x, out_ref)

    for i, (src, dst) in enumerate(weights):
        left(src, w_s.at[i])
    finish_gather(vb, v_s)
    finish_gather(hb, h_s)
    finish_sends(c_out, c_s)
    finish_sends(g_out, g_s)
    for k in range(1, GROUPS):
        left(xb.at[0], x_s.at[k])
    for i in range(4):
        left(part_a.at[0], a1_s.at[i])
    for k in (1, 2, 3):
        s = lax.rem(z + k, 4)
        left(b1_in.at[0], b1_s.at[s])
        left(a2_out.at[0], a2_s.at[s])
    left(b2_out, b2_s.at[0])
    left(att_x.at[0], o_s.at[0])
    left(lay_x.at[0], o_s.at[1])


def run_layer(values, residual_in, norm_gain, out_proj, gate_proj, up_proj, down_proj):
    rows, width = values.shape
    total_rows, feats = residual_in.shape
    ff = gate_proj.shape[1]
    both = 2 * feats
    a_cols, b_cols = ff + A_EXTRA, ff - A_EXTRA + 128
    f32, bf16 = jnp.float32, jnp.bfloat16
    vmem = pl.BlockSpec(memory_space=pltpu.VMEM)
    hbm = pl.BlockSpec(memory_space=pl.ANY)
    dma = pltpu.SemaphoreType.DMA
    block = jax.ShapeDtypeStruct((feats, total_rows), bf16)
    attended, layer_out = pl.pallas_call(
        layer_kernel,
        name="layer",
        out_shape=(block, block),
        in_specs=[vmem, vmem, vmem, hbm, hbm, hbm, hbm],
        out_specs=(vmem, vmem),
        scratch_shapes=[
            pltpu.VMEM((both, width), bf16),
            pltpu.VMEM((both, ff), bf16),
            pltpu.VMEM((both, ff), bf16),
            pltpu.VMEM((both, ff), bf16),
            pltpu.VMEM((both, total_rows), bf16),
            pltpu.VMEM((feats, 128), bf16),
            pltpu.VMEM((both, 128), bf16),
            pltpu.VMEM((8, rows, width), bf16),
            pltpu.VMEM((8, rows, both), bf16),
            pltpu.VMEM((8, rows, both), bf16),
            pltpu.VMEM((8, rows, both + 128), bf16),
            pltpu.VMEM((8, rows, a_cols), bf16),
            pltpu.VMEM((8, rows, b_cols), bf16),
            pltpu.VMEM((4, rows, a_cols), bf16),
            pltpu.VMEM((4, rows, a_cols), bf16),
            pltpu.VMEM((4, rows, a_cols), bf16),
            pltpu.VMEM((4, 2, rows, b_cols), bf16),
            pltpu.VMEM((rows, b_cols), bf16),
            pltpu.VMEM((rows, b_cols), bf16),
            pltpu.VMEM((rows, b_cols), f32),
            pltpu.VMEM((8, rows, ff), bf16),
            pltpu.VMEM((8, rows, both), bf16),
            pltpu.VMEM((8, rows, both), bf16),
            pltpu.VMEM((total_rows, both), f32),
            pltpu.VMEM((2, rows, both), bf16),
            pltpu.VMEM((2, rows, both), bf16),
            pltpu.VMEM((both, total_rows), f32),
            dma((6,)), dma((6,)), dma((6,)), dma((14,)), dma((14,)),
            dma((8,)), dma((8,)), dma((8,)), dma((8,)),
            dma((4,)), dma((4,)), dma((4,)), dma((4,)), dma((4,)), dma((4,)), dma((1,)), dma((1,)),
            dma((14,)), dma((14,)), dma((8,)), dma((8,)), dma((2,)), dma((2,)),
        ],
        compiler_params=pltpu.CompilerParams(
            collective_id=1, has_side_effects=True, vmem_limit_bytes=56 << 20
        ),
        cost_estimate=pl.CostEstimate(
            flops=2 * total_rows * 8 * feats * (width + 3 * ff), bytes_accessed=10 << 20,
            transcendentals=1 << 20,
        ),
    )(
        values, jnp.swapaxes(residual_in, 0, 1), norm_gain[None, :], jnp.swapaxes(out_proj, 0, 1),
        gate_proj, up_proj, jnp.swapaxes(down_proj, 0, 1),
    )
    return jnp.swapaxes(attended, 0, 1), jnp.swapaxes(layer_out, 0, 1)


def shards(
    queries,
    kv_cache,
    lengths,
    dest_group,
    moved_slot,
    residual_in,
    norm_gain,
    up_value,
    out_proj,
    gate_proj,
    up_proj,
    down_proj,
):
    values = attend_values(lengths, dest_group, moved_slot, queries, kv_cache, up_value)
    return run_layer(values, residual_in, norm_gain, out_proj, gate_proj, up_proj, down_proj)


def solution(mesh):
    return jax.shard_map(
        shards,
        mesh=mesh,
        in_specs=(
            P(("dp", "tp"), None, None),
            P(("dp", "tp"), None, None),
            P(None, "tp", None),
            P(None, "tp"),
            P(None, "tp"),
            P("dp", "tp"),
            P("tp"),
            P("dp", None, None),
            P("dp", "tp"),
            P("tp", "dp"),
            P("tp", "dp"),
            P("dp", "tp"),
        ),
        out_specs=(P("dp", "tp"), P("dp", "tp")),
        check_vma=False,
    )
```

```python
import jax
import jax.numpy as jnp
from jax import lax
from jax.experimental import pallas as pl
from jax.experimental.pallas import tpu as pltpu
from jax.sharding import PartitionSpec as P

MESH = pl.DeviceIdType.MESH
KV = 512
GROUPS = 8
score_scale = 192.0 ** (-0.5)


D = 7168
norm_eps = 1e-06
A_COLS = 1024


def layer_kernel(
    length_ref, partner_ref, slot_ref, query_ref, cache_ref, up_ref, resid_ref, gain_ref,
    wo_ref, wg_ref, wu_ref, wd_ref, att_x, lay_x,
    query_buf, cache_buf, up_buf, lat_out, lat_in, wide, vals,
    wo, wg, wu, wd, resid_both, gain_own, gain_both,
    vb, c_out, c_in, cy_out, cy_in, xb, part_a, part_b, a1_in, a2, am_in, a_in, bm_in, b_in,
    b2_out, b2_in, b_keep, hb, g_out, g_in, gy_out, gy_in, resid_rows, turned,
    load_sem, up_sem, own_sem, l_s, l_r,
    w_l, w_s, w_r, v_s, v_r, c_s, c_r, x_s, x_r, a1_s, a1_r, a_s, a_r, b_s, b_r, b2_s, b2_r,
    h_s, h_r, g_s, g_r, o_s, o_r,
):
    g = lax.axis_index("dp")
    t = lax.axis_index("tp")
    c = lax.rem(t, 2)
    q = t // 2
    z = q // 2
    yh = lax.rem(q, 2)
    x = g // 2
    yl = lax.rem(g, 2)
    slots = query_ref.shape[0]
    heads = up_ref.shape[0]
    rows = GROUPS * slots
    feats = wo_ref.shape[0]
    ff = wg_ref.shape[1]
    both = 2 * feats
    b_half = ff - A_COLS
    b_cols = 2 * b_half
    half = rows // 2
    f32 = jnp.float32
    bf16 = jnp.bfloat16

    def other_group(k):
        return (lax.rem(g + k, GROUPS), t)

    def other_z(k):
        return (g, lax.rem(z + k, 4) * 4 + yh * 2 + c)

    def chip(zp):
        return (g, zp * 4 + yh * 2 + c)

    def other_x(k):
        return (lax.rem(x + k, 4) * 2 + yl, t)

    low_peer = (x * 2 + 1 - yl, t)
    y_peer = (g, z * 4 + (1 - yh) * 2 + c)
    sibling = (g, q * 2 + 1 - c)

    def remote(src, dst, send_sem, recv_sem, device):
        return pltpu.make_async_remote_copy(
            src_ref=src, dst_ref=dst, send_sem=send_sem, recv_sem=recv_sem,
            device_id=device, device_id_type=MESH,
        )

    def arrived(ref, sem):
        remote(ref, ref, sem, sem, sibling).wait_recv()

    def left(ref, sem):
        remote(ref, ref, sem, sem, sibling).wait_send()

    def order(i):
        return i + (i // 2) * (5 - 2 * i)

    def loads(r):
        return (
            pltpu.make_async_copy(query_ref.at[r], query_buf.at[r], load_sem.at[0, r]),
            pltpu.make_async_copy(cache_ref.at[r], cache_buf.at[r], load_sem.at[1, r]),
        )

    for r in range(slots):
        for copy in loads(r):
            copy.start()
    up_copy = pltpu.make_async_copy(up_ref, up_buf, up_sem)
    up_copy.start()
    barrier = pltpu.get_barrier_semaphore()
    greeted = [other_group(k) for k in range(1, GROUPS)]
    greeted += [other_z(k) for k in (1, 2, 3)] + [y_peer, sibling]
    for device in greeted:
        pl.semaphore_signal(barrier, inc=1, device_id=device, device_id_type=MESH)

    own_rows = pl.ds(pl.multiple_of(c * feats, feats), feats)
    gain_own[...] = jnp.transpose(
        jnp.broadcast_to(gain_ref[...].astype(f32), (128, feats)), (1, 0)
    ).astype(bf16)
    weights = (
        (wo_ref, wo), (resid_ref, resid_both), (gain_own, gain_both),
        (wg_ref, wg), (wu_ref, wu), (wd_ref, wd),
    )

    def start_weights():
        for i, (src, dst) in enumerate(weights):
            remote(src, dst.at[own_rows], w_s.at[i], w_r.at[i], sibling).start()
            pltpu.make_async_copy(src, dst.at[own_rows], w_l.at[i]).start()

    pl.semaphore_wait(barrier, len(greeted))

    upper = pl.ds(0, half)
    lower = pl.ds(half, half)

    def gather_start(buf, s, r):
        own_a = buf.at[q, upper]
        own_b = buf.at[q, lower]
        remote(own_a, own_a, s.at[0], r.at[0], y_peer).start()
        for k in (2, 1, 3):
            remote(own_b, own_b, s.at[k], r.at[k], other_z(k)).start()
        remote(own_b, own_b, s.at[10], r.at[10], y_peer).start()
        for k in (2, 1, 3):
            remote(own_a, own_a, s.at[3 + k], r.at[3 + k], other_z(k)).start()

    def forward_y(buf, s, r):
        block = buf.at[z * 2 + 1 - yh, upper]
        arrived(block, r.at[0])
        for k in (2, 1, 3):
            remote(block, block, s.at[6 + k], r.at[6 + k], other_z(k)).start()

    def forward_z(buf, s, r, k):
        block = buf.at[lax.rem(z + 4 - k, 4) * 2 + yh, lower]
        arrived(block, r.at[k])
        remote(block, block, s.at[10 + k], r.at[10 + k], y_peer).start()

    def project(buf, w, s, r, out, landed, out_s, out_r):
        forward_y(buf, s, r)
        forward_z(buf, s, r, 1)
        forward_z(buf, s, r, 3)

        def step(i, carry):
            k = jnp.where(i == 0, 0, 1 + lax.rem(i + 2 + x, 3))
            zp = lax.rem(z + 4 - k, 4)
            arrived(buf.at[0, lower], r.at[10 + k])

            @pl.when(k > 0)
            def _():
                arrived(buf.at[0, upper], r.at[3 + k])
                arrived(buf.at[0, upper], r.at[6 + k])

            left_rows = buf[pl.ds(2 * zp, 2)].reshape(2 * rows, buf.shape[2])
            product = lax.dot_general(
                left_rows, w[...], (((1,), (1,)), ((), ())), preferred_element_type=f32
            )
            out[pl.ds(2 * zp, 2)] = product.astype(bf16).reshape(2, rows, both)

            @pl.when(zp != x)
            def _():
                remote(
                    out.at[pl.ds(2 * zp, 2)], landed.at[x], out_s.at[zp], out_r.at[x],
                    (zp * 2 + yl, t),
                ).start()

            @pl.when(i == 0)
            def _():
                forward_z(buf, s, r, 2)

            return carry

        lax.fori_loop(0, 4, step, 0)

    def gathered_sum(out, landed, y_out, y_in, out_s, out_r):
        for k in (1, 3, 2):
            p = lax.rem(x + k, 4)
            arrived(landed.at[p], out_r.at[p])

        def over_x(j):
            total = out[2 * x + j].astype(f32)
            for k in (1, 3, 2):
                total += landed[lax.rem(x + k, 4), j].astype(f32)
            return total

        y_out[...] = over_x(1 - yl).astype(bf16)
        remote(y_out, y_in, out_s.at[4], out_r.at[4], low_peer).start()
        total = over_x(yl)
        arrived(y_in, out_r.at[4])
        return total + y_in[...].astype(f32)

    def finish_gather(buf, s):
        for i in range(14):
            left(buf.at[0, upper], s.at[i])

    def finish_sends(out, y_out, out_s):
        for k in (1, 2, 3):
            left(out.at[pl.ds(0, 2)], out_s.at[lax.rem(x + k, 4)])
        left(y_out, out_s.at[4])

    def with_sum(square_sum):
        high = square_sum.astype(bf16).astype(f32)
        lane = lax.broadcasted_iota(jnp.int32, (square_sum.shape[0], 128), 1)
        return jnp.where(
            lane == 0, high, jnp.where(lane == 1, square_sum - high, 0.0)
        ).astype(bf16)

    def send(k, r):
        p = lax.rem(g + k, GROUPS)
        return pltpu.make_async_remote_copy(
            src_ref=lat_out.at[pl.ds(r, 2), pl.ds(pl.multiple_of(p * heads, heads), heads)],
            dst_ref=lat_in.at[g, pl.ds(r, 2)],
            send_sem=l_s.at[k],
            recv_sem=l_r.at[g],
            device_id=(p, t),
            device_id_type=MESH,
        )

    def attend(r):
        for copy in loads(r):
            copy.wait()
        length = length_ref[g, r]
        cache = cache_buf[r]
        scores = lax.dot_general(
            query_buf[r], cache, (((0,), (0,)), ((), ())), preferred_element_type=jnp.float32
        )
        position = lax.broadcasted_iota(jnp.int32, scores.shape, 1)
        masked = jnp.where(position < length, scores * score_scale, -jnp.inf)
        largest = jnp.max(masked, axis=1, keepdims=True)
        expterm = jnp.exp(masked - largest)
        total = jnp.sum(expterm, axis=1, keepdims=True)
        weights = (expterm / total).astype(jnp.bfloat16)
        latent = lax.dot_general(
            weights, cache[:KV], (((1,), (1,)), ((), ())), preferred_element_type=jnp.float32
        )
        lat_out[r] = latent.astype(jnp.bfloat16)

    def pair(i, carry):
        attend(2 * i)
        attend(2 * i + 1)
        for k in (4, 3, 5, 2, 6, 1, 7):
            send(k, 2 * i).start()

        @pl.when(i == 0)
        def _():
            start_weights()

        return carry

    lax.fori_loop(0, slots // 2, pair, 0)
    own = pltpu.make_async_copy(
        lat_out.at[:, pl.ds(pl.multiple_of(g * heads, heads), heads)], lat_in.at[g], own_sem
    )
    own.start()
    own.wait()
    up_copy.wait()

    def widen(k, carry):
        s = lax.rem(g + k, GROUPS)

        @pl.when(k > 0)
        def _():
            pltpu.make_async_remote_copy(
                src_ref=lat_in.at[s], dst_ref=lat_in.at[s], send_sem=l_s.at[0],
                recv_sem=l_r.at[s], device_id=(s, t), device_id_type=MESH,
            ).wait_recv()

        step_rows = slots * heads
        block = lat_in[s].astype(jnp.float32).reshape(step_rows, KV)
        for lane in range(KV // 128):
            wide[lane, pl.ds(pl.multiple_of(s * step_rows, step_rows), step_rows)] = block[
                :, lane * 128 : (lane + 1) * 128
            ]
        return carry

    lax.fori_loop(0, GROUPS, widen, 0)
    count = GROUPS * slots
    for h in range(heads):
        head_rows = jnp.concatenate(
            [wide[lane, pl.ds(h, count, stride=heads), :] for lane in range(KV // 128)], axis=1
        )
        vals[:, h * 128 : (h + 1) * 128] = jnp.dot(
            head_rows.astype(jnp.bfloat16),
            up_buf[h],
            preferred_element_type=jnp.float32,
        ).astype(jnp.bfloat16)
    row = lax.broadcasted_iota(jnp.int32, (count, count), 0)
    column = lax.broadcasted_iota(jnp.int32, (count, count), 1)
    source = row
    for group in range(GROUPS):
        partner = partner_ref[group]
        own_row = group * slots + slot_ref[group]
        source = jnp.where(row == own_row, partner * slots + slot_ref[partner], source)
    place = jnp.where(column == source, 1.0, 0.0).astype(jnp.bfloat16)
    vb[q] = jnp.dot(place, vals[...], preferred_element_type=jnp.float32).astype(
        jnp.bfloat16
    )
    gather_start(vb, v_s, v_r)

    def weight_ready(i):
        src, dst = weights[i]
        pltpu.make_async_copy(src, dst.at[own_rows], w_l.at[i]).wait()
        arrived(dst.at[own_rows], w_r.at[i])

    for i in range(3):
        weight_ready(i)
    mine = pl.ds(pl.multiple_of(c * rows, rows), rows)
    turned[...] = resid_both[...].astype(f32)
    resid_rows[...] = jnp.transpose(turned[...], (1, 0))
    project(vb, wo, v_s, v_r, c_out, c_in, c_s, c_r)
    attn = gathered_sum(c_out, c_in, cy_out, cy_in, c_s, c_r)
    att_x[c] = attn.astype(bf16)
    remote(att_x.at[c], att_x.at[c], o_s.at[0], o_r.at[0], sibling).start()
    resid = resid_rows[mine] + attn
    resid_rows[mine] = resid
    gain = jnp.transpose(gain_both[...].astype(f32), (1, 0))[:1]
    xb[g, :, :both] = (resid * gain).astype(bf16)
    xb[g, :, both:] = with_sum(jnp.sum(resid * resid, axis=1, keepdims=True))
    remote(xb.at[g], xb.at[g], x_s.at[0], x_r.at[0], low_peer).start()
    for k in (1, 3, 2):
        remote(xb.at[g], xb.at[g], x_s.at[k], x_r.at[k], other_x(k)).start()
    low_block = xb.at[x * 2 + 1 - yl]
    arrived(low_block, x_r.at[0])
    for k in (1, 3, 2):
        remote(low_block, low_block, x_s.at[3 + k], x_r.at[3 + k], other_x(k)).start()
    for i in range(3, 6):
        weight_ready(i)

    def first_products(i, carry):
        k = order(i)
        xp = lax.rem(x + 4 - k, 4)

        @pl.when(k > 0)
        def _():
            arrived(xb.at[0], x_r.at[k])
            arrived(xb.at[0], x_r.at[3 + k])

        block = xb[pl.ds(2 * xp, 2)].reshape(2 * rows, both + 128)
        pair = pl.ds(2 * xp, 2)
        lhs = block[:, :both]

        def product(w, start, width):
            return jnp.dot(
                lhs, w[:, start : start + width], preferred_element_type=f32
            ).astype(bf16).reshape(2, rows, width)

        part_a[pair, :, :A_COLS] = product(wg, 0, A_COLS)
        part_a[pair, :, A_COLS:] = product(wu, 0, A_COLS)
        remote(
            part_a.at[2 * xp + 1 - yh], a1_in.at[xp], a1_s.at[xp], a1_r.at[xp], y_peer
        ).start()
        part_b[pair, :, :b_half] = product(wg, A_COLS, b_half)
        part_b[pair, :, b_half:b_cols] = product(wu, A_COLS, b_half)
        part_b[pair, :, b_cols:] = block[:, both:].reshape(2, rows, 128)
        role = lax.rem(xp + 4 - z, 4)

        @pl.when(role == 2)
        def _():
            for j in range(2):
                remote(
                    part_b.at[2 * xp + j], bm_in.at[j], b_s.at[j], b_r.at[j], other_z(1 + 2 * j)
                ).start()

        for j in range(2):

            @pl.when(role == 3 - 2 * j)
            def _():
                remote(
                    part_b.at[2 * xp + j], b_in.at[1 - j, j], b_s.at[2 + j], b_r.at[2 + j],
                    other_z(3 - 2 * j),
                ).start()

        return carry

    lax.fori_loop(0, 4, first_products, 0)
    halves = (upper, lower)

    def second_a(i, carry):
        xp = lax.rem(x + 4 - order(i), 4)
        arrived(a1_in.at[xp], a1_r.at[xp])
        a2[xp] = (part_a[2 * xp + yh].astype(f32) + a1_in[xp].astype(f32)).astype(bf16)
        role = lax.rem(xp + 4 - z, 4)

        @pl.when(role == 2)
        def _():
            for j in range(2):
                remote(
                    a2.at[xp, halves[j]], am_in.at[j], a_s.at[j], a_r.at[j], other_z(1 + 2 * j)
                ).start()

        for j in range(2):

            @pl.when(role == 3 - 2 * j)
            def _():
                remote(
                    a2.at[xp, halves[j]], a_in.at[1 - j, halves[j]], a_s.at[2 + j],
                    a_r.at[2 + j], other_z(3 - 2 * j),
                ).start()

        return carry

    def total_squares(block):
        return block[:, 0:1] + block[:, 1:2]

    def relay_b(j):
        block = 2 * lax.rem(z + 1 + 2 * j, 4) + j
        arrived(bm_in.at[j], b_r.at[j])
        total = part_b[block].astype(f32) + bm_in[j].astype(f32)
        part_b[block, :, :b_cols] = total[:, :b_cols].astype(bf16)
        part_b[block, :, b_cols:] = with_sum(total_squares(total[:, b_cols:]))
        remote(
            part_b.at[block], b_in.at[j, j], b_s.at[4 + j], b_r.at[4 + j], other_z(1 + 2 * j)
        ).start()

    def relay_a(j):
        block = lax.rem(z + 1 + 2 * j, 4)
        arrived(am_in.at[j], a_r.at[j])
        a2[block, halves[j]] = (
            a2[block, halves[j]].astype(f32) + am_in[j].astype(f32)
        ).astype(bf16)
        remote(
            a2.at[block, halves[j]], a_in.at[j, halves[j]], a_s.at[4 + j], a_r.at[4 + j],
            other_z(1 + 2 * j),
        ).start()

    lax.fori_loop(0, 1, second_a, 0)
    for j in range(2):
        relay_b(j)
    lax.fori_loop(1, 3, second_a, 0)
    for j in range(2):
        arrived(b_in.at[1 - j, j], b_r.at[2 + j])
        arrived(b_in.at[j, j], b_r.at[4 + j])

    def sum_b(j):
        return part_b[2 * z + j].astype(f32) + b_in[0, j].astype(f32) + b_in[1, j].astype(f32)

    away = sum_b(1 - yh)
    b2_out[:, :b_cols] = away[:, :b_cols].astype(bf16)
    b2_out[:, b_cols:] = with_sum(total_squares(away[:, b_cols:]))
    remote(b2_out, b2_in, b2_s.at[0], b2_r.at[0], y_peer).start()
    b_keep[...] = sum_b(yh)
    lax.fori_loop(3, 4, second_a, 0)
    for j in range(2):
        relay_a(j)
    arrived(b2_in, b2_r.at[0])

    def sum_b2(start, width):
        cols = slice(start, start + width)
        return b_keep[:, cols] + b2_in[:, cols].astype(f32)

    scale = lax.rsqrt(total_squares(sum_b2(b_cols, 128)) / D + norm_eps)

    def write_hidden(start, gate, upward):
        gate = gate * scale
        hb[q, :, start : start + gate.shape[1]] = (
            gate / (1.0 + jnp.exp(-gate)) * (upward * scale)
        ).astype(bf16)

    write_hidden(A_COLS, sum_b2(0, b_half), sum_b2(b_half, b_half))
    for j in range(2):
        arrived(a_in.at[1 - j, halves[j]], a_r.at[2 + j])
        arrived(a_in.at[j, halves[j]], a_r.at[4 + j])

    def sum_a(start):
        cols = slice(start, start + A_COLS)
        return (
            a2[z, :, cols].astype(f32) + a_in[0, :, cols].astype(f32)
            + a_in[1, :, cols].astype(f32)
        )

    write_hidden(0, sum_a(0), sum_a(A_COLS))
    gather_start(hb, h_s, h_r)
    project(hb, wd, h_s, h_r, g_out, g_in, g_s, g_r)
    down = gathered_sum(g_out, g_in, gy_out, gy_in, g_s, g_r)
    lay_x[c] = (resid_rows[mine] + down).astype(bf16)
    remote(lay_x.at[c], lay_x.at[c], o_s.at[1], o_r.at[1], sibling).start()
    arrived(att_x.at[1 - c], o_r.at[0])
    arrived(lay_x.at[1 - c], o_r.at[1])

    for k in range(1, GROUPS):
        left(lat_in.at[0], l_s.at[k])
    for i, (src, dst) in enumerate(weights):
        left(src, w_s.at[i])
    finish_gather(vb, v_s)
    finish_gather(hb, h_s)
    finish_sends(c_out, cy_out, c_s)
    finish_sends(g_out, gy_out, g_s)
    for k in range(7):
        left(xb.at[0], x_s.at[k])
    for i in range(4):
        left(part_a.at[0], a1_s.at[i])
    for i in range(6):
        left(part_b.at[0], b_s.at[i])
        left(a2.at[0, upper], a_s.at[i])
    left(b2_out, b2_s.at[0])
    left(att_x.at[0], o_s.at[0])
    left(lay_x.at[0], o_s.at[1])


def finish_kernel(att_ref, lay_ref, attended_ref, out_ref, turned):
    feats = attended_ref.shape[0]
    c = lax.rem(lax.axis_index("tp"), 2)
    own = pl.ds(pl.multiple_of(c * feats, feats), feats)
    for exchange, target in ((att_ref, attended_ref), (lay_ref, out_ref)):
        stacked = exchange[...].reshape(-1, 2 * feats).astype(jnp.float32)
        turned[...] = jnp.transpose(stacked, (1, 0))
        target[...] = turned[own].astype(target.dtype)


def run_layer(
    lengths, dest_group, moved_slot, queries, kv_cache, residual_in, norm_gain, up_value, out_proj,
    gate_proj, up_proj, down_proj,
):
    slots, all_heads, _ = queries.shape
    heads = up_value.shape[0]
    rows, width = GROUPS * slots, heads * 128
    queries = jnp.swapaxes(queries, 1, 2)
    kv_cache = jnp.swapaxes(kv_cache, 1, 2)
    total_rows, feats = residual_in.shape
    ff = gate_proj.shape[1]
    both = 2 * feats
    a_cols, b_cols = 2 * A_COLS, 2 * (ff - A_COLS) + 128
    f32, bf16 = jnp.float32, jnp.bfloat16
    vmem = pl.BlockSpec(memory_space=pltpu.VMEM)
    smem = pl.BlockSpec(memory_space=pltpu.SMEM)
    hbm = pl.BlockSpec(memory_space=pl.ANY)
    dma = pltpu.SemaphoreType.DMA
    block = jax.ShapeDtypeStruct((2, rows, both), bf16)
    turned = jax.ShapeDtypeStruct((feats, total_rows), bf16)
    att_x, lay_x = pl.pallas_call(
        layer_kernel,
        name="layer",
        out_shape=(block, block),
        in_specs=[smem, smem, smem, hbm, hbm, hbm, hbm, vmem, hbm, hbm, hbm, hbm],
        out_specs=(vmem, vmem),
        scratch_shapes=[
            pltpu.VMEM(queries.shape, bf16),
            pltpu.VMEM(kv_cache.shape, bf16),
            pltpu.VMEM(up_value.shape, bf16),
            pltpu.VMEM((slots, all_heads, KV), bf16),
            pltpu.VMEM((GROUPS, slots, heads, KV), bf16),
            pltpu.VMEM((KV // 128, rows * heads, 128), f32),
            pltpu.VMEM((rows, width), bf16),
            pltpu.VMEM((both, width), bf16),
            pltpu.VMEM((both, ff), bf16),
            pltpu.VMEM((both, ff), bf16),
            pltpu.VMEM((both, ff), bf16),
            pltpu.VMEM((both, total_rows), bf16),
            pltpu.VMEM((feats, 128), bf16),
            pltpu.VMEM((both, 128), bf16),
            pltpu.VMEM((8, rows, width), bf16),
            pltpu.VMEM((8, rows, both), bf16),
            pltpu.VMEM((4, 2, rows, both), bf16),
            pltpu.VMEM((rows, both), bf16),
            pltpu.VMEM((rows, both), bf16),
            pltpu.VMEM((8, rows, both + 128), bf16),
            pltpu.VMEM((8, rows, a_cols), bf16),
            pltpu.VMEM((8, rows, b_cols), bf16),
            pltpu.VMEM((4, rows, a_cols), bf16),
            pltpu.VMEM((4, rows, a_cols), bf16),
            pltpu.VMEM((2, rows // 2, a_cols), bf16),
            pltpu.VMEM((2, rows, a_cols), bf16),
            pltpu.VMEM((2, rows, b_cols), bf16),
            pltpu.VMEM((2, 2, rows, b_cols), bf16),
            pltpu.VMEM((rows, b_cols), bf16),
            pltpu.VMEM((rows, b_cols), bf16),
            pltpu.VMEM((rows, b_cols), f32),
            pltpu.VMEM((8, rows, ff), bf16),
            pltpu.VMEM((8, rows, both), bf16),
            pltpu.VMEM((4, 2, rows, both), bf16),
            pltpu.VMEM((rows, both), bf16),
            pltpu.VMEM((rows, both), bf16),
            pltpu.VMEM((total_rows, both), f32),
            pltpu.VMEM((both, total_rows), f32),
            dma((2, slots)), dma, dma, dma((8,)), dma((8,)),
            dma((6,)), dma((6,)), dma((6,)), dma((14,)), dma((14,)),
            dma((5,)), dma((5,)), dma((7,)), dma((7,)),
            dma((4,)), dma((4,)), dma((6,)), dma((6,)), dma((6,)), dma((6,)), dma((1,)), dma((1,)),
            dma((14,)), dma((14,)), dma((5,)), dma((5,)), dma((2,)), dma((2,)),
        ],
        compiler_params=pltpu.CompilerParams(
            collective_id=0, has_side_effects=True, vmem_limit_bytes=62 << 20
        ),
        cost_estimate=pl.CostEstimate(
            flops=2 * total_rows * 8 * feats * (width + 3 * ff), bytes_accessed=30 << 20,
            transcendentals=1 << 20,
        ),
    )(
        lengths[:, 0, :], dest_group[:, 0], moved_slot[:, 0], queries, kv_cache, up_value,
        jnp.swapaxes(residual_in, 0, 1), norm_gain[None, :], jnp.swapaxes(out_proj, 0, 1),
        gate_proj, up_proj, jnp.swapaxes(down_proj, 0, 1),
    )
    attended, layer_out = pl.pallas_call(
        finish_kernel,
        name="finish",
        out_shape=(turned, turned),
        in_specs=[vmem, vmem],
        out_specs=(vmem, vmem),
        scratch_shapes=[pltpu.VMEM((both, total_rows), f32)],
    )(att_x, lay_x)
    return jnp.swapaxes(attended, 0, 1), jnp.swapaxes(layer_out, 0, 1)


def shards(
    queries,
    kv_cache,
    lengths,
    dest_group,
    moved_slot,
    residual_in,
    norm_gain,
    up_value,
    out_proj,
    gate_proj,
    up_proj,
    down_proj,
):
    return run_layer(
        lengths, dest_group, moved_slot, queries, kv_cache, residual_in, norm_gain, up_value,
        out_proj, gate_proj, up_proj, down_proj,
    )


def solution(mesh):
    return jax.shard_map(
        shards,
        mesh=mesh,
        in_specs=(
            P(("dp", "tp"), None, None),
            P(("dp", "tp"), None, None),
            P(None, "tp", None),
            P(None, "tp"),
            P(None, "tp"),
            P("dp", "tp"),
            P("tp"),
            P("dp", None, None),
            P("dp", "tp"),
            P("tp", "dp"),
            P("tp", "dp"),
            P("dp", "tp"),
        ),
        out_specs=(P("dp", "tp"), P("dp", "tp")),
        check_vma=False,
    )
```

```python
import jax
import jax.numpy as jnp
from jax import lax
from jax.experimental import pallas as pl
from jax.experimental.pallas import tpu as pltpu
from jax.sharding import PartitionSpec as P

MESH = pl.DeviceIdType.MESH
KV = 512
GROUPS = 8
exponent_scale = 192.0 ** (-0.5) * 1.4426950408889634


D = 7168
norm_eps = 1e-06
A_COLS = 1024


def layer_kernel(
    length_ref, partner_ref, slot_ref, query_ref, cache_ref, up_ref, resid_ref, gain_ref,
    wo_ref, wg_ref, wu_ref, wd_ref, att_x, lay_x,
    query_buf, cache_buf, up_buf, lat_out, lat_in, wide, vals,
    wo, wg, wu, wd, resid_both, gain_own, gain_both,
    vb, c_out, c_in, cy_out, cy_in, xb, part_a, part_b, a1_in, a2, am_in, a_in, bm_in, b_in,
    b2_out, b2_in, b_keep, hb, g_out, g_in, gy_out, gy_in, resid_rows, turned,
    load_sem, up_sem, own_sem, l_s, l_r,
    w_l, w_s, w_r, v_s, v_r, c_s, c_r, x_s, x_r, a1_s, a1_r, a_s, a_r, b_s, b_r, b2_s, b2_r,
    h_s, h_r, g_s, g_r, o_s, o_r,
):
    g = lax.axis_index("dp")
    t = lax.axis_index("tp")
    c = lax.rem(t, 2)
    q = t // 2
    z = q // 2
    yh = lax.rem(q, 2)
    x = g // 2
    yl = lax.rem(g, 2)
    slots = query_ref.shape[0]
    heads = up_ref.shape[0]
    rows = GROUPS * slots
    feats = wo_ref.shape[0]
    ff = wg_ref.shape[1]
    both = 2 * feats
    b_half = ff - A_COLS
    b_cols = 2 * b_half
    half = rows // 2
    f32 = jnp.float32
    bf16 = jnp.bfloat16

    def other_group(k):
        return (lax.rem(g + k, GROUPS), t)

    def other_z(k):
        return (g, lax.rem(z + k, 4) * 4 + yh * 2 + c)

    def chip(zp):
        return (g, zp * 4 + yh * 2 + c)

    def other_x(k):
        return (lax.rem(x + k, 4) * 2 + yl, t)

    low_peer = (x * 2 + 1 - yl, t)
    y_peer = (g, z * 4 + (1 - yh) * 2 + c)
    sibling = (g, q * 2 + 1 - c)

    def remote(src, dst, send_sem, recv_sem, device):
        return pltpu.make_async_remote_copy(
            src_ref=src, dst_ref=dst, send_sem=send_sem, recv_sem=recv_sem,
            device_id=device, device_id_type=MESH,
        )

    def arrived(ref, sem):
        remote(ref, ref, sem, sem, sibling).wait_recv()

    def left(ref, sem):
        remote(ref, ref, sem, sem, sibling).wait_send()

    def order(i):
        return i + (i // 2) * (5 - 2 * i)

    def loads(r):
        return (
            pltpu.make_async_copy(query_ref.at[r], query_buf.at[r], load_sem.at[0, r]),
            pltpu.make_async_copy(cache_ref.at[r], cache_buf.at[r], load_sem.at[1, r]),
        )

    for r in range(slots):
        for copy in loads(r):
            copy.start()
    up_copy = pltpu.make_async_copy(up_ref, up_buf, up_sem)
    up_copy.start()
    barrier = pltpu.get_barrier_semaphore()
    greeted = [other_group(k) for k in range(1, GROUPS)]
    greeted += [other_z(k) for k in (1, 2, 3)] + [y_peer, sibling]
    for device in greeted:
        pl.semaphore_signal(barrier, inc=1, device_id=device, device_id_type=MESH)

    own_rows = pl.ds(pl.multiple_of(c * feats, feats), feats)
    gain_own[...] = jnp.transpose(
        jnp.broadcast_to(gain_ref[...].astype(f32), (128, feats)), (1, 0)
    ).astype(bf16)
    weights = (
        (wo_ref, wo), (resid_ref, resid_both), (gain_own, gain_both),
        (wg_ref, wg), (wu_ref, wu), (wd_ref, wd),
    )

    def start_weights():
        for i, (src, dst) in enumerate(weights):
            remote(src, dst.at[own_rows], w_s.at[i], w_r.at[i], sibling).start()
            pltpu.make_async_copy(src, dst.at[own_rows], w_l.at[i]).start()

    pl.semaphore_wait(barrier, len(greeted))

    upper = pl.ds(0, half)
    lower = pl.ds(half, half)

    quarter = half // 2
    first = pl.ds(0, quarter)
    second = pl.ds(quarter, quarter)
    third = pl.ds(half, quarter)
    fourth = pl.ds(half + quarter, quarter)
    over_z = (other_z, y_peer, lambda k: lax.rem(z + 4 - k, 4) * 2 + yh,
              lambda k: lax.rem(z + 4 - k, 4) * 2 + 1 - yh)
    over_x = (other_x, low_peer, lambda k: lax.rem(x + 4 - k, 4) * 2 + yl,
              lambda k: lax.rem(x + 4 - k, 4) * 2 + 1 - yl)

    def push(ref, s, r, i, device):
        remote(ref, ref, s.at[i], r.at[i], device).start()

    def gather_start(buf, s, r, ways):
        ring, peer, near, far = ways
        own = buf.at[near(0)]
        push(own.at[upper], s, r, 0, peer)
        push(own.at[lower], s, r, 1, ring(1))
        push(own.at[lower], s, r, 2, ring(3))
        push(own.at[upper], s, r, 3, ring(1))
        push(own.at[upper], s, r, 4, ring(3))
        push(own.at[lower], s, r, 5, peer)

    def gather_relay(buf, s, r, ways):
        ring, peer, near, far = ways
        block = buf.at[far(0), upper]
        arrived(block, r.at[0])
        push(block, s, r, 6, ring(1))
        push(block, s, r, 7, ring(3))
        arrived(block, r.at[1])
        push(buf.at[near(1), third], s, r, 8, ring(1))
        push(buf.at[near(1), lower], s, r, 9, peer)
        arrived(block, r.at[2])
        push(buf.at[near(3), fourth], s, r, 10, ring(3))
        push(buf.at[near(3), lower], s, r, 11, peer)
        arrived(block, r.at[3])
        push(buf.at[near(1), first], s, r, 12, ring(1))
        arrived(block, r.at[4])
        push(buf.at[near(3), second], s, r, 13, ring(3))

    def gather_step(buf, s, r, ways, i):
        ring, peer, near, far = ways
        block = buf.at[far(0), upper]
        piece = buf.at[far(0), first]

        @pl.when(i == 0)
        def _():
            arrived(block, r.at[5])

        @pl.when(i == 1)
        def _():
            arrived(block, r.at[6])
            push(buf.at[far(1), first], s, r, 14, ring(1))
            arrived(block, r.at[7])
            push(buf.at[far(3), second], s, r, 15, ring(3))
            arrived(piece, r.at[8])
            push(buf.at[near(2), third], s, r, 16, peer)
            arrived(piece, r.at[10])
            push(buf.at[near(2), fourth], s, r, 17, peer)
            arrived(block, r.at[9])

        @pl.when(i == 2)
        def _():
            arrived(block, r.at[11])

        @pl.when(i == 3)
        def _():
            for j in range(12, 18):
                arrived(piece, r.at[j])

    def finish_gather(buf, s):
        for i in range(18):
            left(buf.at[0, upper if i in (0, 1, 2, 3, 4, 5, 6, 7, 9, 11) else first], s.at[i])

    def project(buf, w, s, r, out, landed, out_s, out_r):
        gather_relay(buf, s, r, over_z)

        def step(i, carry):
            zp = lax.rem(z + 4 - order(i), 4)
            gather_step(buf, s, r, over_z, i)
            left_rows = buf[pl.ds(2 * zp, 2)].reshape(2 * rows, buf.shape[2])
            product = lax.dot_general(
                left_rows, w[...], (((1,), (1,)), ((), ())), preferred_element_type=f32
            )
            out[pl.ds(2 * zp, 2)] = product.astype(bf16).reshape(2, rows, both)

            @pl.when(zp != x)
            def _():
                remote(
                    out.at[pl.ds(2 * zp, 2)], landed.at[x], out_s.at[zp], out_r.at[x],
                    (zp * 2 + yl, t),
                ).start()

            return carry

        lax.fori_loop(0, 4, step, 0)

    def gathered_sum(out, landed, y_out, y_in, out_s, out_r):
        for k in (1, 3, 2):
            p = lax.rem(x + k, 4)
            arrived(landed.at[p], out_r.at[p])

        def over_x(j):
            total = out[2 * x + j].astype(f32)
            for k in (1, 3, 2):
                total += landed[lax.rem(x + k, 4), j].astype(f32)
            return total

        y_out[...] = over_x(1 - yl).astype(bf16)
        remote(y_out, y_in, out_s.at[4], out_r.at[4], low_peer).start()
        total = over_x(yl)
        arrived(y_in, out_r.at[4])
        return total + y_in[...].astype(f32)

    def finish_sends(out, y_out, out_s):
        for k in (1, 2, 3):
            left(out.at[pl.ds(0, 2)], out_s.at[lax.rem(x + k, 4)])
        left(y_out, out_s.at[4])

    def with_sum(square_sum):
        high = square_sum.astype(bf16).astype(f32)
        lane = lax.broadcasted_iota(jnp.int32, (square_sum.shape[0], 128), 1)
        return jnp.where(
            lane == 0, high, jnp.where(lane == 1, square_sum - high, 0.0)
        ).astype(bf16)

    def send(k, r):
        p = lax.rem(g + k, GROUPS)
        return pltpu.make_async_remote_copy(
            src_ref=lat_out.at[pl.ds(r, 2), pl.ds(pl.multiple_of(p * heads, heads), heads)],
            dst_ref=lat_in.at[g, pl.ds(r, 2)],
            send_sem=l_s.at[k],
            recv_sem=l_r.at[g],
            device_id=(p, t),
            device_id_type=MESH,
        )

    def attend(r):
        for copy in loads(r):
            copy.wait()
        length = length_ref[g, r]
        cache = cache_buf[r]
        scores = lax.dot_general(
            query_buf[r], cache, (((0,), (0,)), ((), ())), preferred_element_type=jnp.float32
        )
        position = lax.broadcasted_iota(jnp.int32, scores.shape, 1)
        masked = jnp.where(position < length, scores, -jnp.inf)
        largest = jnp.max(masked, axis=1, keepdims=True)
        expterm = jnp.exp2((masked - largest) * exponent_scale)
        total = jnp.sum(expterm, axis=1, keepdims=True)
        latent = lax.dot_general(
            expterm.astype(jnp.bfloat16), cache[:KV], (((1,), (1,)), ((), ())),
            preferred_element_type=jnp.float32,
        )
        lat_out[r] = (latent * (1.0 / total)).astype(jnp.bfloat16)

    def pair(i, carry):
        attend(2 * i)
        attend(2 * i + 1)
        for k in (4, 3, 5, 2, 6, 1, 7):
            send(k, 2 * i).start()

        @pl.when(i == 0)
        def _():
            start_weights()

        return carry

    lax.fori_loop(0, slots // 2, pair, 0)
    own = pltpu.make_async_copy(
        lat_out.at[:, pl.ds(pl.multiple_of(g * heads, heads), heads)], lat_in.at[g], own_sem
    )
    own.start()
    own.wait()
    up_copy.wait()

    def widen(k, carry):
        s = lax.rem(g + k, GROUPS)

        @pl.when(k > 0)
        def _():
            pltpu.make_async_remote_copy(
                src_ref=lat_in.at[s], dst_ref=lat_in.at[s], send_sem=l_s.at[0],
                recv_sem=l_r.at[s], device_id=(s, t), device_id_type=MESH,
            ).wait_recv()

        step_rows = slots * heads
        block = lat_in[s].astype(jnp.float32).reshape(step_rows, KV)
        for lane in range(KV // 128):
            wide[lane, pl.ds(pl.multiple_of(s * step_rows, step_rows), step_rows)] = block[
                :, lane * 128 : (lane + 1) * 128
            ]
        return carry

    lax.fori_loop(0, GROUPS, widen, 0)
    count = GROUPS * slots
    for h in range(heads):
        head_rows = jnp.concatenate(
            [wide[lane, pl.ds(h, count, stride=heads), :] for lane in range(KV // 128)], axis=1
        )
        vals[:, h * 128 : (h + 1) * 128] = jnp.dot(
            head_rows.astype(jnp.bfloat16),
            up_buf[h],
            preferred_element_type=jnp.float32,
        ).astype(jnp.bfloat16)
    row = lax.broadcasted_iota(jnp.int32, (count, count), 0)
    column = lax.broadcasted_iota(jnp.int32, (count, count), 1)
    source = row
    for group in range(GROUPS):
        partner = partner_ref[group]
        own_row = group * slots + slot_ref[group]
        source = jnp.where(row == own_row, partner * slots + slot_ref[partner], source)
    place = jnp.where(column == source, 1.0, 0.0).astype(jnp.bfloat16)
    vb[q] = jnp.dot(place, vals[...], preferred_element_type=jnp.float32).astype(
        jnp.bfloat16
    )
    gather_start(vb, v_s, v_r, over_z)

    def weight_ready(i):
        src, dst = weights[i]
        pltpu.make_async_copy(src, dst.at[own_rows], w_l.at[i]).wait()
        arrived(dst.at[own_rows], w_r.at[i])

    for i in range(3):
        weight_ready(i)
    mine = pl.ds(pl.multiple_of(c * rows, rows), rows)
    turned[...] = resid_both[...].astype(f32)
    resid_rows[...] = jnp.transpose(turned[...], (1, 0))
    project(vb, wo, v_s, v_r, c_out, c_in, c_s, c_r)
    attn = gathered_sum(c_out, c_in, cy_out, cy_in, c_s, c_r)
    att_x[c] = attn.astype(bf16)
    remote(att_x.at[c], att_x.at[c], o_s.at[0], o_r.at[0], sibling).start()
    resid = resid_rows[mine] + attn
    resid_rows[mine] = resid
    gain = jnp.transpose(gain_both[...].astype(f32), (1, 0))[:1]
    xb[g, :, :both] = (resid * gain).astype(bf16)
    xb[g, :, both:] = with_sum(jnp.sum(resid * resid, axis=1, keepdims=True))
    gather_start(xb, x_s, x_r, over_x)
    for i in range(3, 6):
        weight_ready(i)

    gather_relay(xb, x_s, x_r, over_x)

    def first_products(i, carry):
        xp = lax.rem(x + 4 - order(i), 4)
        gather_step(xb, x_s, x_r, over_x, i)
        block = xb[pl.ds(2 * xp, 2)].reshape(2 * rows, both + 128)
        pair = pl.ds(2 * xp, 2)
        lhs = block[:, :both]

        def product(w, start, width):
            return jnp.dot(
                lhs, w[:, start : start + width], preferred_element_type=f32
            ).astype(bf16).reshape(2, rows, width)

        part_a[pair, :, :A_COLS] = product(wg, 0, A_COLS)
        part_a[pair, :, A_COLS:] = product(wu, 0, A_COLS)
        remote(
            part_a.at[2 * xp + 1 - yh], a1_in.at[xp], a1_s.at[xp], a1_r.at[xp], y_peer
        ).start()
        part_b[pair, :, :b_half] = product(wg, A_COLS, b_half)
        part_b[pair, :, b_half:b_cols] = product(wu, A_COLS, b_half)
        part_b[pair, :, b_cols:] = block[:, both:].reshape(2, rows, 128)
        role = lax.rem(xp + 4 - z, 4)

        @pl.when(role == 2)
        def _():
            for j in range(2):
                remote(
                    part_b.at[2 * xp + j], bm_in.at[j], b_s.at[j], b_r.at[j], other_z(1 + 2 * j)
                ).start()

        for j in range(2):

            @pl.when(role == 3 - 2 * j)
            def _():
                remote(
                    part_b.at[2 * xp + j], b_in.at[1 - j, j], b_s.at[2 + j], b_r.at[2 + j],
                    other_z(3 - 2 * j),
                ).start()

        return carry

    lax.fori_loop(0, 4, first_products, 0)
    halves = (upper, lower)

    def second_a(i, carry):
        xp = lax.rem(x + 4 - order(i), 4)
        arrived(a1_in.at[xp], a1_r.at[xp])
        a2[xp] = (part_a[2 * xp + yh].astype(f32) + a1_in[xp].astype(f32)).astype(bf16)
        role = lax.rem(xp + 4 - z, 4)

        @pl.when(role == 2)
        def _():
            for j in range(2):
                remote(
                    a2.at[xp, halves[j]], am_in.at[j], a_s.at[j], a_r.at[j], other_z(1 + 2 * j)
                ).start()

        for j in range(2):

            @pl.when(role == 3 - 2 * j)
            def _():
                remote(
                    a2.at[xp, halves[j]], a_in.at[1 - j, halves[j]], a_s.at[2 + j],
                    a_r.at[2 + j], other_z(3 - 2 * j),
                ).start()

        return carry

    def total_squares(block):
        return block[:, 0:1] + block[:, 1:2]

    def relay_b(j):
        block = 2 * lax.rem(z + 1 + 2 * j, 4) + j
        arrived(bm_in.at[j], b_r.at[j])
        total = part_b[block].astype(f32) + bm_in[j].astype(f32)
        part_b[block, :, :b_cols] = total[:, :b_cols].astype(bf16)
        part_b[block, :, b_cols:] = with_sum(total_squares(total[:, b_cols:]))
        remote(
            part_b.at[block], b_in.at[j, j], b_s.at[4 + j], b_r.at[4 + j], other_z(1 + 2 * j)
        ).start()

    def relay_a(j):
        block = lax.rem(z + 1 + 2 * j, 4)
        arrived(am_in.at[j], a_r.at[j])
        a2[block, halves[j]] = (
            a2[block, halves[j]].astype(f32) + am_in[j].astype(f32)
        ).astype(bf16)
        remote(
            a2.at[block, halves[j]], a_in.at[j, halves[j]], a_s.at[4 + j], a_r.at[4 + j],
            other_z(1 + 2 * j),
        ).start()

    lax.fori_loop(0, 1, second_a, 0)
    for j in range(2):
        relay_b(j)
    lax.fori_loop(1, 3, second_a, 0)
    for j in range(2):
        arrived(b_in.at[1 - j, j], b_r.at[2 + j])
        arrived(b_in.at[j, j], b_r.at[4 + j])

    def sum_b(j):
        return part_b[2 * z + j].astype(f32) + b_in[0, j].astype(f32) + b_in[1, j].astype(f32)

    away = sum_b(1 - yh)
    b2_out[:, :b_cols] = away[:, :b_cols].astype(bf16)
    b2_out[:, b_cols:] = with_sum(total_squares(away[:, b_cols:]))
    remote(b2_out, b2_in, b2_s.at[0], b2_r.at[0], y_peer).start()
    b_keep[...] = sum_b(yh)
    lax.fori_loop(3, 4, second_a, 0)
    for j in range(2):
        relay_a(j)
    arrived(b2_in, b2_r.at[0])

    def sum_b2(start, width):
        cols = slice(start, start + width)
        return b_keep[:, cols] + b2_in[:, cols].astype(f32)

    scale = lax.rsqrt(total_squares(sum_b2(b_cols, 128)) / D + norm_eps)

    def write_hidden(start, gate, upward):
        gate = gate * scale
        hb[q, :, start : start + gate.shape[1]] = (
            gate / (1.0 + jnp.exp(-gate)) * (upward * scale)
        ).astype(bf16)

    write_hidden(A_COLS, sum_b2(0, b_half), sum_b2(b_half, b_half))
    for j in range(2):
        arrived(a_in.at[1 - j, halves[j]], a_r.at[2 + j])
        arrived(a_in.at[j, halves[j]], a_r.at[4 + j])

    def sum_a(start):
        cols = slice(start, start + A_COLS)
        return (
            a2[z, :, cols].astype(f32) + a_in[0, :, cols].astype(f32)
            + a_in[1, :, cols].astype(f32)
        )

    write_hidden(0, sum_a(0), sum_a(A_COLS))
    gather_start(hb, h_s, h_r, over_z)
    project(hb, wd, h_s, h_r, g_out, g_in, g_s, g_r)
    down = gathered_sum(g_out, g_in, gy_out, gy_in, g_s, g_r)
    lay_x[c] = (resid_rows[mine] + down).astype(bf16)
    remote(lay_x.at[c], lay_x.at[c], o_s.at[1], o_r.at[1], sibling).start()
    arrived(att_x.at[1 - c], o_r.at[0])
    arrived(lay_x.at[1 - c], o_r.at[1])

    for k in range(1, GROUPS):
        left(lat_in.at[0], l_s.at[k])
    for i, (src, dst) in enumerate(weights):
        left(src, w_s.at[i])
    finish_gather(vb, v_s)
    finish_gather(hb, h_s)
    finish_sends(c_out, cy_out, c_s)
    finish_sends(g_out, gy_out, g_s)
    finish_gather(xb, x_s)
    for i in range(4):
        left(part_a.at[0], a1_s.at[i])
    for i in range(6):
        left(part_b.at[0], b_s.at[i])
        left(a2.at[0, upper], a_s.at[i])
    left(b2_out, b2_s.at[0])
    left(att_x.at[0], o_s.at[0])
    left(lay_x.at[0], o_s.at[1])


def finish_kernel(att_ref, lay_ref, attended_ref, out_ref, turned):
    feats = attended_ref.shape[0]
    c = lax.rem(lax.axis_index("tp"), 2)
    own = pl.ds(pl.multiple_of(c * feats, feats), feats)
    for exchange, target in ((att_ref, attended_ref), (lay_ref, out_ref)):
        stacked = exchange[...].reshape(-1, 2 * feats).astype(jnp.float32)
        turned[...] = jnp.transpose(stacked, (1, 0))
        target[...] = turned[own].astype(target.dtype)


def run_layer(
    lengths, dest_group, moved_slot, queries, kv_cache, residual_in, norm_gain, up_value, out_proj,
    gate_proj, up_proj, down_proj,
):
    slots, all_heads, _ = queries.shape
    heads = up_value.shape[0]
    rows, width = GROUPS * slots, heads * 128
    queries = jnp.swapaxes(queries, 1, 2)
    kv_cache = jnp.swapaxes(kv_cache, 1, 2)
    total_rows, feats = residual_in.shape
    ff = gate_proj.shape[1]
    both = 2 * feats
    a_cols, b_cols = 2 * A_COLS, 2 * (ff - A_COLS) + 128
    f32, bf16 = jnp.float32, jnp.bfloat16
    vmem = pl.BlockSpec(memory_space=pltpu.VMEM)
    smem = pl.BlockSpec(memory_space=pltpu.SMEM)
    hbm = pl.BlockSpec(memory_space=pl.ANY)
    dma = pltpu.SemaphoreType.DMA
    block = jax.ShapeDtypeStruct((2, rows, both), bf16)
    turned = jax.ShapeDtypeStruct((feats, total_rows), bf16)
    att_x, lay_x = pl.pallas_call(
        layer_kernel,
        name="layer",
        out_shape=(block, block),
        in_specs=[smem, smem, smem, hbm, hbm, hbm, hbm, vmem, hbm, hbm, hbm, hbm],
        out_specs=(vmem, vmem),
        scratch_shapes=[
            pltpu.VMEM(queries.shape, bf16),
            pltpu.VMEM(kv_cache.shape, bf16),
            pltpu.VMEM(up_value.shape, bf16),
            pltpu.VMEM((slots, all_heads, KV), bf16),
            pltpu.VMEM((GROUPS, slots, heads, KV), bf16),
            pltpu.VMEM((KV // 128, rows * heads, 128), f32),
            pltpu.VMEM((rows, width), bf16),
            pltpu.VMEM((both, width), bf16),
            pltpu.VMEM((both, ff), bf16),
            pltpu.VMEM((both, ff), bf16),
            pltpu.VMEM((both, ff), bf16),
            pltpu.VMEM((both, total_rows), bf16),
            pltpu.VMEM((feats, 128), bf16),
            pltpu.VMEM((both, 128), bf16),
            pltpu.VMEM((8, rows, width), bf16),
            pltpu.VMEM((8, rows, both), bf16),
            pltpu.VMEM((4, 2, rows, both), bf16),
            pltpu.VMEM((rows, both), bf16),
            pltpu.VMEM((rows, both), bf16),
            pltpu.VMEM((8, rows, both + 128), bf16),
            pltpu.VMEM((8, rows, a_cols), bf16),
            pltpu.VMEM((8, rows, b_cols), bf16),
            pltpu.VMEM((4, rows, a_cols), bf16),
            pltpu.VMEM((4, rows, a_cols), bf16),
            pltpu.VMEM((2, rows // 2, a_cols), bf16),
            pltpu.VMEM((2, rows, a_cols), bf16),
            pltpu.VMEM((2, rows, b_cols), bf16),
            pltpu.VMEM((2, 2, rows, b_cols), bf16),
            pltpu.VMEM((rows, b_cols), bf16),
            pltpu.VMEM((rows, b_cols), bf16),
            pltpu.VMEM((rows, b_cols), f32),
            pltpu.VMEM((8, rows, ff), bf16),
            pltpu.VMEM((8, rows, both), bf16),
            pltpu.VMEM((4, 2, rows, both), bf16),
            pltpu.VMEM((rows, both), bf16),
            pltpu.VMEM((rows, both), bf16),
            pltpu.VMEM((total_rows, both), f32),
            pltpu.VMEM((both, total_rows), f32),
            dma((2, slots)), dma, dma, dma((8,)), dma((8,)),
            dma((6,)), dma((6,)), dma((6,)), dma((18,)), dma((18,)),
            dma((5,)), dma((5,)), dma((18,)), dma((18,)),
            dma((4,)), dma((4,)), dma((6,)), dma((6,)), dma((6,)), dma((6,)), dma((1,)), dma((1,)),
            dma((18,)), dma((18,)), dma((5,)), dma((5,)), dma((2,)), dma((2,)),
        ],
        compiler_params=pltpu.CompilerParams(
            collective_id=0, has_side_effects=True, vmem_limit_bytes=62 << 20
        ),
        cost_estimate=pl.CostEstimate(
            flops=2 * total_rows * 8 * feats * (width + 3 * ff), bytes_accessed=30 << 20,
            transcendentals=1 << 20,
        ),
    )(
        lengths[:, 0, :], dest_group[:, 0], moved_slot[:, 0], queries, kv_cache, up_value,
        jnp.swapaxes(residual_in, 0, 1), norm_gain, jnp.swapaxes(out_proj, 0, 1),
        gate_proj, up_proj, jnp.swapaxes(down_proj, 0, 1),
    )
    attended, layer_out = pl.pallas_call(
        finish_kernel,
        name="finish",
        out_shape=(turned, turned),
        in_specs=[vmem, vmem],
        out_specs=(vmem, vmem),
        scratch_shapes=[pltpu.VMEM((both, total_rows), f32)],
    )(att_x, lay_x)
    return jnp.swapaxes(attended, 0, 1), jnp.swapaxes(layer_out, 0, 1)


def shards(
    queries,
    kv_cache,
    lengths,
    dest_group,
    moved_slot,
    residual_in,
    norm_gain,
    up_value,
    out_proj,
    gate_proj,
    up_proj,
    down_proj,
):
    return run_layer(
        lengths, dest_group, moved_slot, queries, kv_cache, residual_in, norm_gain, up_value,
        out_proj, gate_proj, up_proj, down_proj,
    )


def solution(mesh):
    return jax.shard_map(
        shards,
        mesh=mesh,
        in_specs=(
            P(("dp", "tp"), None, None),
            P(("dp", "tp"), None, None),
            P(None, "tp", None),
            P(None, "tp"),
            P(None, "tp"),
            P("dp", "tp"),
            P("tp"),
            P("dp", None, None),
            P("dp", "tp"),
            P("tp", "dp"),
            P("tp", "dp"),
            P("dp", "tp"),
        ),
        out_specs=(P("dp", "tp"), P("dp", "tp")),
        check_vma=False,
    )
```

```python
import jax
import jax.numpy as jnp
from jax import lax
from jax.experimental import pallas as pl
from jax.experimental.pallas import tpu as pltpu
from jax.sharding import PartitionSpec as P

MESH = pl.DeviceIdType.MESH
KV = 512
GROUPS = 8
exponent_scale = 192.0 ** (-0.5) * 1.4426950408889634


D = 7168
norm_eps = 1e-06
A_COLS = 1152


def layer_kernel(
    length_ref, partner_ref, slot_ref, query_ref, cache_ref, up_ref, resid_ref, gain_ref,
    wo_ref, wg_ref, wu_ref, wd_ref, att_x, lay_x,
    query_buf, cache_buf, up_buf, lat_out, lat_in, wide, vals,
    wo, wg, wu, wd, resid_both, gain_own, gain_both,
    vb, c_out, c_in, cy_out, cy_in, cl_in, xb, part_a, part_b, a1_in, a2, am_in, a_in, bm_in, b_in,
    b2_out, b2_in, b_keep, hb, g_out, g_in, gy_out, gy_in, gl_in, summed, resid_rows, gain_row, turned,
    load_sem, up_sem, own_sem, l_s, l_r,
    w_l, w_s, w_r, v_s, v_r, c_s, c_r, x_s, x_r, a1_s, a1_r, a_s, a_r, b_s, b_r, b2_s, b2_r,
    h_s, h_r, g_s, g_r, o_s, o_r,
):
    g = lax.axis_index("dp")
    t = lax.axis_index("tp")
    c = lax.rem(t, 2)
    q = t // 2
    z = q // 2
    yh = lax.rem(q, 2)
    x = g // 2
    yl = lax.rem(g, 2)
    slots = query_ref.shape[0]
    heads = up_ref.shape[0]
    rows = GROUPS * slots
    feats = wo_ref.shape[0]
    ff = wg_ref.shape[1]
    both = 2 * feats
    b_half = ff - A_COLS
    b_cols = 2 * b_half
    half = rows // 2
    f32 = jnp.float32
    bf16 = jnp.bfloat16

    def other_group(k):
        return (lax.rem(g + k, GROUPS), t)

    def other_z(k):
        return (g, lax.rem(z + k, 4) * 4 + yh * 2 + c)

    def chip(zp):
        return (g, zp * 4 + yh * 2 + c)

    def other_x(k):
        return (lax.rem(x + k, 4) * 2 + yl, t)

    low_peer = (x * 2 + 1 - yl, t)
    y_peer = (g, z * 4 + (1 - yh) * 2 + c)
    sibling = (g, q * 2 + 1 - c)

    def remote(src, dst, send_sem, recv_sem, device):
        return pltpu.make_async_remote_copy(
            src_ref=src, dst_ref=dst, send_sem=send_sem, recv_sem=recv_sem,
            device_id=device, device_id_type=MESH,
        )

    def arrived(ref, sem):
        remote(ref, ref, sem, sem, sibling).wait_recv()

    def left(ref, sem):
        remote(ref, ref, sem, sem, sibling).wait_send()

    def order(i):
        return i + (i // 2) * (5 - 2 * i)

    def loads(r):
        return (
            pltpu.make_async_copy(query_ref.at[r], query_buf.at[r], load_sem.at[0, r]),
            pltpu.make_async_copy(cache_ref.at[r], cache_buf.at[r], load_sem.at[1, r]),
        )

    for r in range(slots):
        for copy in loads(r):
            copy.start()
    up_copy = pltpu.make_async_copy(up_ref, up_buf, up_sem)
    up_copy.start()
    barrier = pltpu.get_barrier_semaphore()
    greeted = [other_group(k) for k in range(1, GROUPS)]
    greeted += [other_z(k) for k in (1, 2, 3)] + [y_peer, sibling]
    for device in greeted:
        pl.semaphore_signal(barrier, inc=1, device_id=device, device_id_type=MESH)

    own_rows = pl.ds(pl.multiple_of(c * feats, feats), feats)
    gain_own[...] = jnp.transpose(
        jnp.broadcast_to(gain_ref[...].astype(f32), (128, feats)), (1, 0)
    ).astype(bf16)
    weights = (
        (wo_ref, wo), (resid_ref, resid_both), (gain_own, gain_both),
        (wg_ref, wg), (wu_ref, wu), (wd_ref, wd),
    )

    def start_weights():
        for i, (src, dst) in enumerate(weights):
            remote(src, dst.at[own_rows], w_s.at[i], w_r.at[i], sibling).start()
            pltpu.make_async_copy(src, dst.at[own_rows], w_l.at[i]).start()

    upper = pl.ds(0, half)
    lower = pl.ds(half, half)

    quarter = half // 2
    first = pl.ds(0, quarter)
    second = pl.ds(quarter, quarter)
    third = pl.ds(half, quarter)
    fourth = pl.ds(half + quarter, quarter)
    over_z = (other_z, y_peer, lambda k: lax.rem(z + 4 - k, 4) * 2 + yh,
              lambda k: lax.rem(z + 4 - k, 4) * 2 + 1 - yh)
    over_x = (other_x, low_peer, lambda k: lax.rem(x + 4 - k, 4) * 2 + yl,
              lambda k: lax.rem(x + 4 - k, 4) * 2 + 1 - yl)

    def push(ref, s, r, i, device):
        remote(ref, ref, s.at[i], r.at[i], device).start()

    def gather_start(buf, s, r, ways):
        ring, peer, near, far = ways
        own = buf.at[near(0)]
        push(own.at[upper], s, r, 0, peer)
        push(own.at[lower], s, r, 1, ring(1))
        push(own.at[lower], s, r, 2, ring(3))
        push(own.at[upper], s, r, 3, ring(1))
        push(own.at[upper], s, r, 4, ring(3))
        push(own.at[lower], s, r, 5, peer)

    def gather_relay(buf, s, r, ways):
        ring, peer, near, far = ways
        block = buf.at[far(0), upper]
        arrived(block, r.at[0])
        push(block, s, r, 6, ring(1))
        push(block, s, r, 7, ring(3))
        arrived(block, r.at[1])
        push(buf.at[near(1), third], s, r, 8, ring(1))
        push(buf.at[near(1), lower], s, r, 9, peer)
        arrived(block, r.at[2])
        push(buf.at[near(3), fourth], s, r, 10, ring(3))
        push(buf.at[near(3), lower], s, r, 11, peer)

    def gather_more(buf, s, r, ways):
        ring, peer, near, far = ways
        block = buf.at[far(0), upper]
        arrived(block, r.at[3])
        push(buf.at[near(1), first], s, r, 12, ring(1))
        arrived(block, r.at[4])
        push(buf.at[near(3), second], s, r, 13, ring(3))

    def gather_step(buf, s, r, ways, i):
        ring, peer, near, far = ways
        block = buf.at[far(0), upper]
        piece = buf.at[far(0), first]

        @pl.when(i == 0)
        def _():
            arrived(block, r.at[5])

        @pl.when(i == 1)
        def _():
            gather_more(buf, s, r, ways)
            arrived(block, r.at[6])
            push(buf.at[far(1), first], s, r, 14, ring(1))
            arrived(block, r.at[7])
            push(buf.at[far(3), second], s, r, 15, ring(3))
            arrived(piece, r.at[8])
            push(buf.at[near(2), third], s, r, 16, peer)
            arrived(piece, r.at[10])
            push(buf.at[near(2), fourth], s, r, 17, peer)
            arrived(block, r.at[9])

        @pl.when(i == 2)
        def _():
            arrived(block, r.at[11])

        @pl.when(i == 3)
        def _():
            for j in range(12, 18):
                arrived(piece, r.at[j])

    def finish_gather(buf, s):
        for i in range(18):
            left(buf.at[0, upper if i in (0, 1, 2, 3, 4, 5, 6, 7, 9, 11) else first], s.at[i])

    last = lax.rem(z + 2, 4)

    def project(buf, w, s, r, out, landed, late_in, out_s, out_r):
        gather_relay(buf, s, r, over_z)

        def step(i, carry):
            zp = lax.rem(z + 4 - order(i), 4)
            gather_step(buf, s, r, over_z, i)
            left_rows = buf[pl.ds(2 * zp, 2)].reshape(2 * rows, buf.shape[2])
            product = lax.dot_general(
                left_rows, w[...], (((1,), (1,)), ((), ())), preferred_element_type=f32
            )
            out[pl.ds(2 * zp, 2)] = product.astype(bf16).reshape(2, rows, both)

            @pl.when((zp != x) & (i < 3))
            def _():
                remote(
                    out.at[pl.ds(2 * zp, 2)], landed.at[x], out_s.at[zp], out_r.at[x],
                    (zp * 2 + yl, t),
                ).start()

            return carry

        lax.fori_loop(0, 4, step, 0)
        there = out.at[2 * last + 1 - yl]
        remote(there, late_in, out_s.at[5], out_r.at[5], low_peer).start()
        arrived(late_in, out_r.at[5])
        here = 2 * last + yl
        out[here] = (out[here].astype(f32) + late_in[...].astype(f32)).astype(bf16)

        @pl.when(last != x)
        def _():
            remote(
                out.at[here], landed.at[x, yl], out_s.at[last], out_r.at[x], (last * 2 + yl, t)
            ).start()

    def gathered_sum(out, landed, y_out, y_in, out_s, out_r):
        def over_x(j):
            total = out[2 * x + j].astype(f32)
            for k in (1, 3, 2):
                total += landed[lax.rem(x + k, 4), j].astype(f32)
            return total

        @pl.when(last != x)
        def _():
            for k in (1, 3, 2):
                p = lax.rem(x + k, 4)
                arrived(landed.at[p], out_r.at[p])
            y_out[...] = over_x(1 - yl).astype(bf16)
            remote(y_out, y_in, out_s.at[4], out_r.at[4], low_peer).start()
            total = over_x(yl)
            arrived(y_in, out_r.at[4])
            summed[...] = total + y_in[...].astype(f32)

        @pl.when(last == x)
        def _():
            for k in (1, 3, 2):
                p = lax.rem(x + k, 4)
                arrived(landed.at[p, yl], out_r.at[p])
            summed[...] = over_x(yl)

        return summed[...]

    def finish_sends(out, y_out, out_s):
        for k in (1, 2, 3):
            p = lax.rem(x + k, 4)

            @pl.when(p != last)
            def _():
                left(out.at[pl.ds(0, 2)], out_s.at[p])

            @pl.when(p == last)
            def _():
                left(out.at[0], out_s.at[p])

        @pl.when(last != x)
        def _():
            left(y_out, out_s.at[4])

        left(out.at[0], out_s.at[5])

    def with_sum(square_sum):
        high = square_sum.astype(bf16).astype(f32)
        lane = lax.broadcasted_iota(jnp.int32, (square_sum.shape[0], 128), 1)
        return jnp.where(
            lane == 0, high, jnp.where(lane == 1, square_sum - high, 0.0)
        ).astype(bf16)

    def send(k, r):
        p = lax.rem(g + k, GROUPS)
        return pltpu.make_async_remote_copy(
            src_ref=lat_out.at[pl.ds(r, 2), pl.ds(pl.multiple_of(p * heads, heads), heads)],
            dst_ref=lat_in.at[g, pl.ds(r, 2)],
            send_sem=l_s.at[k],
            recv_sem=l_r.at[g],
            device_id=(p, t),
            device_id_type=MESH,
        )

    def attend(r):
        for copy in loads(r):
            copy.wait()
        length = length_ref[g, r]
        cache = cache_buf[r]
        scores = lax.dot_general(
            query_buf[r], cache, (((0,), (0,)), ((), ())), preferred_element_type=jnp.float32
        )
        position = lax.broadcasted_iota(jnp.int32, scores.shape, 1)
        masked = jnp.where(position < length, scores, -jnp.inf)
        largest = jnp.max(masked, axis=1, keepdims=True)
        expterm = jnp.exp2((masked - largest) * exponent_scale)
        total = jnp.sum(expterm, axis=1, keepdims=True)
        latent = lax.dot_general(
            expterm.astype(jnp.bfloat16), cache[:KV], (((1,), (1,)), ((), ())),
            preferred_element_type=jnp.float32,
        )
        lat_out[r] = (latent * (1.0 / total)).astype(jnp.bfloat16)

    def pair(i, carry):
        attend(2 * i)
        attend(2 * i + 1)
        for k in (4, 3, 5, 2, 6, 1, 7):
            send(k, 2 * i).start()
        return carry

    attend(0)
    attend(1)
    pl.semaphore_wait(barrier, len(greeted))
    for k in (4, 3, 5, 2, 6, 1, 7):
        send(k, 0).start()
    lax.fori_loop(1, slots // 2, pair, 0)
    start_weights()
    own = pltpu.make_async_copy(
        lat_out.at[:, pl.ds(pl.multiple_of(g * heads, heads), heads)], lat_in.at[g], own_sem
    )
    own.start()
    own.wait()
    up_copy.wait()

    def widen(k, carry):
        s = lax.rem(g + k, GROUPS)

        @pl.when(k > 0)
        def _():
            pltpu.make_async_remote_copy(
                src_ref=lat_in.at[s], dst_ref=lat_in.at[s], send_sem=l_s.at[0],
                recv_sem=l_r.at[s], device_id=(s, t), device_id_type=MESH,
            ).wait_recv()

        step_rows = slots * heads
        block = lat_in[s].astype(jnp.float32).reshape(step_rows, KV)
        for lane in range(KV // 128):
            wide[lane, pl.ds(pl.multiple_of(s * step_rows, step_rows), step_rows)] = block[
                :, lane * 128 : (lane + 1) * 128
            ]
        return carry

    lax.fori_loop(0, GROUPS, widen, 0)
    count = GROUPS * slots
    for h in range(heads):
        head_rows = jnp.concatenate(
            [wide[lane, pl.ds(h, count, stride=heads), :] for lane in range(KV // 128)], axis=1
        )
        vals[:, h * 128 : (h + 1) * 128] = jnp.dot(
            head_rows.astype(jnp.bfloat16),
            up_buf[h],
            preferred_element_type=jnp.float32,
        ).astype(jnp.bfloat16)
    row = lax.broadcasted_iota(jnp.int32, (count, count), 0)
    column = lax.broadcasted_iota(jnp.int32, (count, count), 1)
    source = row
    for group in range(GROUPS):
        partner = partner_ref[group]
        own_row = group * slots + slot_ref[group]
        source = jnp.where(row == own_row, partner * slots + slot_ref[partner], source)
    place = jnp.where(column == source, 1.0, 0.0).astype(jnp.bfloat16)
    vb[q] = jnp.dot(place, vals[...], preferred_element_type=jnp.float32).astype(
        jnp.bfloat16
    )
    gather_start(vb, v_s, v_r, over_z)

    def weight_ready(i):
        src, dst = weights[i]
        pltpu.make_async_copy(src, dst.at[own_rows], w_l.at[i]).wait()
        arrived(dst.at[own_rows], w_r.at[i])

    for i in range(3):
        weight_ready(i)
    mine = pl.ds(pl.multiple_of(c * rows, rows), rows)
    turned[...] = resid_both[...].astype(f32)
    resid_rows[...] = jnp.transpose(turned[...], (1, 0))
    gain_row[...] = jnp.transpose(gain_both[...].astype(f32), (1, 0))[:1]
    project(vb, wo, v_s, v_r, c_out, c_in, cl_in, c_s, c_r)
    attn = gathered_sum(c_out, c_in, cy_out, cy_in, c_s, c_r)
    att_x[c] = attn.astype(bf16)
    remote(att_x.at[c], att_x.at[c], o_s.at[0], o_r.at[0], sibling).start()
    resid = resid_rows[mine] + attn
    resid_rows[mine] = resid
    xb[g, :, :both] = (resid * gain_row[...]).astype(bf16)
    xb[g, :, both:] = with_sum(jnp.sum(resid * resid, axis=1, keepdims=True))
    gather_start(xb, x_s, x_r, over_x)
    for i in range(3, 6):
        weight_ready(i)

    gather_relay(xb, x_s, x_r, over_x)

    def first_products(i, carry):
        xp = lax.rem(x + 4 - order(i), 4)
        gather_step(xb, x_s, x_r, over_x, i)
        block = xb[pl.ds(2 * xp, 2)].reshape(2 * rows, both + 128)
        pair = pl.ds(2 * xp, 2)
        lhs = block[:, :both]

        def product(w, start, width):
            return jnp.dot(
                lhs, w[:, start : start + width], preferred_element_type=f32
            ).astype(bf16).reshape(2, rows, width)

        part_a[pair, :, :A_COLS] = product(wg, 0, A_COLS)
        part_a[pair, :, A_COLS:] = product(wu, 0, A_COLS)
        remote(
            part_a.at[2 * xp + 1 - yh], a1_in.at[xp], a1_s.at[xp], a1_r.at[xp], y_peer
        ).start()
        part_b[pair, :, :b_half] = product(wg, A_COLS, b_half)
        part_b[pair, :, b_half:b_cols] = product(wu, A_COLS, b_half)
        part_b[pair, :, b_cols:] = block[:, both:].reshape(2, rows, 128)
        role = lax.rem(xp + 4 - z, 4)

        @pl.when(role == 2)
        def _():
            for j in range(2):
                remote(
                    part_b.at[2 * xp + j], bm_in.at[j], b_s.at[j], b_r.at[j], other_z(1 + 2 * j)
                ).start()

        for j in range(2):

            @pl.when(role == 3 - 2 * j)
            def _():
                remote(
                    part_b.at[2 * xp + j], b_in.at[1 - j, j], b_s.at[2 + j], b_r.at[2 + j],
                    other_z(3 - 2 * j),
                ).start()

        return carry

    lax.fori_loop(0, 4, first_products, 0)
    halves = (upper, lower)

    def second_a(i, carry):
        xp = lax.rem(x + 4 - order(i), 4)
        arrived(a1_in.at[xp], a1_r.at[xp])
        a2[xp] = (part_a[2 * xp + yh].astype(f32) + a1_in[xp].astype(f32)).astype(bf16)
        role = lax.rem(xp + 4 - z, 4)

        @pl.when(role == 2)
        def _():
            for j in range(2):
                remote(
                    a2.at[xp, halves[j]], am_in.at[j], a_s.at[j], a_r.at[j], other_z(1 + 2 * j)
                ).start()

        for j in range(2):

            @pl.when(role == 3 - 2 * j)
            def _():
                remote(
                    a2.at[xp, halves[j]], a_in.at[1 - j, halves[j]], a_s.at[2 + j],
                    a_r.at[2 + j], other_z(3 - 2 * j),
                ).start()

        return carry

    def total_squares(block):
        return block[:, 0:1] + block[:, 1:2]

    def relay_b(j):
        block = 2 * lax.rem(z + 1 + 2 * j, 4) + j
        arrived(bm_in.at[j], b_r.at[j])
        total = part_b[block].astype(f32) + bm_in[j].astype(f32)
        part_b[block, :, :b_cols] = total[:, :b_cols].astype(bf16)
        part_b[block, :, b_cols:] = with_sum(total_squares(total[:, b_cols:]))
        remote(
            part_b.at[block], b_in.at[j, j], b_s.at[4 + j], b_r.at[4 + j], other_z(1 + 2 * j)
        ).start()

    def relay_a(j):
        block = lax.rem(z + 1 + 2 * j, 4)
        arrived(am_in.at[j], a_r.at[j])
        a2[block, halves[j]] = (
            a2[block, halves[j]].astype(f32) + am_in[j].astype(f32)
        ).astype(bf16)
        remote(
            a2.at[block, halves[j]], a_in.at[j, halves[j]], a_s.at[4 + j], a_r.at[4 + j],
            other_z(1 + 2 * j),
        ).start()

    lax.fori_loop(0, 1, second_a, 0)
    for j in range(2):
        relay_b(j)
    lax.fori_loop(1, 3, second_a, 0)
    for j in range(2):
        arrived(b_in.at[1 - j, j], b_r.at[2 + j])
        arrived(b_in.at[j, j], b_r.at[4 + j])

    def sum_b(j):
        return part_b[2 * z + j].astype(f32) + b_in[0, j].astype(f32) + b_in[1, j].astype(f32)

    away = sum_b(1 - yh)
    b2_out[:, :b_cols] = away[:, :b_cols].astype(bf16)
    b2_out[:, b_cols:] = with_sum(total_squares(away[:, b_cols:]))
    remote(b2_out, b2_in, b2_s.at[0], b2_r.at[0], y_peer).start()
    b_keep[...] = sum_b(yh)
    lax.fori_loop(3, 4, second_a, 0)
    for j in range(2):
        relay_a(j)
    arrived(b2_in, b2_r.at[0])

    def sum_b2(start, width):
        cols = slice(start, start + width)
        return b_keep[:, cols] + b2_in[:, cols].astype(f32)

    scale = lax.rsqrt(total_squares(sum_b2(b_cols, 128)) / D + norm_eps)

    def write_hidden(start, gate, upward):
        gate = gate * scale
        hb[q, :, start : start + gate.shape[1]] = (
            gate / (1.0 + jnp.exp(-gate)) * (upward * scale)
        ).astype(bf16)

    write_hidden(A_COLS, sum_b2(0, b_half), sum_b2(b_half, b_half))
    for j in range(2):
        arrived(a_in.at[1 - j, halves[j]], a_r.at[2 + j])
        arrived(a_in.at[j, halves[j]], a_r.at[4 + j])

    def sum_a(start):
        cols = slice(start, start + A_COLS)
        return (
            a2[z, :, cols].astype(f32) + a_in[0, :, cols].astype(f32)
            + a_in[1, :, cols].astype(f32)
        )

    write_hidden(0, sum_a(0), sum_a(A_COLS))
    gather_start(hb, h_s, h_r, over_z)
    project(hb, wd, h_s, h_r, g_out, g_in, gl_in, g_s, g_r)
    down = gathered_sum(g_out, g_in, gy_out, gy_in, g_s, g_r)
    lay_x[c] = (resid_rows[mine] + down).astype(bf16)
    remote(lay_x.at[c], lay_x.at[c], o_s.at[1], o_r.at[1], sibling).start()
    arrived(att_x.at[1 - c], o_r.at[0])
    arrived(lay_x.at[1 - c], o_r.at[1])

    for k in range(1, GROUPS):
        left(lat_in.at[0], l_s.at[k])
    for i, (src, dst) in enumerate(weights):
        left(src, w_s.at[i])
    finish_gather(vb, v_s)
    finish_gather(hb, h_s)
    finish_sends(c_out, cy_out, c_s)
    finish_sends(g_out, gy_out, g_s)
    finish_gather(xb, x_s)
    for i in range(4):
        left(part_a.at[0], a1_s.at[i])
    for i in range(6):
        left(part_b.at[0], b_s.at[i])
        left(a2.at[0, upper], a_s.at[i])
    left(b2_out, b2_s.at[0])
    left(att_x.at[0], o_s.at[0])
    left(lay_x.at[0], o_s.at[1])


def finish_kernel(att_ref, lay_ref, attended_ref, out_ref, turned):
    feats = attended_ref.shape[0]
    c = lax.rem(lax.axis_index("tp"), 2)
    own = pl.ds(pl.multiple_of(c * feats, feats), feats)
    for exchange, target in ((att_ref, attended_ref), (lay_ref, out_ref)):
        stacked = exchange[...].reshape(-1, 2 * feats).astype(jnp.float32)
        turned[...] = jnp.transpose(stacked, (1, 0))
        target[...] = turned[own].astype(target.dtype)


def run_layer(
    lengths, dest_group, moved_slot, queries, kv_cache, residual_in, norm_gain, up_value, out_proj,
    gate_proj, up_proj, down_proj,
):
    slots, all_heads, _ = queries.shape
    heads = up_value.shape[0]
    rows, width = GROUPS * slots, heads * 128
    queries = jnp.swapaxes(queries, 1, 2)
    kv_cache = jnp.swapaxes(kv_cache, 1, 2)
    total_rows, feats = residual_in.shape
    ff = gate_proj.shape[1]
    both = 2 * feats
    a_cols, b_cols = 2 * A_COLS, 2 * (ff - A_COLS) + 128
    f32, bf16 = jnp.float32, jnp.bfloat16
    vmem = pl.BlockSpec(memory_space=pltpu.VMEM)
    smem = pl.BlockSpec(memory_space=pltpu.SMEM)
    hbm = pl.BlockSpec(memory_space=pl.ANY)
    dma = pltpu.SemaphoreType.DMA
    block = jax.ShapeDtypeStruct((2, rows, both), bf16)
    turned = jax.ShapeDtypeStruct((feats, total_rows), bf16)
    att_x, lay_x = pl.pallas_call(
        layer_kernel,
        name="layer",
        out_shape=(block, block),
        in_specs=[smem, smem, smem, hbm, hbm, hbm, hbm, vmem, hbm, hbm, hbm, hbm],
        out_specs=(vmem, vmem),
        scratch_shapes=[
            pltpu.VMEM(queries.shape, bf16),
            pltpu.VMEM(kv_cache.shape, bf16),
            pltpu.VMEM(up_value.shape, bf16),
            pltpu.VMEM((slots, all_heads, KV), bf16),
            pltpu.VMEM((GROUPS, slots, heads, KV), bf16),
            pltpu.VMEM((KV // 128, rows * heads, 128), f32),
            pltpu.VMEM((rows, width), bf16),
            pltpu.VMEM((both, width), bf16),
            pltpu.VMEM((both, ff), bf16),
            pltpu.VMEM((both, ff), bf16),
            pltpu.VMEM((both, ff), bf16),
            pltpu.VMEM((both, total_rows), bf16),
            pltpu.VMEM((feats, 128), bf16),
            pltpu.VMEM((both, 128), bf16),
            pltpu.VMEM((8, rows, width), bf16),
            pltpu.VMEM((8, rows, both), bf16),
            pltpu.VMEM((4, 2, rows, both), bf16),
            pltpu.VMEM((rows, both), bf16),
            pltpu.VMEM((rows, both), bf16),
            pltpu.VMEM((rows, both), bf16),
            pltpu.VMEM((8, rows, both + 128), bf16),
            pltpu.VMEM((8, rows, a_cols), bf16),
            pltpu.VMEM((8, rows, b_cols), bf16),
            pltpu.VMEM((4, rows, a_cols), bf16),
            pltpu.VMEM((4, rows, a_cols), bf16),
            pltpu.VMEM((2, rows // 2, a_cols), bf16),
            pltpu.VMEM((2, rows, a_cols), bf16),
            pltpu.VMEM((2, rows, b_cols), bf16),
            pltpu.VMEM((2, 2, rows, b_cols), bf16),
            pltpu.VMEM((rows, b_cols), bf16),
            pltpu.VMEM((rows, b_cols), bf16),
            pltpu.VMEM((rows, b_cols), f32),
            pltpu.VMEM((8, rows, ff), bf16),
            pltpu.VMEM((8, rows, both), bf16),
            pltpu.VMEM((4, 2, rows, both), bf16),
            pltpu.VMEM((rows, both), bf16),
            pltpu.VMEM((rows, both), bf16),
            pltpu.VMEM((rows, both), bf16),
            pltpu.VMEM((rows, both), f32),
            pltpu.VMEM((total_rows, both), f32),
            pltpu.VMEM((1, both), f32),
            pltpu.VMEM((both, total_rows), f32),
            dma((2, slots)), dma, dma, dma((8,)), dma((8,)),
            dma((6,)), dma((6,)), dma((6,)), dma((18,)), dma((18,)),
            dma((6,)), dma((6,)), dma((18,)), dma((18,)),
            dma((4,)), dma((4,)), dma((6,)), dma((6,)), dma((6,)), dma((6,)), dma((1,)), dma((1,)),
            dma((18,)), dma((18,)), dma((6,)), dma((6,)), dma((2,)), dma((2,)),
        ],
        compiler_params=pltpu.CompilerParams(
            collective_id=0, has_side_effects=True, vmem_limit_bytes=62 << 20
        ),
        cost_estimate=pl.CostEstimate(
            flops=2 * total_rows * 8 * feats * (width + 3 * ff), bytes_accessed=30 << 20,
            transcendentals=1 << 20,
        ),
    )(
        lengths[:, 0, :], dest_group[:, 0], moved_slot[:, 0], queries, kv_cache, up_value,
        jnp.swapaxes(residual_in, 0, 1), norm_gain, jnp.swapaxes(out_proj, 0, 1),
        gate_proj, up_proj, jnp.swapaxes(down_proj, 0, 1),
    )
    attended, layer_out = pl.pallas_call(
        finish_kernel,
        name="finish",
        out_shape=(turned, turned),
        in_specs=[vmem, vmem],
        out_specs=(vmem, vmem),
        scratch_shapes=[pltpu.VMEM((both, total_rows), f32)],
    )(att_x, lay_x)
    return jnp.swapaxes(attended, 0, 1), jnp.swapaxes(layer_out, 0, 1)


def shards(
    queries,
    kv_cache,
    lengths,
    dest_group,
    moved_slot,
    residual_in,
    norm_gain,
    up_value,
    out_proj,
    gate_proj,
    up_proj,
    down_proj,
):
    return run_layer(
        lengths, dest_group, moved_slot, queries, kv_cache, residual_in, norm_gain, up_value,
        out_proj, gate_proj, up_proj, down_proj,
    )


def solution(mesh):
    return jax.shard_map(
        shards,
        mesh=mesh,
        in_specs=(
            P(("dp", "tp"), None, None),
            P(("dp", "tp"), None, None),
            P(None, "tp", None),
            P(None, "tp"),
            P(None, "tp"),
            P("dp", "tp"),
            P("tp"),
            P("dp", None, None),
            P("dp", "tp"),
            P("tp", "dp"),
            P("tp", "dp"),
            P("dp", "tp"),
        ),
        out_specs=(P("dp", "tp"), P("dp", "tp")),
        check_vma=False,
    )
```

```python
import jax
import jax.numpy as jnp
from jax import lax
from jax.experimental import pallas as pl
from jax.experimental.pallas import tpu as pltpu
from jax.sharding import PartitionSpec as P

MESH = pl.DeviceIdType.MESH
KV = 512
GROUPS = 8
exponent_scale = 192.0 ** (-0.5) * 1.4426950408889634


D = 7168
norm_eps = 1e-06
A_COLS = 1152


def layer_kernel(
    length_ref, partner_ref, slot_ref, query_ref, cache_ref, up_ref, resid_ref, gain_ref,
    wo_ref, wg_ref, wu_ref, wd_ref, att_x, lay_x,
    query_buf, cache_buf, up_buf, lat_out, lat_in, wide, vals,
    wo, wg, wu, wd, resid_both, gain_own, gain_both,
    vb, c_out, c_in, cy_out, cy_in, cl_in, xb, part_a, part_b, a1_in, a2, am_in, a_in, bm_in, b_in,
    b2_out, b2_in, b_keep, hb, g_out, g_in, gy_out, gy_in, gl_in, summed, resid_rows, gain_row, turned,
    load_sem, up_sem, own_sem, l_s, l_r,
    w_l, w_s, w_r, v_s, v_r, c_s, c_r, x_s, x_r, a1_s, a1_r, a_s, a_r, b_s, b_r, b2_s, b2_r,
    h_s, h_r, g_s, g_r, o_s, o_r,
):
    g = lax.axis_index("dp")
    t = lax.axis_index("tp")
    c = lax.rem(t, 2)
    q = t // 2
    z = q // 2
    yh = lax.rem(q, 2)
    x = g // 2
    yl = lax.rem(g, 2)
    slots = query_ref.shape[0]
    heads = up_ref.shape[0]
    rows = GROUPS * slots
    feats = wo_ref.shape[0]
    ff = wg_ref.shape[1]
    both = 2 * feats
    b_half = ff - A_COLS
    b_cols = 2 * b_half
    half = rows // 2
    f32 = jnp.float32
    bf16 = jnp.bfloat16

    def other_group(k):
        return (lax.rem(g + k, GROUPS), t)

    def other_z(k):
        return (g, lax.rem(z + k, 4) * 4 + yh * 2 + c)

    def chip(zp):
        return (g, zp * 4 + yh * 2 + c)

    def other_x(k):
        return (lax.rem(x + k, 4) * 2 + yl, t)

    low_peer = (x * 2 + 1 - yl, t)
    y_peer = (g, z * 4 + (1 - yh) * 2 + c)
    sibling = (g, q * 2 + 1 - c)

    def remote(src, dst, send_sem, recv_sem, device):
        return pltpu.make_async_remote_copy(
            src_ref=src, dst_ref=dst, send_sem=send_sem, recv_sem=recv_sem,
            device_id=device, device_id_type=MESH,
        )

    def arrived(ref, sem):
        remote(ref, ref, sem, sem, sibling).wait_recv()

    def left(ref, sem):
        remote(ref, ref, sem, sem, sibling).wait_send()

    def order(i):
        return i + (i // 2) * (5 - 2 * i)

    def loads(r):
        return (
            pltpu.make_async_copy(query_ref.at[r], query_buf.at[r], load_sem.at[0, r]),
            pltpu.make_async_copy(cache_ref.at[r], cache_buf.at[r], load_sem.at[1, r]),
        )

    for r in range(slots):
        for copy in loads(r):
            copy.start()
    up_copy = pltpu.make_async_copy(up_ref, up_buf, up_sem)
    up_copy.start()
    barrier = pltpu.get_barrier_semaphore()
    greeted = [other_group(k) for k in range(1, GROUPS)]
    greeted += [other_z(k) for k in (1, 2, 3)] + [y_peer, sibling]
    for device in greeted:
        pl.semaphore_signal(barrier, inc=1, device_id=device, device_id_type=MESH)

    own_rows = pl.ds(pl.multiple_of(c * feats, feats), feats)
    gain_own[...] = jnp.transpose(
        jnp.broadcast_to(gain_ref[...].astype(f32), (128, feats)), (1, 0)
    ).astype(bf16)
    weights = (
        (wo_ref, wo), (resid_ref, resid_both), (gain_own, gain_both),
        (wg_ref, wg), (wu_ref, wu), (wd_ref, wd),
    )

    def start_weights():
        for i, (src, dst) in enumerate(weights):
            remote(src, dst.at[own_rows], w_s.at[i], w_r.at[i], sibling).start()
            pltpu.make_async_copy(src, dst.at[own_rows], w_l.at[i]).start()

    upper = pl.ds(0, half)
    lower = pl.ds(half, half)

    quarter = half // 2
    first = pl.ds(0, quarter)
    second = pl.ds(quarter, quarter)
    third = pl.ds(half, quarter)
    fourth = pl.ds(half + quarter, quarter)
    over_z = (other_z, y_peer, lambda k: lax.rem(z + 4 - k, 4) * 2 + yh,
              lambda k: lax.rem(z + 4 - k, 4) * 2 + 1 - yh)
    over_x = (other_x, low_peer, lambda k: lax.rem(x + 4 - k, 4) * 2 + yl,
              lambda k: lax.rem(x + 4 - k, 4) * 2 + 1 - yl)

    def push(ref, s, r, i, device):
        remote(ref, ref, s.at[i], r.at[i], device).start()

    def gather_start(buf, s, r, ways):
        ring, peer, near, far = ways
        own = buf.at[near(0)]
        push(own.at[upper], s, r, 0, peer)
        push(own.at[lower], s, r, 1, ring(1))
        push(own.at[lower], s, r, 2, ring(3))
        push(own.at[upper], s, r, 3, ring(1))
        push(own.at[upper], s, r, 4, ring(3))
        push(own.at[lower], s, r, 5, peer)

    def gather_relay(buf, s, r, ways):
        ring, peer, near, far = ways
        block = buf.at[far(0), upper]
        arrived(block, r.at[0])
        push(block, s, r, 6, ring(1))
        push(block, s, r, 7, ring(3))
        arrived(block, r.at[1])
        push(buf.at[near(1), third], s, r, 8, ring(1))
        push(buf.at[near(1), lower], s, r, 9, peer)
        arrived(block, r.at[2])
        push(buf.at[near(3), fourth], s, r, 10, ring(3))
        push(buf.at[near(3), lower], s, r, 11, peer)

    def gather_more(buf, s, r, ways):
        ring, peer, near, far = ways
        block = buf.at[far(0), upper]
        arrived(block, r.at[3])
        push(buf.at[near(1), first], s, r, 12, ring(1))
        arrived(block, r.at[4])
        push(buf.at[near(3), second], s, r, 13, ring(3))

    def gather_far(buf, s, r, ways, i):
        ring, peer, near, far = ways
        block = buf.at[far(0), upper]
        piece = buf.at[far(0), first]

        @pl.when(i == 1)
        def _():
            gather_more(buf, s, r, ways)
            arrived(block, r.at[6])
            push(buf.at[far(1), first], s, r, 14, ring(1))
            arrived(block, r.at[7])
            push(buf.at[far(3), second], s, r, 15, ring(3))
            arrived(piece, r.at[8])
            push(buf.at[near(2), third], s, r, 16, peer)
            arrived(piece, r.at[10])
            push(buf.at[near(2), fourth], s, r, 17, peer)

    def gather_ready(buf, r, ways, i):
        far = ways[3]
        block = buf.at[far(0), upper]
        piece = buf.at[far(0), first]

        @pl.when(i == 0)
        def _():
            arrived(block, r.at[5])

        @pl.when(i == 1)
        def _():
            arrived(block, r.at[9])

        @pl.when(i == 2)
        def _():
            arrived(block, r.at[11])

        @pl.when(i == 3)
        def _():
            for j in range(12, 18):
                arrived(piece, r.at[j])

    def finish_gather(buf, s):
        for i in range(18):
            left(buf.at[0, upper if i in (0, 1, 2, 3, 4, 5, 6, 7, 9, 11) else first], s.at[i])

    last = lax.rem(z + 2, 4)

    def project(buf, parts, columns, w, s, r, out, landed, late_in, out_s, out_r):
        for p, part in enumerate(parts):
            gather_relay(part, s.at[p], r.at[p], over_z)

        def step(i, carry):
            zp = lax.rem(z + 4 - order(i), 4)
            for p, part in enumerate(parts):
                gather_far(part, s.at[p], r.at[p], over_z, i)
            product = 0.0
            for p, part in enumerate(parts):
                gather_ready(part, r.at[p], over_z, i)
                start, width = columns[p]
                left_rows = buf[pl.ds(2 * zp, 2), :, start : start + width]
                product += lax.dot_general(
                    left_rows.reshape(2 * rows, width), w[:, start : start + width],
                    (((1,), (1,)), ((), ())), preferred_element_type=f32,
                )
            out[pl.ds(2 * zp, 2)] = product.astype(bf16).reshape(2, rows, both)

            @pl.when((zp != x) & (i < 3))
            def _():
                remote(
                    out.at[pl.ds(2 * zp, 2)], landed.at[x], out_s.at[zp], out_r.at[x],
                    (zp * 2 + yl, t),
                ).start()

            return carry

        lax.fori_loop(0, 4, step, 0)
        there = out.at[2 * last + 1 - yl]
        remote(there, late_in, out_s.at[5], out_r.at[5], low_peer).start()
        arrived(late_in, out_r.at[5])
        here = 2 * last + yl
        out[here] = (out[here].astype(f32) + late_in[...].astype(f32)).astype(bf16)

        @pl.when(last != x)
        def _():
            remote(
                out.at[here], landed.at[x, yl], out_s.at[last], out_r.at[x], (last * 2 + yl, t)
            ).start()

    def gathered_sum(out, landed, y_out, y_in, out_s, out_r):
        def over_x(j):
            total = out[2 * x + j].astype(f32)
            for k in (1, 3, 2):
                total += landed[lax.rem(x + k, 4), j].astype(f32)
            return total

        @pl.when(last != x)
        def _():
            for k in (1, 3, 2):
                p = lax.rem(x + k, 4)
                arrived(landed.at[p], out_r.at[p])
            y_out[...] = over_x(1 - yl).astype(bf16)
            remote(y_out, y_in, out_s.at[4], out_r.at[4], low_peer).start()
            total = over_x(yl)
            arrived(y_in, out_r.at[4])
            summed[...] = total + y_in[...].astype(f32)

        @pl.when(last == x)
        def _():
            for k in (1, 3, 2):
                p = lax.rem(x + k, 4)
                arrived(landed.at[p, yl], out_r.at[p])
            summed[...] = over_x(yl)

        return summed[...]

    def finish_sends(out, y_out, out_s):
        for k in (1, 2, 3):
            p = lax.rem(x + k, 4)

            @pl.when(p != last)
            def _():
                left(out.at[pl.ds(0, 2)], out_s.at[p])

            @pl.when(p == last)
            def _():
                left(out.at[0], out_s.at[p])

        @pl.when(last != x)
        def _():
            left(y_out, out_s.at[4])

        left(out.at[0], out_s.at[5])

    def with_sum(square_sum):
        high = square_sum.astype(bf16).astype(f32)
        lane = lax.broadcasted_iota(jnp.int32, (square_sum.shape[0], 128), 1)
        return jnp.where(
            lane == 0, high, jnp.where(lane == 1, square_sum - high, 0.0)
        ).astype(bf16)

    def send(k, r):
        p = lax.rem(g + k, GROUPS)
        return pltpu.make_async_remote_copy(
            src_ref=lat_out.at[pl.ds(r, 2), pl.ds(pl.multiple_of(p * heads, heads), heads)],
            dst_ref=lat_in.at[g, pl.ds(r, 2)],
            send_sem=l_s.at[k],
            recv_sem=l_r.at[g],
            device_id=(p, t),
            device_id_type=MESH,
        )

    def attend(r):
        for copy in loads(r):
            copy.wait()
        length = length_ref[g, r]
        cache = cache_buf[r]
        scores = lax.dot_general(
            query_buf[r], cache, (((0,), (0,)), ((), ())), preferred_element_type=jnp.float32
        )
        position = lax.broadcasted_iota(jnp.int32, scores.shape, 1)
        masked = jnp.where(position < length, scores, -jnp.inf)
        largest = jnp.max(masked, axis=1, keepdims=True)
        expterm = jnp.exp2((masked - largest) * exponent_scale)
        total = jnp.sum(expterm, axis=1, keepdims=True)
        latent = lax.dot_general(
            expterm.astype(jnp.bfloat16), cache[:KV], (((1,), (1,)), ((), ())),
            preferred_element_type=jnp.float32,
        )
        lat_out[r] = (latent * (1.0 / total)).astype(jnp.bfloat16)

    def pair(i, carry):
        attend(2 * i)
        attend(2 * i + 1)
        for k in (4, 3, 5, 2, 6, 1, 7):
            send(k, 2 * i).start()
        return carry

    attend(0)
    attend(1)
    pl.semaphore_wait(barrier, len(greeted))
    for k in (4, 3, 5, 2, 6, 1, 7):
        send(k, 0).start()
    lax.fori_loop(1, slots // 2, pair, 0)
    start_weights()
    own = pltpu.make_async_copy(
        lat_out.at[:, pl.ds(pl.multiple_of(g * heads, heads), heads)], lat_in.at[g], own_sem
    )
    own.start()
    own.wait()
    up_copy.wait()

    def widen(k, carry):
        s = lax.rem(g + k, GROUPS)

        @pl.when(k > 0)
        def _():
            pltpu.make_async_remote_copy(
                src_ref=lat_in.at[s], dst_ref=lat_in.at[s], send_sem=l_s.at[0],
                recv_sem=l_r.at[s], device_id=(s, t), device_id_type=MESH,
            ).wait_recv()

        step_rows = slots * heads
        block = lat_in[s].astype(jnp.float32).reshape(step_rows, KV)
        for lane in range(KV // 128):
            wide[lane, pl.ds(pl.multiple_of(s * step_rows, step_rows), step_rows)] = block[
                :, lane * 128 : (lane + 1) * 128
            ]
        return carry

    lax.fori_loop(0, GROUPS, widen, 0)
    count = GROUPS * slots
    row = lax.broadcasted_iota(jnp.int32, (count, count), 0)
    column = lax.broadcasted_iota(jnp.int32, (count, count), 1)
    source = row
    for group in range(GROUPS):
        partner = partner_ref[group]
        own_row = group * slots + slot_ref[group]
        source = jnp.where(row == own_row, partner * slots + slot_ref[partner], source)
    place = jnp.where(column == source, 1.0, 0.0).astype(jnp.bfloat16)
    half_cols = heads * 64
    v_parts = [vb.at[:, :, pl.ds(p * half_cols, half_cols)] for p in range(2)]
    for p in range(2):
        cols = slice(p * half_cols, (p + 1) * half_cols)
        for h in range(p * heads // 2, (p + 1) * heads // 2):
            head_rows = jnp.concatenate(
                [wide[lane, pl.ds(h, count, stride=heads), :] for lane in range(KV // 128)], axis=1
            )
            vals[:, h * 128 : (h + 1) * 128] = jnp.dot(
                head_rows.astype(jnp.bfloat16),
                up_buf[h],
                preferred_element_type=jnp.float32,
            ).astype(jnp.bfloat16)
        vb[q, :, cols] = jnp.dot(
            place, vals[:, cols], preferred_element_type=jnp.float32
        ).astype(jnp.bfloat16)
        gather_start(v_parts[p], v_s.at[p], v_r.at[p], over_z)

    def weight_ready(i):
        src, dst = weights[i]
        pltpu.make_async_copy(src, dst.at[own_rows], w_l.at[i]).wait()
        arrived(dst.at[own_rows], w_r.at[i])

    for i in range(3):
        weight_ready(i)
    mine = pl.ds(pl.multiple_of(c * rows, rows), rows)
    turned[...] = resid_both[...].astype(f32)
    resid_rows[...] = jnp.transpose(turned[...], (1, 0))
    gain_row[...] = jnp.transpose(gain_both[...].astype(f32), (1, 0))[:1]
    project(vb, v_parts, ((0, half_cols), (half_cols, half_cols)), wo, v_s, v_r, c_out, c_in, cl_in, c_s, c_r)
    attn = gathered_sum(c_out, c_in, cy_out, cy_in, c_s, c_r)
    resid = resid_rows[mine] + attn
    resid_rows[mine] = resid
    xb[g, :, :both] = (resid * gain_row[...]).astype(bf16)
    xb[g, :, both:] = with_sum(jnp.sum(resid * resid, axis=1, keepdims=True))
    gather_start(xb, x_s, x_r, over_x)
    att_x[c] = attn.astype(bf16)
    remote(att_x.at[c], att_x.at[c], o_s.at[0], o_r.at[0], sibling).start()
    for i in range(3, 6):
        weight_ready(i)

    gather_relay(xb, x_s, x_r, over_x)

    def first_products(i, carry):
        xp = lax.rem(x + 4 - order(i), 4)
        gather_far(xb, x_s, x_r, over_x, i)
        gather_ready(xb, x_r, over_x, i)
        block = xb[pl.ds(2 * xp, 2)].reshape(2 * rows, both + 128)
        pair = pl.ds(2 * xp, 2)
        lhs = block[:, :both]

        def product(w, start, width):
            return jnp.dot(
                lhs, w[:, start : start + width], preferred_element_type=f32
            ).astype(bf16).reshape(2, rows, width)

        part_a[pair, :, :A_COLS] = product(wg, 0, A_COLS)
        part_a[pair, :, A_COLS:] = product(wu, 0, A_COLS)
        remote(
            part_a.at[2 * xp + 1 - yh], a1_in.at[xp], a1_s.at[xp], a1_r.at[xp], y_peer
        ).start()
        part_b[pair, :, :b_half] = product(wg, A_COLS, b_half)
        part_b[pair, :, b_half:b_cols] = product(wu, A_COLS, b_half)
        part_b[pair, :, b_cols:] = block[:, both:].reshape(2, rows, 128)
        role = lax.rem(xp + 4 - z, 4)

        @pl.when(role == 2)
        def _():
            for j in range(2):
                remote(
                    part_b.at[2 * xp + j], bm_in.at[j], b_s.at[j], b_r.at[j], other_z(1 + 2 * j)
                ).start()

        for j in range(2):

            @pl.when(role == 3 - 2 * j)
            def _():
                remote(
                    part_b.at[2 * xp + j], b_in.at[1 - j, j], b_s.at[2 + j], b_r.at[2 + j],
                    other_z(3 - 2 * j),
                ).start()

        return carry

    lax.fori_loop(0, 4, first_products, 0)
    halves = (upper, lower)

    def second_a(i, carry):
        xp = lax.rem(x + 4 - order(i), 4)
        arrived(a1_in.at[xp], a1_r.at[xp])
        a2[xp] = (part_a[2 * xp + yh].astype(f32) + a1_in[xp].astype(f32)).astype(bf16)
        role = lax.rem(xp + 4 - z, 4)

        @pl.when(role == 2)
        def _():
            for j in range(2):
                remote(
                    a2.at[xp, halves[j]], am_in.at[j], a_s.at[j], a_r.at[j], other_z(1 + 2 * j)
                ).start()

        for j in range(2):

            @pl.when(role == 3 - 2 * j)
            def _():
                remote(
                    a2.at[xp, halves[j]], a_in.at[1 - j, halves[j]], a_s.at[2 + j],
                    a_r.at[2 + j], other_z(3 - 2 * j),
                ).start()

        return carry

    def total_squares(block):
        return block[:, 0:1] + block[:, 1:2]

    def relay_b(j):
        block = 2 * lax.rem(z + 1 + 2 * j, 4) + j
        arrived(bm_in.at[j], b_r.at[j])
        total = part_b[block].astype(f32) + bm_in[j].astype(f32)
        part_b[block, :, :b_cols] = total[:, :b_cols].astype(bf16)
        part_b[block, :, b_cols:] = with_sum(total_squares(total[:, b_cols:]))
        remote(
            part_b.at[block], b_in.at[j, j], b_s.at[4 + j], b_r.at[4 + j], other_z(1 + 2 * j)
        ).start()

    def relay_a(j):
        block = lax.rem(z + 1 + 2 * j, 4)
        arrived(am_in.at[j], a_r.at[j])
        a2[block, halves[j]] = (
            a2[block, halves[j]].astype(f32) + am_in[j].astype(f32)
        ).astype(bf16)
        remote(
            a2.at[block, halves[j]], a_in.at[j, halves[j]], a_s.at[4 + j], a_r.at[4 + j],
            other_z(1 + 2 * j),
        ).start()

    for j in range(2):
        relay_b(j)
    lax.fori_loop(0, 2, second_a, 0)
    for j in range(2):
        arrived(b_in.at[1 - j, j], b_r.at[2 + j])
        arrived(b_in.at[j, j], b_r.at[4 + j])

    def sum_b(j):
        return part_b[2 * z + j].astype(f32) + b_in[0, j].astype(f32) + b_in[1, j].astype(f32)

    away = sum_b(1 - yh)
    b2_out[:, :b_cols] = away[:, :b_cols].astype(bf16)
    b2_out[:, b_cols:] = with_sum(total_squares(away[:, b_cols:]))
    remote(b2_out, b2_in, b2_s.at[0], b2_r.at[0], y_peer).start()
    b_keep[...] = sum_b(yh)
    lax.fori_loop(2, 4, second_a, 0)
    for j in range(2):
        relay_a(j)
    arrived(b2_in, b2_r.at[0])

    def sum_b2(start, width):
        cols = slice(start, start + width)
        return b_keep[:, cols] + b2_in[:, cols].astype(f32)

    scale = lax.rsqrt(total_squares(sum_b2(b_cols, 128)) / D + norm_eps)

    def write_hidden(start, gate, upward):
        gate = gate * scale
        hb[q, :, start : start + gate.shape[1]] = (
            gate / (1.0 + jnp.exp(-gate)) * (upward * scale)
        ).astype(bf16)

    h_parts = (hb.at[:, :, pl.ds(A_COLS, b_half)], hb.at[:, :, pl.ds(0, A_COLS)])
    write_hidden(A_COLS, sum_b2(0, b_half), sum_b2(b_half, b_half))
    gather_start(h_parts[0], h_s.at[0], h_r.at[0], over_z)
    for j in range(2):
        arrived(a_in.at[1 - j, halves[j]], a_r.at[2 + j])
        arrived(a_in.at[j, halves[j]], a_r.at[4 + j])

    def sum_a(start):
        cols = slice(start, start + A_COLS)
        return (
            a2[z, :, cols].astype(f32) + a_in[0, :, cols].astype(f32)
            + a_in[1, :, cols].astype(f32)
        )

    write_hidden(0, sum_a(0), sum_a(A_COLS))
    gather_start(h_parts[1], h_s.at[1], h_r.at[1], over_z)
    project(hb, h_parts, ((A_COLS, b_half), (0, A_COLS)), wd, h_s, h_r, g_out, g_in, gl_in, g_s, g_r)
    down = gathered_sum(g_out, g_in, gy_out, gy_in, g_s, g_r)
    lay_x[c] = (resid_rows[mine] + down).astype(bf16)
    remote(lay_x.at[c], lay_x.at[c], o_s.at[1], o_r.at[1], sibling).start()
    arrived(att_x.at[1 - c], o_r.at[0])
    arrived(lay_x.at[1 - c], o_r.at[1])

    for k in range(1, GROUPS):
        left(lat_in.at[0], l_s.at[k])
    for i, (src, dst) in enumerate(weights):
        left(src, w_s.at[i])
    for p in range(2):
        finish_gather(v_parts[p], v_s.at[p])
        finish_gather(h_parts[p], h_s.at[p])
    finish_sends(c_out, cy_out, c_s)
    finish_sends(g_out, gy_out, g_s)
    finish_gather(xb, x_s)
    for i in range(4):
        left(part_a.at[0], a1_s.at[i])
    for i in range(6):
        left(part_b.at[0], b_s.at[i])
        left(a2.at[0, upper], a_s.at[i])
    left(b2_out, b2_s.at[0])
    left(att_x.at[0], o_s.at[0])
    left(lay_x.at[0], o_s.at[1])


def finish_kernel(att_ref, lay_ref, attended_ref, out_ref, turned):
    feats = attended_ref.shape[0]
    c = lax.rem(lax.axis_index("tp"), 2)
    own = pl.ds(pl.multiple_of(c * feats, feats), feats)
    for exchange, target in ((att_ref, attended_ref), (lay_ref, out_ref)):
        stacked = exchange[...].reshape(-1, 2 * feats).astype(jnp.float32)
        turned[...] = jnp.transpose(stacked, (1, 0))
        target[...] = turned[own].astype(target.dtype)


def run_layer(
    lengths, dest_group, moved_slot, queries, kv_cache, residual_in, norm_gain, up_value, out_proj,
    gate_proj, up_proj, down_proj,
):
    slots, all_heads, _ = queries.shape
    heads = up_value.shape[0]
    rows, width = GROUPS * slots, heads * 128
    queries = jnp.swapaxes(queries, 1, 2)
    kv_cache = jnp.swapaxes(kv_cache, 1, 2)
    total_rows, feats = residual_in.shape
    ff = gate_proj.shape[1]
    both = 2 * feats
    a_cols, b_cols = 2 * A_COLS, 2 * (ff - A_COLS) + 128
    f32, bf16 = jnp.float32, jnp.bfloat16
    vmem = pl.BlockSpec(memory_space=pltpu.VMEM)
    smem = pl.BlockSpec(memory_space=pltpu.SMEM)
    hbm = pl.BlockSpec(memory_space=pl.ANY)
    dma = pltpu.SemaphoreType.DMA
    block = jax.ShapeDtypeStruct((2, rows, both), bf16)
    turned = jax.ShapeDtypeStruct((feats, total_rows), bf16)
    att_x, lay_x = pl.pallas_call(
        layer_kernel,
        name="layer",
        out_shape=(block, block),
        in_specs=[smem, smem, smem, hbm, hbm, hbm, hbm, vmem, hbm, hbm, hbm, hbm],
        out_specs=(vmem, vmem),
        scratch_shapes=[
            pltpu.VMEM(queries.shape, bf16),
            pltpu.VMEM(kv_cache.shape, bf16),
            pltpu.VMEM(up_value.shape, bf16),
            pltpu.VMEM((slots, all_heads, KV), bf16),
            pltpu.VMEM((GROUPS, slots, heads, KV), bf16),
            pltpu.VMEM((KV // 128, rows * heads, 128), f32),
            pltpu.VMEM((rows, width), bf16),
            pltpu.VMEM((both, width), bf16),
            pltpu.VMEM((both, ff), bf16),
            pltpu.VMEM((both, ff), bf16),
            pltpu.VMEM((both, ff), bf16),
            pltpu.VMEM((both, total_rows), bf16),
            pltpu.VMEM((feats, 128), bf16),
            pltpu.VMEM((both, 128), bf16),
            pltpu.VMEM((8, rows, width), bf16),
            pltpu.VMEM((8, rows, both), bf16),
            pltpu.VMEM((4, 2, rows, both), bf16),
            pltpu.VMEM((rows, both), bf16),
            pltpu.VMEM((rows, both), bf16),
            pltpu.VMEM((rows, both), bf16),
            pltpu.VMEM((8, rows, both + 128), bf16),
            pltpu.VMEM((8, rows, a_cols), bf16),
            pltpu.VMEM((8, rows, b_cols), bf16),
            pltpu.VMEM((4, rows, a_cols), bf16),
            pltpu.VMEM((4, rows, a_cols), bf16),
            pltpu.VMEM((2, rows // 2, a_cols), bf16),
            pltpu.VMEM((2, rows, a_cols), bf16),
            pltpu.VMEM((2, rows, b_cols), bf16),
            pltpu.VMEM((2, 2, rows, b_cols), bf16),
            pltpu.VMEM((rows, b_cols), bf16),
            pltpu.VMEM((rows, b_cols), bf16),
            pltpu.VMEM((rows, b_cols), f32),
            pltpu.VMEM((8, rows, ff), bf16),
            pltpu.VMEM((8, rows, both), bf16),
            pltpu.VMEM((4, 2, rows, both), bf16),
            pltpu.VMEM((rows, both), bf16),
            pltpu.VMEM((rows, both), bf16),
            pltpu.VMEM((rows, both), bf16),
            pltpu.VMEM((rows, both), f32),
            pltpu.VMEM((total_rows, both), f32),
            pltpu.VMEM((1, both), f32),
            pltpu.VMEM((both, total_rows), f32),
            dma((2, slots)), dma, dma, dma((8,)), dma((8,)),
            dma((6,)), dma((6,)), dma((6,)), dma((2, 18)), dma((2, 18)),
            dma((6,)), dma((6,)), dma((18,)), dma((18,)),
            dma((4,)), dma((4,)), dma((6,)), dma((6,)), dma((6,)), dma((6,)), dma((1,)), dma((1,)),
            dma((2, 18)), dma((2, 18)), dma((6,)), dma((6,)), dma((2,)), dma((2,)),
        ],
        compiler_params=pltpu.CompilerParams(
            collective_id=0, has_side_effects=True, vmem_limit_bytes=62 << 20
        ),
        cost_estimate=pl.CostEstimate(
            flops=2 * total_rows * 8 * feats * (width + 3 * ff), bytes_accessed=30 << 20,
            transcendentals=1 << 20,
        ),
    )(
        lengths[:, 0, :], dest_group[:, 0], moved_slot[:, 0], queries, kv_cache, up_value,
        jnp.swapaxes(residual_in, 0, 1), norm_gain, jnp.swapaxes(out_proj, 0, 1),
        gate_proj, up_proj, jnp.swapaxes(down_proj, 0, 1),
    )
    attended, layer_out = pl.pallas_call(
        finish_kernel,
        name="finish",
        out_shape=(turned, turned),
        in_specs=[vmem, vmem],
        out_specs=(vmem, vmem),
        scratch_shapes=[pltpu.VMEM((both, total_rows), f32)],
    )(att_x, lay_x)
    return jnp.swapaxes(attended, 0, 1), jnp.swapaxes(layer_out, 0, 1)


def shards(
    queries,
    kv_cache,
    lengths,
    dest_group,
    moved_slot,
    residual_in,
    norm_gain,
    up_value,
    out_proj,
    gate_proj,
    up_proj,
    down_proj,
):
    return run_layer(
        lengths, dest_group, moved_slot, queries, kv_cache, residual_in, norm_gain, up_value,
        out_proj, gate_proj, up_proj, down_proj,
    )


def solution(mesh):
    return jax.shard_map(
        shards,
        mesh=mesh,
        in_specs=(
            P(("dp", "tp"), None, None),
            P(("dp", "tp"), None, None),
            P(None, "tp", None),
            P(None, "tp"),
            P(None, "tp"),
            P("dp", "tp"),
            P("tp"),
            P("dp", None, None),
            P("dp", "tp"),
            P("tp", "dp"),
            P("tp", "dp"),
            P("dp", "tp"),
        ),
        out_specs=(P("dp", "tp"), P("dp", "tp")),
        check_vma=False,
    )
```

```python
import jax
import jax.numpy as jnp
from jax import lax
from jax.experimental import pallas as pl
from jax.experimental.pallas import tpu as pltpu
from jax.sharding import PartitionSpec as P

MESH = pl.DeviceIdType.MESH
KV = 512
GROUPS = 8
exponent_scale = 192.0 ** (-0.5) * 1.4426950408889634


D = 7168
norm_eps = 1e-06
A_COLS = 1152


def layer_kernel(
    length_ref, partner_ref, slot_ref, query_ref, cache_ref, up_ref, resid_ref, gain_ref,
    wo_ref, wg_ref, wu_ref, wd_ref, att_x, lay_x,
    query_buf, cache_buf, up_buf, lat_out, lat_in, wide, vals,
    wo, wg, wu, wd, resid_both, gain_own, gain_both,
    vb, c_out, c_in, cy_out, cy_in, cl_in, xb, part_a, part_b, a1_in, a2, am_in, a_in, bm_in, b_in,
    b2_out, b2_in, b_keep, hb, g_out, g_in, gy_out, gy_in, gl_in, summed, resid_rows, gain_row, turned,
    load_sem, up_sem, own_sem, l_s, l_r,
    w_l, w_s, w_r, v_s, v_r, c_s, c_r, x_s, x_r, a1_s, a1_r, a_s, a_r, b_s, b_r, b2_s, b2_r,
    h_s, h_r, g_s, g_r, o_s, o_r,
):
    g = lax.axis_index("dp")
    t = lax.axis_index("tp")
    c = lax.rem(t, 2)
    q = t // 2
    z = q // 2
    yh = lax.rem(q, 2)
    x = g // 2
    yl = lax.rem(g, 2)
    slots = query_ref.shape[0]
    heads = up_ref.shape[0]
    rows = GROUPS * slots
    feats = wo_ref.shape[0]
    ff = wg_ref.shape[1]
    both = 2 * feats
    b_half = ff - A_COLS
    b_cols = 2 * b_half
    half = rows // 2
    f32 = jnp.float32
    bf16 = jnp.bfloat16

    def other_group(k):
        return (lax.rem(g + k, GROUPS), t)

    def other_z(k):
        return (g, lax.rem(z + k, 4) * 4 + yh * 2 + c)

    def chip(zp):
        return (g, zp * 4 + yh * 2 + c)

    def other_x(k):
        return (lax.rem(x + k, 4) * 2 + yl, t)

    low_peer = (x * 2 + 1 - yl, t)
    y_peer = (g, z * 4 + (1 - yh) * 2 + c)
    sibling = (g, q * 2 + 1 - c)

    def remote(src, dst, send_sem, recv_sem, device):
        return pltpu.make_async_remote_copy(
            src_ref=src, dst_ref=dst, send_sem=send_sem, recv_sem=recv_sem,
            device_id=device, device_id_type=MESH,
        )

    def arrived(ref, sem):
        remote(ref, ref, sem, sem, sibling).wait_recv()

    def left(ref, sem):
        remote(ref, ref, sem, sem, sibling).wait_send()

    def order(i):
        return i + (i // 2) * (5 - 2 * i)

    def loads(r):
        return (
            pltpu.make_async_copy(query_ref.at[r], query_buf.at[r], load_sem.at[0, r]),
            pltpu.make_async_copy(cache_ref.at[r], cache_buf.at[r], load_sem.at[1, r]),
        )

    for r in range(slots):
        for copy in loads(r):
            copy.start()
    up_copy = pltpu.make_async_copy(up_ref, up_buf, up_sem)
    up_copy.start()
    barrier = pltpu.get_barrier_semaphore()
    greeted = [other_group(k) for k in range(1, GROUPS)]
    greeted += [other_z(k) for k in (1, 2, 3)] + [y_peer, sibling]
    for device in greeted:
        pl.semaphore_signal(barrier, inc=1, device_id=device, device_id_type=MESH)

    own_rows = pl.ds(pl.multiple_of(c * feats, feats), feats)
    gain_own[...] = jnp.transpose(
        jnp.broadcast_to(gain_ref[...].astype(f32), (128, feats)), (1, 0)
    ).astype(bf16)
    weights = (
        (wo_ref, wo), (resid_ref, resid_both), (gain_own, gain_both),
        (wg_ref, wg), (wu_ref, wu), (wd_ref, wd),
    )

    def start_weights():
        for i, (src, dst) in enumerate(weights):
            remote(src, dst.at[own_rows], w_s.at[i], w_r.at[i], sibling).start()
            pltpu.make_async_copy(src, dst.at[own_rows], w_l.at[i]).start()

    upper = pl.ds(0, half)
    lower = pl.ds(half, half)

    quarter = half // 2
    first = pl.ds(0, quarter)
    second = pl.ds(quarter, quarter)
    third = pl.ds(half, quarter)
    fourth = pl.ds(half + quarter, quarter)
    over_z = (other_z, y_peer, lambda k: lax.rem(z + 4 - k, 4) * 2 + yh,
              lambda k: lax.rem(z + 4 - k, 4) * 2 + 1 - yh)
    over_x = (other_x, low_peer, lambda k: lax.rem(x + 4 - k, 4) * 2 + yl,
              lambda k: lax.rem(x + 4 - k, 4) * 2 + 1 - yl)

    def push(ref, s, r, i, device):
        remote(ref, ref, s.at[i], r.at[i], device).start()

    def gather_start(buf, s, r, ways):
        ring, peer, near, far = ways
        own = buf.at[near(0)]
        push(own.at[upper], s, r, 0, peer)
        push(own.at[lower], s, r, 1, ring(1))
        push(own.at[lower], s, r, 2, ring(3))
        push(own.at[upper], s, r, 3, ring(1))
        push(own.at[upper], s, r, 4, ring(3))
        push(own.at[lower], s, r, 5, peer)

    def gather_relay(buf, s, r, ways):
        ring, peer, near, far = ways
        block = buf.at[far(0), upper]
        arrived(block, r.at[0])
        push(block, s, r, 6, ring(1))
        push(block, s, r, 7, ring(3))
        arrived(block, r.at[1])
        push(buf.at[near(1), third], s, r, 8, ring(1))
        push(buf.at[near(1), lower], s, r, 9, peer)
        arrived(block, r.at[2])
        push(buf.at[near(3), fourth], s, r, 10, ring(3))
        push(buf.at[near(3), lower], s, r, 11, peer)

    def gather_more(buf, s, r, ways):
        ring, peer, near, far = ways
        block = buf.at[far(0), upper]
        arrived(block, r.at[3])
        push(buf.at[near(1), first], s, r, 12, ring(1))
        arrived(block, r.at[4])
        push(buf.at[near(3), second], s, r, 13, ring(3))

    def gather_far(buf, s, r, ways, i):
        ring, peer, near, far = ways
        block = buf.at[far(0), upper]
        piece = buf.at[far(0), first]

        @pl.when(i == 1)
        def _():
            gather_more(buf, s, r, ways)
            arrived(block, r.at[6])
            push(buf.at[far(1), first], s, r, 14, ring(1))
            arrived(block, r.at[7])
            push(buf.at[far(3), second], s, r, 15, ring(3))
            arrived(piece, r.at[8])
            push(buf.at[near(2), third], s, r, 16, peer)
            arrived(piece, r.at[10])
            push(buf.at[near(2), fourth], s, r, 17, peer)

    def gather_ready(buf, r, ways, i):
        far = ways[3]
        block = buf.at[far(0), upper]
        piece = buf.at[far(0), first]

        @pl.when(i == 0)
        def _():
            arrived(block, r.at[5])

        @pl.when(i == 1)
        def _():
            arrived(block, r.at[9])

        @pl.when(i == 2)
        def _():
            arrived(block, r.at[11])

        @pl.when(i == 3)
        def _():
            for j in range(12, 18):
                arrived(piece, r.at[j])

    def finish_gather(buf, s):
        for i in range(18):
            left(buf.at[0, upper if i in (0, 1, 2, 3, 4, 5, 6, 7, 9, 11) else first], s.at[i])

    last = lax.rem(z + 2, 4)

    def project(buf, parts, columns, w, s, r, out, landed, late_in, out_s, out_r):
        for p, part in enumerate(parts):
            gather_relay(part, s.at[p], r.at[p], over_z)

        def step(i, carry):
            zp = lax.rem(z + 4 - order(i), 4)
            for p, part in enumerate(parts):
                gather_far(part, s.at[p], r.at[p], over_z, i)
            product = 0.0
            for p, part in enumerate(parts):
                gather_ready(part, r.at[p], over_z, i)
                start, width = columns[p]
                left_rows = buf[pl.ds(2 * zp, 2), :, start : start + width]
                product += lax.dot_general(
                    left_rows.reshape(2 * rows, width), w[:, start : start + width],
                    (((1,), (1,)), ((), ())), preferred_element_type=f32,
                )
            out[pl.ds(2 * zp, 2)] = product.astype(bf16).reshape(2, rows, both)

            @pl.when((zp != x) & (i < 3))
            def _():
                remote(
                    out.at[pl.ds(2 * zp, 2)], landed.at[x], out_s.at[zp], out_r.at[x],
                    (zp * 2 + yl, t),
                ).start()

            return carry

        lax.fori_loop(0, 4, step, 0)
        there = out.at[2 * last + 1 - yl]
        remote(there, late_in, out_s.at[5], out_r.at[5], low_peer).start()
        arrived(late_in, out_r.at[5])
        here = 2 * last + yl
        out[here] = (out[here].astype(f32) + late_in[...].astype(f32)).astype(bf16)

        @pl.when(last != x)
        def _():
            remote(
                out.at[here], landed.at[x, yl], out_s.at[last], out_r.at[x], (last * 2 + yl, t)
            ).start()

    def gathered_sum(out, landed, y_out, y_in, out_s, out_r):
        def over_x(j):
            total = out[2 * x + j].astype(f32)
            for k in (1, 3, 2):
                total += landed[lax.rem(x + k, 4), j].astype(f32)
            return total

        @pl.when(last != x)
        def _():
            for k in (1, 3, 2):
                p = lax.rem(x + k, 4)
                arrived(landed.at[p], out_r.at[p])
            y_out[...] = over_x(1 - yl).astype(bf16)
            remote(y_out, y_in, out_s.at[4], out_r.at[4], low_peer).start()
            total = over_x(yl)
            arrived(y_in, out_r.at[4])
            summed[...] = total + y_in[...].astype(f32)

        @pl.when(last == x)
        def _():
            for k in (1, 3, 2):
                p = lax.rem(x + k, 4)
                arrived(landed.at[p, yl], out_r.at[p])
            summed[...] = over_x(yl)

        return summed[...]

    def finish_sends(out, y_out, out_s):
        for k in (1, 2, 3):
            p = lax.rem(x + k, 4)

            @pl.when(p != last)
            def _():
                left(out.at[pl.ds(0, 2)], out_s.at[p])

            @pl.when(p == last)
            def _():
                left(out.at[0], out_s.at[p])

        @pl.when(last != x)
        def _():
            left(y_out, out_s.at[4])

        left(out.at[0], out_s.at[5])

    def with_sum(square_sum):
        high = square_sum.astype(bf16).astype(f32)
        lane = lax.broadcasted_iota(jnp.int32, (square_sum.shape[0], 128), 1)
        return jnp.where(
            lane == 0, high, jnp.where(lane == 1, square_sum - high, 0.0)
        ).astype(bf16)

    def send(k, r):
        p = lax.rem(g + k, GROUPS)
        return pltpu.make_async_remote_copy(
            src_ref=lat_out.at[pl.ds(r, 2), pl.ds(pl.multiple_of(p * heads, heads), heads)],
            dst_ref=lat_in.at[g, pl.ds(r, 2)],
            send_sem=l_s.at[k],
            recv_sem=l_r.at[g],
            device_id=(p, t),
            device_id_type=MESH,
        )

    def attend(r):
        for copy in loads(r):
            copy.wait()
        length = length_ref[g, r]
        cache = cache_buf[r]
        scores = lax.dot_general(
            query_buf[r], cache, (((0,), (0,)), ((), ())), preferred_element_type=jnp.float32
        )
        position = lax.broadcasted_iota(jnp.int32, scores.shape, 1)
        masked = jnp.where(position < length, scores, -jnp.inf)
        largest = jnp.max(masked, axis=1, keepdims=True)
        expterm = jnp.exp2((masked - largest) * exponent_scale)
        total = jnp.sum(expterm, axis=1, keepdims=True)
        latent = lax.dot_general(
            expterm.astype(jnp.bfloat16), cache[:KV], (((1,), (1,)), ((), ())),
            preferred_element_type=jnp.float32,
        )
        lat_out[r] = (latent * (1.0 / total)).astype(jnp.bfloat16)

    def pair(i, carry):
        attend(2 * i)
        attend(2 * i + 1)
        for k in (4, 3, 5, 2, 6, 1, 7):
            send(k, 2 * i).start()
        return carry

    attend(0)
    attend(1)
    pl.semaphore_wait(barrier, len(greeted))
    for k in (4, 3, 5, 2, 6, 1, 7):
        send(k, 0).start()
    lax.fori_loop(1, slots // 2, pair, 0)
    start_weights()
    own = pltpu.make_async_copy(
        lat_out.at[:, pl.ds(pl.multiple_of(g * heads, heads), heads)], lat_in.at[g], own_sem
    )
    own.start()
    own.wait()
    up_copy.wait()

    def widen(k, carry):
        s = lax.rem(g + k, GROUPS)

        @pl.when(k > 0)
        def _():
            pltpu.make_async_remote_copy(
                src_ref=lat_in.at[s], dst_ref=lat_in.at[s], send_sem=l_s.at[0],
                recv_sem=l_r.at[s], device_id=(s, t), device_id_type=MESH,
            ).wait_recv()

        step_rows = slots * heads
        block = lat_in[s].astype(jnp.float32).reshape(step_rows, KV)
        for lane in range(KV // 128):
            wide[lane, pl.ds(pl.multiple_of(s * step_rows, step_rows), step_rows)] = block[
                :, lane * 128 : (lane + 1) * 128
            ]
        return carry

    lax.fori_loop(0, GROUPS, widen, 0)
    count = GROUPS * slots
    row = lax.broadcasted_iota(jnp.int32, (count, count), 0)
    column = lax.broadcasted_iota(jnp.int32, (count, count), 1)
    source = row
    for group in range(GROUPS):
        partner = partner_ref[group]
        own_row = group * slots + slot_ref[group]
        source = jnp.where(row == own_row, partner * slots + slot_ref[partner], source)
    place = jnp.where(column == source, 1.0, 0.0).astype(jnp.bfloat16)
    half_cols = heads * 64
    v_parts = [vb.at[:, :, pl.ds(p * half_cols, half_cols)] for p in range(2)]
    for p in range(2):
        cols = slice(p * half_cols, (p + 1) * half_cols)
        for h in range(p * heads // 2, (p + 1) * heads // 2):
            head_rows = jnp.concatenate(
                [wide[lane, pl.ds(h, count, stride=heads), :] for lane in range(KV // 128)], axis=1
            )
            vals[:, h * 128 : (h + 1) * 128] = jnp.dot(
                head_rows.astype(jnp.bfloat16),
                up_buf[h],
                preferred_element_type=jnp.float32,
            ).astype(jnp.bfloat16)
        vb[q, :, cols] = jnp.dot(
            place, vals[:, cols], preferred_element_type=jnp.float32
        ).astype(jnp.bfloat16)
        gather_start(v_parts[p], v_s.at[p], v_r.at[p], over_z)

    def weight_ready(i):
        src, dst = weights[i]
        pltpu.make_async_copy(src, dst.at[own_rows], w_l.at[i]).wait()
        arrived(dst.at[own_rows], w_r.at[i])

    for i in range(3):
        weight_ready(i)
    mine = pl.ds(pl.multiple_of(c * rows, rows), rows)
    turned[...] = resid_both[...].astype(f32)
    resid_rows[...] = jnp.transpose(turned[...], (1, 0))
    gain_row[...] = jnp.transpose(gain_both[...].astype(f32), (1, 0))[:1]
    project(vb, v_parts, ((0, half_cols), (half_cols, half_cols)), wo, v_s, v_r, c_out, c_in, cl_in, c_s, c_r)
    attn = gathered_sum(c_out, c_in, cy_out, cy_in, c_s, c_r)
    resid = resid_rows[mine] + attn
    resid_rows[mine] = resid
    xb[g, :, :both] = (resid * gain_row[...]).astype(bf16)
    xb[g, :, both:] = with_sum(jnp.sum(resid * resid, axis=1, keepdims=True))
    gather_start(xb, x_s, x_r, over_x)
    att_x[c] = attn.astype(bf16)
    remote(att_x.at[c], att_x.at[c], o_s.at[0], o_r.at[0], sibling).start()
    for i in range(3, 6):
        weight_ready(i)

    gather_relay(xb, x_s, x_r, over_x)

    def first_products(i, carry):
        xp = lax.rem(x + 4 - order(i), 4)
        gather_far(xb, x_s, x_r, over_x, i)
        gather_ready(xb, x_r, over_x, i)
        block = xb[pl.ds(2 * xp, 2)].reshape(2 * rows, both + 128)
        pair = pl.ds(2 * xp, 2)
        lhs = block[:, :both]

        def product(w, start, width):
            return jnp.dot(
                lhs, w[:, start : start + width], preferred_element_type=f32
            ).astype(bf16).reshape(2, rows, width)

        part_a[pair, :, :A_COLS] = product(wg, 0, A_COLS)
        part_a[pair, :, A_COLS:] = product(wu, 0, A_COLS)
        remote(
            part_a.at[2 * xp + 1 - yh], a1_in.at[xp], a1_s.at[xp], a1_r.at[xp], y_peer
        ).start()
        part_b[pair, :, :b_half] = product(wg, A_COLS, b_half)
        part_b[pair, :, b_half:b_cols] = product(wu, A_COLS, b_half)
        part_b[pair, :, b_cols:] = block[:, both:].reshape(2, rows, 128)
        role = lax.rem(xp + 4 - z, 4)

        @pl.when(role == 2)
        def _():
            for j in range(2):
                remote(
                    part_b.at[2 * xp + j], bm_in.at[j], b_s.at[j], b_r.at[j], other_z(1 + 2 * j)
                ).start()

        for j in range(2):

            @pl.when(role == 3 - 2 * j)
            def _():
                remote(
                    part_b.at[2 * xp + j], b_in.at[1 - j, j], b_s.at[2 + j], b_r.at[2 + j],
                    other_z(3 - 2 * j),
                ).start()

        return carry

    lax.fori_loop(0, 4, first_products, 0)
    halves = (upper, lower)

    def second_a(i, carry):
        xp = lax.rem(x + 4 - order(i), 4)
        arrived(a1_in.at[xp], a1_r.at[xp])
        a2[xp] = (part_a[2 * xp + yh].astype(f32) + a1_in[xp].astype(f32)).astype(bf16)
        role = lax.rem(xp + 4 - z, 4)

        @pl.when(role == 2)
        def _():
            for j in range(2):
                remote(
                    a2.at[xp, halves[j]], am_in.at[j], a_s.at[j], a_r.at[j], other_z(1 + 2 * j)
                ).start()

        for j in range(2):

            @pl.when(role == 3 - 2 * j)
            def _():
                remote(
                    a2.at[xp, halves[j]], a_in.at[1 - j, halves[j]], a_s.at[2 + j],
                    a_r.at[2 + j], other_z(3 - 2 * j),
                ).start()

        return carry

    def total_squares(block):
        return block[:, 0:1] + block[:, 1:2]

    def relay_b(j):
        block = 2 * lax.rem(z + 1 + 2 * j, 4) + j
        arrived(bm_in.at[j], b_r.at[j])
        total = part_b[block].astype(f32) + bm_in[j].astype(f32)
        part_b[block, :, :b_cols] = total[:, :b_cols].astype(bf16)
        part_b[block, :, b_cols:] = with_sum(total_squares(total[:, b_cols:]))
        remote(
            part_b.at[block], b_in.at[j, j], b_s.at[4 + j], b_r.at[4 + j], other_z(1 + 2 * j)
        ).start()

    def relay_a(j):
        block = lax.rem(z + 1 + 2 * j, 4)
        arrived(am_in.at[j], a_r.at[j])
        a2[block, halves[j]] = (
            a2[block, halves[j]].astype(f32) + am_in[j].astype(f32)
        ).astype(bf16)
        remote(
            a2.at[block, halves[j]], a_in.at[j, halves[j]], a_s.at[4 + j], a_r.at[4 + j],
            other_z(1 + 2 * j),
        ).start()

    for j in range(2):
        relay_b(j)
    lax.fori_loop(0, 2, second_a, 0)
    for j in range(2):
        arrived(b_in.at[1 - j, j], b_r.at[2 + j])
        arrived(b_in.at[j, j], b_r.at[4 + j])

    def sum_b(j):
        return part_b[2 * z + j].astype(f32) + b_in[0, j].astype(f32) + b_in[1, j].astype(f32)

    away = sum_b(1 - yh)
    b2_out[:, :b_cols] = away[:, :b_cols].astype(bf16)
    b2_out[:, b_cols:] = with_sum(total_squares(away[:, b_cols:]))
    remote(b2_out, b2_in, b2_s.at[0], b2_r.at[0], y_peer).start()
    b_keep[...] = sum_b(yh)
    lax.fori_loop(2, 4, second_a, 0)
    for j in range(2):
        relay_a(j)
    arrived(b2_in, b2_r.at[0])

    def sum_b2(start, width):
        cols = slice(start, start + width)
        return b_keep[:, cols] + b2_in[:, cols].astype(f32)

    scale = lax.rsqrt(total_squares(sum_b2(b_cols, 128)) / D + norm_eps)

    def write_hidden(start, gate, upward):
        gate = gate * scale
        hb[q, :, start : start + gate.shape[1]] = (
            gate / (1.0 + jnp.exp(-gate)) * (upward * scale)
        ).astype(bf16)

    h_parts = (hb.at[:, :, pl.ds(A_COLS, b_half)], hb.at[:, :, pl.ds(0, A_COLS)])
    write_hidden(A_COLS, sum_b2(0, b_half), sum_b2(b_half, b_half))
    gather_start(h_parts[0], h_s.at[0], h_r.at[0], over_z)
    for j in range(2):
        arrived(a_in.at[1 - j, halves[j]], a_r.at[2 + j])
        arrived(a_in.at[j, halves[j]], a_r.at[4 + j])

    def sum_a(start):
        cols = slice(start, start + A_COLS)
        return (
            a2[z, :, cols].astype(f32) + a_in[0, :, cols].astype(f32)
            + a_in[1, :, cols].astype(f32)
        )

    write_hidden(0, sum_a(0), sum_a(A_COLS))
    gather_start(h_parts[1], h_s.at[1], h_r.at[1], over_z)
    project(hb, h_parts, ((A_COLS, b_half), (0, A_COLS)), wd, h_s, h_r, g_out, g_in, gl_in, g_s, g_r)
    down = gathered_sum(g_out, g_in, gy_out, gy_in, g_s, g_r)
    lay_x[c] = (resid_rows[mine] + down).astype(bf16)
    remote(lay_x.at[c], lay_x.at[c], o_s.at[1], o_r.at[1], sibling).start()
    arrived(att_x.at[1 - c], o_r.at[0])
    arrived(lay_x.at[1 - c], o_r.at[1])

    for k in range(1, GROUPS):
        left(lat_in.at[0], l_s.at[k])
    for i, (src, dst) in enumerate(weights):
        left(src, w_s.at[i])
    for p in range(2):
        finish_gather(v_parts[p], v_s.at[p])
        finish_gather(h_parts[p], h_s.at[p])
    finish_sends(c_out, cy_out, c_s)
    finish_sends(g_out, gy_out, g_s)
    finish_gather(xb, x_s)
    for i in range(4):
        left(part_a.at[0], a1_s.at[i])
    for i in range(6):
        left(part_b.at[0], b_s.at[i])
        left(a2.at[0, upper], a_s.at[i])
    left(b2_out, b2_s.at[0])
    left(att_x.at[0], o_s.at[0])
    left(lay_x.at[0], o_s.at[1])


def finish_kernel(att_ref, lay_ref, attended_ref, out_ref):
    feats = attended_ref.shape[0]
    both = 2 * feats
    width = pl.cdiv(feats, 128) * 128
    c = lax.rem(lax.axis_index("tp"), 2)
    for exchange, target in ((att_ref, attended_ref), (lay_ref, out_ref)):
        rows = 2 * exchange.shape[1]

        @pl.when(c == 0)
        def _():
            block = exchange[:, :, :width].reshape(rows, width)
            target[...] = jnp.transpose(block, (1, 0))[:feats]

        @pl.when(c == 1)
        def _():
            block = exchange[:, :, both - width :].reshape(rows, width)
            target[...] = jnp.transpose(block, (1, 0))[width - feats :]


def run_layer(
    lengths, dest_group, moved_slot, queries, kv_cache, residual_in, norm_gain, up_value, out_proj,
    gate_proj, up_proj, down_proj,
):
    slots, all_heads, _ = queries.shape
    heads = up_value.shape[0]
    rows, width = GROUPS * slots, heads * 128
    queries = jnp.swapaxes(queries, 1, 2)
    kv_cache = jnp.swapaxes(kv_cache, 1, 2)
    total_rows, feats = residual_in.shape
    ff = gate_proj.shape[1]
    both = 2 * feats
    a_cols, b_cols = 2 * A_COLS, 2 * (ff - A_COLS) + 128
    f32, bf16 = jnp.float32, jnp.bfloat16
    vmem = pl.BlockSpec(memory_space=pltpu.VMEM)
    smem = pl.BlockSpec(memory_space=pltpu.SMEM)
    hbm = pl.BlockSpec(memory_space=pl.ANY)
    dma = pltpu.SemaphoreType.DMA
    block = jax.ShapeDtypeStruct((2, rows, both), bf16)
    turned = jax.ShapeDtypeStruct((feats, total_rows), bf16)
    att_x, lay_x = pl.pallas_call(
        layer_kernel,
        name="layer",
        out_shape=(block, block),
        in_specs=[smem, smem, smem, hbm, hbm, hbm, hbm, vmem, hbm, hbm, hbm, hbm],
        out_specs=(vmem, vmem),
        scratch_shapes=[
            pltpu.VMEM(queries.shape, bf16),
            pltpu.VMEM(kv_cache.shape, bf16),
            pltpu.VMEM(up_value.shape, bf16),
            pltpu.VMEM((slots, all_heads, KV), bf16),
            pltpu.VMEM((GROUPS, slots, heads, KV), bf16),
            pltpu.VMEM((KV // 128, rows * heads, 128), f32),
            pltpu.VMEM((rows, width), bf16),
            pltpu.VMEM((both, width), bf16),
            pltpu.VMEM((both, ff), bf16),
            pltpu.VMEM((both, ff), bf16),
            pltpu.VMEM((both, ff), bf16),
            pltpu.VMEM((both, total_rows), bf16),
            pltpu.VMEM((feats, 128), bf16),
            pltpu.VMEM((both, 128), bf16),
            pltpu.VMEM((8, rows, width), bf16),
            pltpu.VMEM((8, rows, both), bf16),
            pltpu.VMEM((4, 2, rows, both), bf16),
            pltpu.VMEM((rows, both), bf16),
            pltpu.VMEM((rows, both), bf16),
            pltpu.VMEM((rows, both), bf16),
            pltpu.VMEM((8, rows, both + 128), bf16),
            pltpu.VMEM((8, rows, a_cols), bf16),
            pltpu.VMEM((8, rows, b_cols), bf16),
            pltpu.VMEM((4, rows, a_cols), bf16),
            pltpu.VMEM((4, rows, a_cols), bf16),
            pltpu.VMEM((2, rows // 2, a_cols), bf16),
            pltpu.VMEM((2, rows, a_cols), bf16),
            pltpu.VMEM((2, rows, b_cols), bf16),
            pltpu.VMEM((2, 2, rows, b_cols), bf16),
            pltpu.VMEM((rows, b_cols), bf16),
            pltpu.VMEM((rows, b_cols), bf16),
            pltpu.VMEM((rows, b_cols), f32),
            pltpu.VMEM((8, rows, ff), bf16),
            pltpu.VMEM((8, rows, both), bf16),
            pltpu.VMEM((4, 2, rows, both), bf16),
            pltpu.VMEM((rows, both), bf16),
            pltpu.VMEM((rows, both), bf16),
            pltpu.VMEM((rows, both), bf16),
            pltpu.VMEM((rows, both), f32),
            pltpu.VMEM((total_rows, both), f32),
            pltpu.VMEM((1, both), f32),
            pltpu.VMEM((both, total_rows), f32),
            dma((2, slots)), dma, dma, dma((8,)), dma((8,)),
            dma((6,)), dma((6,)), dma((6,)), dma((2, 18)), dma((2, 18)),
            dma((6,)), dma((6,)), dma((18,)), dma((18,)),
            dma((4,)), dma((4,)), dma((6,)), dma((6,)), dma((6,)), dma((6,)), dma((1,)), dma((1,)),
            dma((2, 18)), dma((2, 18)), dma((6,)), dma((6,)), dma((2,)), dma((2,)),
        ],
        compiler_params=pltpu.CompilerParams(
            collective_id=0, has_side_effects=True, vmem_limit_bytes=62 << 20
        ),
        cost_estimate=pl.CostEstimate(
            flops=2 * total_rows * 8 * feats * (width + 3 * ff), bytes_accessed=30 << 20,
            transcendentals=1 << 20,
        ),
    )(
        lengths[:, 0, :], dest_group[:, 0], moved_slot[:, 0], queries, kv_cache, up_value,
        jnp.swapaxes(residual_in, 0, 1), norm_gain, jnp.swapaxes(out_proj, 0, 1),
        gate_proj, up_proj, jnp.swapaxes(down_proj, 0, 1),
    )
    attended, layer_out = pl.pallas_call(
        finish_kernel,
        name="finish",
        out_shape=(turned, turned),
        in_specs=[vmem, vmem],
        out_specs=(vmem, vmem),
    )(att_x, lay_x)
    return jnp.swapaxes(attended, 0, 1), jnp.swapaxes(layer_out, 0, 1)


def shards(
    queries,
    kv_cache,
    lengths,
    dest_group,
    moved_slot,
    residual_in,
    norm_gain,
    up_value,
    out_proj,
    gate_proj,
    up_proj,
    down_proj,
):
    return run_layer(
        lengths, dest_group, moved_slot, queries, kv_cache, residual_in, norm_gain, up_value,
        out_proj, gate_proj, up_proj, down_proj,
    )


def solution(mesh):
    return jax.shard_map(
        shards,
        mesh=mesh,
        in_specs=(
            P(("dp", "tp"), None, None),
            P(("dp", "tp"), None, None),
            P(None, "tp", None),
            P(None, "tp"),
            P(None, "tp"),
            P("dp", "tp"),
            P("tp"),
            P("dp", None, None),
            P("dp", "tp"),
            P("tp", "dp"),
            P("tp", "dp"),
            P("dp", "tp"),
        ),
        out_specs=(P("dp", "tp"), P("dp", "tp")),
        check_vma=False,
    )
```

```python
import jax
import jax.numpy as jnp
from jax import lax
from jax.experimental import pallas as pl
from jax.experimental.pallas import tpu as pltpu
from jax.sharding import PartitionSpec as P

MESH = pl.DeviceIdType.MESH
KV = 512
GROUPS = 8
exponent_scale = 192.0 ** (-0.5) * 1.4426950408889634


D = 7168
norm_eps = 1e-06
A_COLS = 1152


def layer_kernel(
    length_ref, partner_ref, slot_ref, query_ref, cache_ref, up_ref, resid_ref, gain_ref,
    wo_ref, wg_ref, wu_ref, wd_ref, att_x, lay_x,
    query_buf, cache_buf, up_buf, lat_out, lat_in, wide, vals,
    wo, wg, wu, wd, resid_both, gain_own, gain_both,
    vb, c_out, c_in, cy_out, cy_in, cl_in, xb, part_a, part_b, a1_in, a2, am_in, a_in, bm_in, b_in,
    b2_out, b2_in, b_keep, hb, g_out, g_in, gy_out, gy_in, gl_in, summed, resid_rows, gain_row, turned,
    load_sem, up_sem, own_sem, l_s, l_r,
    w_l, w_s, w_r, v_s, v_r, c_s, c_r, x_s, x_r, a1_s, a1_r, a_s, a_r, b_s, b_r, b2_s, b2_r,
    h_s, h_r, g_s, g_r, o_s, o_r,
):
    g = lax.axis_index("dp")
    t = lax.axis_index("tp")
    c = lax.rem(t, 2)
    q = t // 2
    z = q // 2
    yh = lax.rem(q, 2)
    x = g // 2
    yl = lax.rem(g, 2)
    slots = query_ref.shape[0]
    heads = up_ref.shape[0]
    rows = GROUPS * slots
    feats = wo_ref.shape[0]
    ff = wg_ref.shape[1]
    both = 2 * feats
    b_half = ff - A_COLS
    b_cols = 2 * b_half
    half = rows // 2
    f32 = jnp.float32
    bf16 = jnp.bfloat16

    def other_group(k):
        return (lax.rem(g + k, GROUPS), t)

    def other_z(k):
        return (g, lax.rem(z + k, 4) * 4 + yh * 2 + c)

    def chip(zp):
        return (g, zp * 4 + yh * 2 + c)

    def other_x(k):
        return (lax.rem(x + k, 4) * 2 + yl, t)

    low_peer = (x * 2 + 1 - yl, t)
    y_peer = (g, z * 4 + (1 - yh) * 2 + c)
    sibling = (g, q * 2 + 1 - c)

    def remote(src, dst, send_sem, recv_sem, device):
        return pltpu.make_async_remote_copy(
            src_ref=src, dst_ref=dst, send_sem=send_sem, recv_sem=recv_sem,
            device_id=device, device_id_type=MESH,
        )

    def arrived(ref, sem):
        remote(ref, ref, sem, sem, sibling).wait_recv()

    def left(ref, sem):
        remote(ref, ref, sem, sem, sibling).wait_send()

    def order(i):
        return i + (i // 2) * (5 - 2 * i)

    def loads(r):
        return (
            pltpu.make_async_copy(query_ref.at[r], query_buf.at[r], load_sem.at[0, r]),
            pltpu.make_async_copy(cache_ref.at[r], cache_buf.at[r], load_sem.at[1, r]),
        )

    for r in range(slots):
        for copy in loads(r):
            copy.start()
    up_copy = pltpu.make_async_copy(up_ref, up_buf, up_sem)
    up_copy.start()
    barrier = pltpu.get_barrier_semaphore()
    greeted = [other_group(k) for k in range(1, GROUPS)]
    greeted += [other_z(k) for k in (1, 2, 3)] + [y_peer, sibling]
    for device in greeted:
        pl.semaphore_signal(barrier, inc=1, device_id=device, device_id_type=MESH)

    own_rows = pl.ds(pl.multiple_of(c * feats, feats), feats)
    gain_own[...] = jnp.transpose(
        jnp.broadcast_to(gain_ref[...].astype(f32), (128, feats)), (1, 0)
    ).astype(bf16)
    weights = (
        (wo_ref, wo), (resid_ref, resid_both), (gain_own, gain_both),
        (wg_ref, wg), (wu_ref, wu), (wd_ref, wd),
    )

    def start_weights():
        for i, (src, dst) in enumerate(weights):
            remote(src, dst.at[own_rows], w_s.at[i], w_r.at[i], sibling).start()
            pltpu.make_async_copy(src, dst.at[own_rows], w_l.at[i]).start()

    upper = pl.ds(0, half)
    lower = pl.ds(half, half)

    quarter = half // 2
    first = pl.ds(0, quarter)
    second = pl.ds(quarter, quarter)
    third = pl.ds(half, quarter)
    fourth = pl.ds(half + quarter, quarter)
    over_z = (other_z, y_peer, lambda k: lax.rem(z + 4 - k, 4) * 2 + yh,
              lambda k: lax.rem(z + 4 - k, 4) * 2 + 1 - yh)
    over_x = (other_x, low_peer, lambda k: lax.rem(x + 4 - k, 4) * 2 + yl,
              lambda k: lax.rem(x + 4 - k, 4) * 2 + 1 - yl)

    def push(ref, s, r, i, device):
        remote(ref, ref, s.at[i], r.at[i], device).start()

    def gather_start(buf, s, r, ways):
        ring, peer, near, far = ways
        own = buf.at[near(0)]
        push(own.at[upper], s, r, 0, peer)
        push(own.at[lower], s, r, 1, ring(1))
        push(own.at[lower], s, r, 2, ring(3))
        push(own.at[upper], s, r, 3, ring(1))
        push(own.at[upper], s, r, 4, ring(3))
        push(own.at[lower], s, r, 5, peer)

    def gather_relay(buf, s, r, ways):
        ring, peer, near, far = ways
        block = buf.at[far(0), upper]
        arrived(block, r.at[0])
        push(block, s, r, 6, ring(1))
        push(block, s, r, 7, ring(3))
        arrived(block, r.at[1])
        push(buf.at[near(1), third], s, r, 8, ring(1))
        push(buf.at[near(1), lower], s, r, 9, peer)
        arrived(block, r.at[2])
        push(buf.at[near(3), fourth], s, r, 10, ring(3))
        push(buf.at[near(3), lower], s, r, 11, peer)

    def gather_more(buf, s, r, ways):
        ring, peer, near, far = ways
        block = buf.at[far(0), upper]
        arrived(block, r.at[3])
        push(buf.at[near(1), first], s, r, 12, ring(1))
        arrived(block, r.at[4])
        push(buf.at[near(3), second], s, r, 13, ring(3))

    def gather_far(buf, s, r, ways, i):
        ring, peer, near, far = ways
        block = buf.at[far(0), upper]
        piece = buf.at[far(0), first]

        @pl.when(i == 1)
        def _():
            gather_more(buf, s, r, ways)
            arrived(block, r.at[6])
            push(buf.at[far(1), first], s, r, 14, ring(1))
            arrived(block, r.at[7])
            push(buf.at[far(3), second], s, r, 15, ring(3))
            arrived(piece, r.at[8])
            push(buf.at[near(2), third], s, r, 16, peer)
            arrived(piece, r.at[10])
            push(buf.at[near(2), fourth], s, r, 17, peer)

    def gather_ready(buf, r, ways, i):
        far = ways[3]
        block = buf.at[far(0), upper]
        piece = buf.at[far(0), first]

        @pl.when(i == 0)
        def _():
            arrived(block, r.at[5])

        @pl.when(i == 1)
        def _():
            arrived(block, r.at[9])

        @pl.when(i == 2)
        def _():
            arrived(block, r.at[11])

        @pl.when(i == 3)
        def _():
            for j in range(12, 18):
                arrived(piece, r.at[j])

    def finish_gather(buf, s):
        for i in range(18):
            left(buf.at[0, upper if i in (0, 1, 2, 3, 4, 5, 6, 7, 9, 11) else first], s.at[i])

    last = lax.rem(z + 2, 4)

    def project(buf, parts, columns, w, s, r, out, landed, late_in, out_s, out_r):
        for p, part in enumerate(parts):
            gather_relay(part, s.at[p], r.at[p], over_z)

        def step(i, carry):
            zp = lax.rem(z + 4 - order(i), 4)
            for p, part in enumerate(parts):
                gather_far(part, s.at[p], r.at[p], over_z, i)
            product = 0.0
            for p, part in enumerate(parts):
                gather_ready(part, r.at[p], over_z, i)
                start, width = columns[p]
                left_rows = buf[pl.ds(2 * zp, 2), :, start : start + width]
                product += lax.dot_general(
                    left_rows.reshape(2 * rows, width), w[:, start : start + width],
                    (((1,), (1,)), ((), ())), preferred_element_type=f32,
                )
            out[pl.ds(2 * zp, 2)] = product.astype(bf16).reshape(2, rows, both)

            @pl.when((zp != x) & (i < 3))
            def _():
                remote(
                    out.at[pl.ds(2 * zp, 2)], landed.at[x], out_s.at[zp], out_r.at[x],
                    (zp * 2 + yl, t),
                ).start()

            return carry

        lax.fori_loop(0, 4, step, 0)
        there = out.at[2 * last + 1 - yl]
        remote(there, late_in, out_s.at[5], out_r.at[5], low_peer).start()
        arrived(late_in, out_r.at[5])
        here = 2 * last + yl
        out[here] = (out[here].astype(f32) + late_in[...].astype(f32)).astype(bf16)

        @pl.when(last != x)
        def _():
            remote(
                out.at[here], landed.at[x, yl], out_s.at[last], out_r.at[x], (last * 2 + yl, t)
            ).start()

    def gathered_sum(out, landed, y_out, y_in, out_s, out_r):
        def over_x(j):
            total = out[2 * x + j].astype(f32)
            for k in (1, 3, 2):
                total += landed[lax.rem(x + k, 4), j].astype(f32)
            return total

        @pl.when(last != x)
        def _():
            for k in (1, 3, 2):
                p = lax.rem(x + k, 4)
                arrived(landed.at[p], out_r.at[p])
            y_out[...] = over_x(1 - yl).astype(bf16)
            remote(y_out, y_in, out_s.at[4], out_r.at[4], low_peer).start()
            total = over_x(yl)
            arrived(y_in, out_r.at[4])
            summed[...] = total + y_in[...].astype(f32)

        @pl.when(last == x)
        def _():
            for k in (1, 3, 2):
                p = lax.rem(x + k, 4)
                arrived(landed.at[p, yl], out_r.at[p])
            summed[...] = over_x(yl)

        return summed[...]

    def finish_sends(out, y_out, out_s):
        for k in (1, 2, 3):
            p = lax.rem(x + k, 4)

            @pl.when(p != last)
            def _():
                left(out.at[pl.ds(0, 2)], out_s.at[p])

            @pl.when(p == last)
            def _():
                left(out.at[0], out_s.at[p])

        @pl.when(last != x)
        def _():
            left(y_out, out_s.at[4])

        left(out.at[0], out_s.at[5])

    def with_sum(square_sum):
        high = square_sum.astype(bf16).astype(f32)
        lane = lax.broadcasted_iota(jnp.int32, (square_sum.shape[0], 128), 1)
        return jnp.where(
            lane == 0, high, jnp.where(lane == 1, square_sum - high, 0.0)
        ).astype(bf16)

    def send(k, r):
        p = lax.rem(g + k, GROUPS)
        return pltpu.make_async_remote_copy(
            src_ref=lat_out.at[pl.ds(r, 2), pl.ds(pl.multiple_of(p * heads, heads), heads)],
            dst_ref=lat_in.at[g, pl.ds(r, 2)],
            send_sem=l_s.at[k],
            recv_sem=l_r.at[g],
            device_id=(p, t),
            device_id_type=MESH,
        )

    def attend(r):
        for copy in loads(r):
            copy.wait()
        length = length_ref[g, r]
        cache = cache_buf[r]
        scores = lax.dot_general(
            query_buf[r], cache, (((0,), (0,)), ((), ())), preferred_element_type=jnp.float32
        )
        position = lax.broadcasted_iota(jnp.int32, scores.shape, 1)
        masked = jnp.where(position < length, scores, -jnp.inf)
        largest = jnp.max(masked, axis=1, keepdims=True)
        expterm = jnp.exp2((masked - largest) * exponent_scale)
        total = jnp.sum(expterm, axis=1, keepdims=True)
        latent = lax.dot_general(
            expterm.astype(jnp.bfloat16), cache[:KV], (((1,), (1,)), ((), ())),
            preferred_element_type=jnp.float32,
        )
        lat_out[r] = (latent * (1.0 / total)).astype(jnp.bfloat16)

    def pair(i, carry):
        attend(2 * i)
        attend(2 * i + 1)
        for k in (4, 3, 5, 2, 6, 1, 7):
            send(k, 2 * i).start()
        return carry

    attend(0)
    attend(1)
    pl.semaphore_wait(barrier, len(greeted))
    for k in (4, 3, 5, 2, 6, 1, 7):
        send(k, 0).start()
    lax.fori_loop(1, slots // 2, pair, 0)
    start_weights()
    own = pltpu.make_async_copy(
        lat_out.at[:, pl.ds(pl.multiple_of(g * heads, heads), heads)], lat_in.at[g], own_sem
    )
    own.start()
    own.wait()
    up_copy.wait()

    def widen(k, carry):
        s = lax.rem(g + k, GROUPS)

        @pl.when(k > 0)
        def _():
            pltpu.make_async_remote_copy(
                src_ref=lat_in.at[s], dst_ref=lat_in.at[s], send_sem=l_s.at[0],
                recv_sem=l_r.at[s], device_id=(s, t), device_id_type=MESH,
            ).wait_recv()

        step_rows = slots * heads
        block = lat_in[s].astype(jnp.float32).reshape(step_rows, KV)
        for lane in range(KV // 128):
            wide[lane, pl.ds(pl.multiple_of(s * step_rows, step_rows), step_rows)] = block[
                :, lane * 128 : (lane + 1) * 128
            ]
        return carry

    lax.fori_loop(0, GROUPS, widen, 0)
    count = GROUPS * slots
    row = lax.broadcasted_iota(jnp.int32, (count, count), 0)
    column = lax.broadcasted_iota(jnp.int32, (count, count), 1)
    source = row
    for group in range(GROUPS):
        partner = partner_ref[group]
        own_row = group * slots + slot_ref[group]
        source = jnp.where(row == own_row, partner * slots + slot_ref[partner], source)
    place = jnp.where(column == source, 1.0, 0.0).astype(jnp.bfloat16)
    half_cols = heads * 64
    v_parts = [vb.at[:, :, pl.ds(p * half_cols, half_cols)] for p in range(2)]
    for p in range(2):
        cols = slice(p * half_cols, (p + 1) * half_cols)
        for h in range(p * heads // 2, (p + 1) * heads // 2):
            head_rows = jnp.concatenate(
                [wide[lane, pl.ds(h, count, stride=heads), :] for lane in range(KV // 128)], axis=1
            )
            vals[:, h * 128 : (h + 1) * 128] = jnp.dot(
                head_rows.astype(jnp.bfloat16),
                up_buf[h],
                preferred_element_type=jnp.float32,
            ).astype(jnp.bfloat16)
        vb[q, :, cols] = jnp.dot(
            place, vals[:, cols], preferred_element_type=jnp.float32
        ).astype(jnp.bfloat16)
        gather_start(v_parts[p], v_s.at[p], v_r.at[p], over_z)

    def weight_ready(i):
        src, dst = weights[i]
        pltpu.make_async_copy(src, dst.at[own_rows], w_l.at[i]).wait()
        arrived(dst.at[own_rows], w_r.at[i])

    for i in range(3):
        weight_ready(i)
    mine = pl.ds(pl.multiple_of(c * rows, rows), rows)
    turned[...] = resid_both[...].astype(f32)
    resid_rows[...] = jnp.transpose(turned[...], (1, 0))
    gain_row[...] = jnp.transpose(gain_both[...].astype(f32), (1, 0))[:1]
    project(vb, v_parts, ((0, half_cols), (half_cols, half_cols)), wo, v_s, v_r, c_out, c_in, cl_in, c_s, c_r)
    attn = gathered_sum(c_out, c_in, cy_out, cy_in, c_s, c_r)
    resid = resid_rows[mine] + attn
    resid_rows[mine] = resid
    xb[g, :, :both] = (resid * gain_row[...]).astype(bf16)
    xb[g, :, both:] = with_sum(jnp.sum(resid * resid, axis=1, keepdims=True))
    gather_start(xb, x_s, x_r, over_x)
    att_x[c] = attn.astype(bf16)
    remote(att_x.at[c], att_x.at[c], o_s.at[0], o_r.at[0], sibling).start()
    for i in range(3, 6):
        weight_ready(i)

    gather_relay(xb, x_s, x_r, over_x)

    a_parts = (pl.ds(0, A_COLS), pl.ds(A_COLS, A_COLS))

    def first_products(i, carry):
        xp = lax.rem(x + 4 - order(i), 4)
        gather_far(xb, x_s, x_r, over_x, i)
        gather_ready(xb, x_r, over_x, i)
        block = xb[pl.ds(2 * xp, 2)].reshape(2 * rows, both + 128)
        pair = pl.ds(2 * xp, 2)
        lhs = block[:, :both]

        def product(w, start, width):
            return jnp.dot(
                lhs, w[:, start : start + width], preferred_element_type=f32
            ).astype(bf16).reshape(2, rows, width)

        for p, w in enumerate((wg, wu)):
            cols = a_parts[p]
            part_a[pair, :, cols] = product(w, 0, A_COLS)
            remote(
                part_a.at[2 * xp + 1 - yh, :, cols], a1_in.at[xp, :, cols], a1_s.at[p, xp],
                a1_r.at[p, xp], y_peer,
            ).start()
        part_b[pair, :, :b_half] = product(wg, A_COLS, b_half)
        part_b[pair, :, b_half:b_cols] = product(wu, A_COLS, b_half)
        part_b[pair, :, b_cols:] = block[:, both:].reshape(2, rows, 128)
        role = lax.rem(xp + 4 - z, 4)

        @pl.when(role == 2)
        def _():
            for j in range(2):
                remote(
                    part_b.at[2 * xp + j], bm_in.at[j], b_s.at[j], b_r.at[j], other_z(1 + 2 * j)
                ).start()

        for j in range(2):

            @pl.when(role == 3 - 2 * j)
            def _():
                remote(
                    part_b.at[2 * xp + j], b_in.at[1 - j, j], b_s.at[2 + j], b_r.at[2 + j],
                    other_z(3 - 2 * j),
                ).start()

        return carry

    lax.fori_loop(0, 4, first_products, 0)
    halves = (upper, lower)

    def second_a(i, carry):
        xp = lax.rem(x + 4 - order(i), 4)
        for p, cols in enumerate(a_parts):
            arrived(a1_in.at[xp, :, cols], a1_r.at[p, xp])
            a2[xp, :, cols] = (
                part_a[2 * xp + yh, :, cols].astype(f32) + a1_in[xp, :, cols].astype(f32)
            ).astype(bf16)
        role = lax.rem(xp + 4 - z, 4)

        @pl.when(role == 2)
        def _():
            for j in range(2):
                remote(
                    a2.at[xp, halves[j]], am_in.at[j], a_s.at[j], a_r.at[j], other_z(1 + 2 * j)
                ).start()

        for j in range(2):

            @pl.when(role == 3 - 2 * j)
            def _():
                remote(
                    a2.at[xp, halves[j]], a_in.at[1 - j, halves[j]], a_s.at[2 + j],
                    a_r.at[2 + j], other_z(3 - 2 * j),
                ).start()

        return carry

    def total_squares(block):
        return block[:, 0:1] + block[:, 1:2]

    def relay_b(j):
        block = 2 * lax.rem(z + 1 + 2 * j, 4) + j
        arrived(bm_in.at[j], b_r.at[j])
        total = part_b[block].astype(f32) + bm_in[j].astype(f32)
        part_b[block, :, :b_cols] = total[:, :b_cols].astype(bf16)
        part_b[block, :, b_cols:] = with_sum(total_squares(total[:, b_cols:]))
        remote(
            part_b.at[block], b_in.at[j, j], b_s.at[4 + j], b_r.at[4 + j], other_z(1 + 2 * j)
        ).start()

    def relay_a(j):
        block = lax.rem(z + 1 + 2 * j, 4)
        arrived(am_in.at[j], a_r.at[j])
        a2[block, halves[j]] = (
            a2[block, halves[j]].astype(f32) + am_in[j].astype(f32)
        ).astype(bf16)
        remote(
            a2.at[block, halves[j]], a_in.at[j, halves[j]], a_s.at[4 + j], a_r.at[4 + j],
            other_z(1 + 2 * j),
        ).start()

    for j in range(2):
        relay_b(j)
    lax.fori_loop(0, 2, second_a, 0)
    for j in range(2):
        arrived(b_in.at[1 - j, j], b_r.at[2 + j])
        arrived(b_in.at[j, j], b_r.at[4 + j])

    def sum_b(j):
        return part_b[2 * z + j].astype(f32) + b_in[0, j].astype(f32) + b_in[1, j].astype(f32)

    away = sum_b(1 - yh)
    b2_out[:, :b_cols] = away[:, :b_cols].astype(bf16)
    b2_out[:, b_cols:] = with_sum(total_squares(away[:, b_cols:]))
    remote(b2_out, b2_in, b2_s.at[0], b2_r.at[0], y_peer).start()
    b_keep[...] = sum_b(yh)
    lax.fori_loop(2, 4, second_a, 0)
    for j in range(2):
        relay_a(j)
    arrived(b2_in, b2_r.at[0])

    def sum_b2(start, width):
        cols = slice(start, start + width)
        return b_keep[:, cols] + b2_in[:, cols].astype(f32)

    scale = lax.rsqrt(total_squares(sum_b2(b_cols, 128)) / D + norm_eps)

    def write_hidden(start, gate, upward):
        gate = gate * scale
        hb[q, :, start : start + gate.shape[1]] = (
            gate / (1.0 + jnp.exp(-gate)) * (upward * scale)
        ).astype(bf16)

    h_parts = (hb.at[:, :, pl.ds(A_COLS, b_half)], hb.at[:, :, pl.ds(0, A_COLS)])
    write_hidden(A_COLS, sum_b2(0, b_half), sum_b2(b_half, b_half))
    gather_start(h_parts[0], h_s.at[0], h_r.at[0], over_z)
    for j in range(2):
        arrived(a_in.at[1 - j, halves[j]], a_r.at[2 + j])
        arrived(a_in.at[j, halves[j]], a_r.at[4 + j])

    def sum_a(start):
        cols = slice(start, start + A_COLS)
        return (
            a2[z, :, cols].astype(f32) + a_in[0, :, cols].astype(f32)
            + a_in[1, :, cols].astype(f32)
        )

    write_hidden(0, sum_a(0), sum_a(A_COLS))
    gather_start(h_parts[1], h_s.at[1], h_r.at[1], over_z)
    project(hb, h_parts, ((A_COLS, b_half), (0, A_COLS)), wd, h_s, h_r, g_out, g_in, gl_in, g_s, g_r)
    down = gathered_sum(g_out, g_in, gy_out, gy_in, g_s, g_r)
    lay_x[c] = (resid_rows[mine] + down).astype(bf16)
    remote(lay_x.at[c], lay_x.at[c], o_s.at[1], o_r.at[1], sibling).start()
    arrived(att_x.at[1 - c], o_r.at[0])
    arrived(lay_x.at[1 - c], o_r.at[1])

    for k in range(1, GROUPS):
        left(lat_in.at[0], l_s.at[k])
    for i, (src, dst) in enumerate(weights):
        left(src, w_s.at[i])
    for p in range(2):
        finish_gather(v_parts[p], v_s.at[p])
        finish_gather(h_parts[p], h_s.at[p])
    finish_sends(c_out, cy_out, c_s)
    finish_sends(g_out, gy_out, g_s)
    finish_gather(xb, x_s)
    for i in range(4):
        for p, cols in enumerate(a_parts):
            left(part_a.at[0, :, cols], a1_s.at[p, i])
    for i in range(6):
        left(part_b.at[0], b_s.at[i])
        left(a2.at[0, upper], a_s.at[i])
    left(b2_out, b2_s.at[0])
    left(att_x.at[0], o_s.at[0])
    left(lay_x.at[0], o_s.at[1])


def finish_kernel(att_ref, lay_ref, attended_ref, out_ref, turned):
    feats = attended_ref.shape[0]
    c = lax.rem(lax.axis_index("tp"), 2)
    own = pl.ds(pl.multiple_of(c * feats, feats), feats)
    for exchange, target in ((att_ref, attended_ref), (lay_ref, out_ref)):
        stacked = exchange[...].reshape(-1, 2 * feats).astype(jnp.float32)
        turned[...] = jnp.transpose(stacked, (1, 0))
        target[...] = turned[own].astype(target.dtype)


def run_layer(
    lengths, dest_group, moved_slot, queries, kv_cache, residual_in, norm_gain, up_value, out_proj,
    gate_proj, up_proj, down_proj,
):
    slots, all_heads, _ = queries.shape
    heads = up_value.shape[0]
    rows, width = GROUPS * slots, heads * 128
    queries = jnp.swapaxes(queries, 1, 2)
    kv_cache = jnp.swapaxes(kv_cache, 1, 2)
    total_rows, feats = residual_in.shape
    ff = gate_proj.shape[1]
    both = 2 * feats
    a_cols, b_cols = 2 * A_COLS, 2 * (ff - A_COLS) + 128
    f32, bf16 = jnp.float32, jnp.bfloat16
    vmem = pl.BlockSpec(memory_space=pltpu.VMEM)
    smem = pl.BlockSpec(memory_space=pltpu.SMEM)
    hbm = pl.BlockSpec(memory_space=pl.ANY)
    dma = pltpu.SemaphoreType.DMA
    block = jax.ShapeDtypeStruct((2, rows, both), bf16)
    turned = jax.ShapeDtypeStruct((feats, total_rows), bf16)
    att_x, lay_x = pl.pallas_call(
        layer_kernel,
        name="layer",
        out_shape=(block, block),
        in_specs=[smem, smem, smem, hbm, hbm, hbm, hbm, vmem, hbm, hbm, hbm, hbm],
        out_specs=(vmem, vmem),
        scratch_shapes=[
            pltpu.VMEM(queries.shape, bf16),
            pltpu.VMEM(kv_cache.shape, bf16),
            pltpu.VMEM(up_value.shape, bf16),
            pltpu.VMEM((slots, all_heads, KV), bf16),
            pltpu.VMEM((GROUPS, slots, heads, KV), bf16),
            pltpu.VMEM((KV // 128, rows * heads, 128), f32),
            pltpu.VMEM((rows, width), bf16),
            pltpu.VMEM((both, width), bf16),
            pltpu.VMEM((both, ff), bf16),
            pltpu.VMEM((both, ff), bf16),
            pltpu.VMEM((both, ff), bf16),
            pltpu.VMEM((both, total_rows), bf16),
            pltpu.VMEM((feats, 128), bf16),
            pltpu.VMEM((both, 128), bf16),
            pltpu.VMEM((8, rows, width), bf16),
            pltpu.VMEM((8, rows, both), bf16),
            pltpu.VMEM((4, 2, rows, both), bf16),
            pltpu.VMEM((rows, both), bf16),
            pltpu.VMEM((rows, both), bf16),
            pltpu.VMEM((rows, both), bf16),
            pltpu.VMEM((8, rows, both + 128), bf16),
            pltpu.VMEM((8, rows, a_cols), bf16),
            pltpu.VMEM((8, rows, b_cols), bf16),
            pltpu.VMEM((4, rows, a_cols), bf16),
            pltpu.VMEM((4, rows, a_cols), bf16),
            pltpu.VMEM((2, rows // 2, a_cols), bf16),
            pltpu.VMEM((2, rows, a_cols), bf16),
            pltpu.VMEM((2, rows, b_cols), bf16),
            pltpu.VMEM((2, 2, rows, b_cols), bf16),
            pltpu.VMEM((rows, b_cols), bf16),
            pltpu.VMEM((rows, b_cols), bf16),
            pltpu.VMEM((rows, b_cols), f32),
            pltpu.VMEM((8, rows, ff), bf16),
            pltpu.VMEM((8, rows, both), bf16),
            pltpu.VMEM((4, 2, rows, both), bf16),
            pltpu.VMEM((rows, both), bf16),
            pltpu.VMEM((rows, both), bf16),
            pltpu.VMEM((rows, both), bf16),
            pltpu.VMEM((rows, both), f32),
            pltpu.VMEM((total_rows, both), f32),
            pltpu.VMEM((1, both), f32),
            pltpu.VMEM((both, total_rows), f32),
            dma((2, slots)), dma, dma, dma((8,)), dma((8,)),
            dma((6,)), dma((6,)), dma((6,)), dma((2, 18)), dma((2, 18)),
            dma((6,)), dma((6,)), dma((18,)), dma((18,)),
            dma((2, 4)), dma((2, 4)), dma((6,)), dma((6,)), dma((6,)), dma((6,)), dma((1,)), dma((1,)),
            dma((2, 18)), dma((2, 18)), dma((6,)), dma((6,)), dma((2,)), dma((2,)),
        ],
        compiler_params=pltpu.CompilerParams(
            collective_id=0, has_side_effects=True, vmem_limit_bytes=62 << 20
        ),
        cost_estimate=pl.CostEstimate(
            flops=2 * total_rows * 8 * feats * (width + 3 * ff), bytes_accessed=30 << 20,
            transcendentals=1 << 20,
        ),
    )(
        lengths[:, 0, :], dest_group[:, 0], moved_slot[:, 0], queries, kv_cache, up_value,
        jnp.swapaxes(residual_in, 0, 1), norm_gain, jnp.swapaxes(out_proj, 0, 1),
        gate_proj, up_proj, jnp.swapaxes(down_proj, 0, 1),
    )
    attended, layer_out = pl.pallas_call(
        finish_kernel,
        name="finish",
        out_shape=(turned, turned),
        in_specs=[vmem, vmem],
        out_specs=(vmem, vmem),
        scratch_shapes=[pltpu.VMEM((both, total_rows), f32)],
    )(att_x, lay_x)
    return jnp.swapaxes(attended, 0, 1), jnp.swapaxes(layer_out, 0, 1)


def shards(
    queries,
    kv_cache,
    lengths,
    dest_group,
    moved_slot,
    residual_in,
    norm_gain,
    up_value,
    out_proj,
    gate_proj,
    up_proj,
    down_proj,
):
    return run_layer(
        lengths, dest_group, moved_slot, queries, kv_cache, residual_in, norm_gain, up_value,
        out_proj, gate_proj, up_proj, down_proj,
    )


def solution(mesh):
    return jax.shard_map(
        shards,
        mesh=mesh,
        in_specs=(
            P(("dp", "tp"), None, None),
            P(("dp", "tp"), None, None),
            P(None, "tp", None),
            P(None, "tp"),
            P(None, "tp"),
            P("dp", "tp"),
            P("tp"),
            P("dp", None, None),
            P("dp", "tp"),
            P("tp", "dp"),
            P("tp", "dp"),
            P("dp", "tp"),
        ),
        out_specs=(P("dp", "tp"), P("dp", "tp")),
        check_vma=False,
    )
```
